32 devices in a mesh: ctx: 8 (over z, x), tp: 4 (over y, core).
Axes of the slice: x: 2, y: 2, z: 4, core: 2. Of those that a mesh axis runs over, the one named last changes fastest.
Arguments:
- streams: bfloat16 [1280, 3, 4096], P('ctx', None, 'tp'), may hold values from -6 to 6
- short_taps: float32 [7, 3, 4096], P(None, None, 'tp'), may hold values from -2 to 2
- mix_taps: float32 [128, 4096], P(None, 'tp'), may hold values from -0.5 to 0.5
- pole_rate: float32 [16, 4096], P(None, 'tp'), may hold values from 7.8125e-05 to 0.06, as said below
- pole_angle: float32 [16, 4096], P(None, 'tp'), may hold values from -3.140625 to 3.140625
- residue: float32 [2, 16, 4096], P(None, None, 'tp'), may hold values from -1.5 to 1.5
- skip: float32 [4096], P('tp'), may hold values from -3 to 3
- out_weight: bfloat16 [4096, 4096], P('tp', 'ctx'), may hold values from -0.125 to 0.125
Outputs:
- mixed: bfloat16 [1280, 4096], P('ctx', 'tp')
The draws below stay inside these ranges and needn't reach their ends.
Inputs may be any that keep to these rules, and one draw needn't show every extreme that they name: `pole_rate`: each pole's decay rate is positive.
All inputs are finite; a program needn't handle non-finite values.
Results may differ from the reference program's by a relative error of at most 0.0057.
Values may be sent and summed in bfloat16 or wider, within the bound.
No kernel may reach another device: no remote copies, remote signals or barrier semaphores. Data moves between devices by JAX's collectives and lax.ppermute only.
A program may use at most 64 MiB of HBM per device.

```python
import math
import jax
import jax.numpy as jnp
from jax import lax

D = 4096
DOUT = 4096
MODES = 16
TOK_DEV = 160
TOKENS = 1280
N_CTX = 8


def draw_pole_rate(key, part):
    key_pick, key_slow, key_fast = jax.random.split(key, 3)
    share = 0.5
    pick = jax.random.uniform(key_pick, (MODES, D)) < share
    slow = jnp.exp(jax.random.uniform(key_slow, (MODES, D), minval=math.log(0.05), maxval=0.0)) * (2.3 / TOKENS)
    fast = jnp.exp(jax.random.uniform(key_fast, (MODES, D), minval=math.log(0.025), maxval=math.log(0.06)))
    return jnp.where(pick, slow, fast).astype(jnp.float32)


def strengthened(result, own_key, source, target, shards_of, factor):
    def block_of(axis_at):
        return (jnp.arange(result.shape[axis_at]) // (result.shape[axis_at] // shards_of)).reshape((-1,) + (1,) * (result.ndim - 1 - axis_at))

    near = jax.random.permutation(own_key, shards_of)[block_of(target)]
    other_side = (block_of(target) + shards_of // 2) % shards_of
    return jnp.where((block_of(source) == near) | (block_of(source) == other_side), factor * result, result)


def level_of(own_key, extent, cuts, low, top_value):
    def one(position, parts):
        heights = jax.random.uniform(jax.random.fold_in(jax.random.fold_in(own_key, 6), position), (parts,), jnp.float32, low / len(cuts), top_value / len(cuts))
        return jnp.repeat(jnp.exp(heights), extent[position] // parts).reshape((-1,) + (1,) * (len(extent) - position - 1))

    loudness = one(*cuts[0])
    for cut in cuts[1:]:
        loudness = loudness * one(*cut)
    return loudness


def bell_draw(stream_key, shape, spread, reach, cuts=(), kind=jnp.bfloat16):
    result = spread * jax.random.normal(stream_key, shape, jnp.float32)
    if cuts:
        result = result * level_of(stream_key, shape, cuts, -0.22, 0.18)
    return jnp.clip(result, -reach, reach).astype(kind)


def heavy_noise(key, extent, spread, reach, cuts, heavy, kind=jnp.bfloat16):
    result = spread * jax.random.normal(key, extent, jnp.float32)
    if cuts:
        result = result * level_of(key, extent, cuts, -0.22, 0.18)
    return jnp.clip(strengthened(result, jax.random.fold_in(key, 3), *heavy), -reach, reach).astype(kind)


def setup_inputs(seed: int = 0) -> dict:
    key_of = jax.random.split(jax.random.key(seed), 9)
    streams = bell_draw(key_of[0], (TOKENS, 3, D), 1.0, 6.0, ((0, 8), (2, 4)))
    short_taps = bell_draw(key_of[1], (7, 3, D), 7 ** -0.5, 2.0, ((2, 4),), jnp.float32)
    mix_taps = bell_draw(key_of[2], (128, D), 128 ** -0.5, 0.5, ((1, 4),), jnp.float32)
    pole_rate = draw_pole_rate(jax.random.fold_in(key_of[8], 71), 0)
    pole_angle = jnp.clip(jax.random.uniform(key_of[4], (MODES, D), jnp.float32, -3.140625, 3.140625), -3.140625, 3.140625)
    residue = bell_draw(key_of[5], (2, MODES, D), 0.25, 1.5, ((2, 4),), jnp.float32)
    skip = bell_draw(key_of[6], (D,), 0.5, 3.0, ((0, 4),), jnp.float32)
    out_weight = heavy_noise(key_of[7], (D, DOUT), D ** -0.5, 0.125, ((0, 4), (1, 8)), (0, 1, 8, 2.0))
    return {"streams": streams, "short_taps": short_taps, "mix_taps": mix_taps, "pole_rate": pole_rate, "pole_angle": pole_angle, "residue": residue, "skip": skip, "out_weight": out_weight}


def fft_causal(ext, taps, rows):
    width = taps.shape[0]
    total = ext.shape[0] + width
    spec = jnp.fft.rfft(ext, n=total, axis=0) * jnp.fft.rfft(taps, n=total, axis=0)
    full = jnp.fft.irfft(spec, n=total, axis=0)
    start = ext.shape[0] - rows
    return full[start:start + rows].astype(jnp.float32)

def reference(streams, short_taps, mix_taps, pole_rate, pole_angle, residue, skip, out_weight):
    rows = TOK_DEV
    blocks = streams.reshape(N_CTX, rows, 3, D)
    amp = jnp.sqrt(1.0 - jnp.exp(-2.0 * pole_rate))
    res_re = residue[0] * amp
    res_im = residue[1] * amp
    dec_mag = jnp.exp(-pole_rate * rows)
    dec_re = dec_mag * jnp.cos(pole_angle * rows)
    dec_im = dec_mag * jnp.sin(pole_angle * rows)
    steps = jnp.arange(rows).astype(jnp.float32)[:, None]

    def one_block(carry, block):
        rim, st_re, st_im = carry
        ext = jnp.concatenate([rim, block], 0).astype(jnp.float32)
        span = rows + 127
        short = jnp.zeros((span, 3, D), jnp.float32)
        for lag in range(7):
            short = short + short_taps[lag][None] * ext[6 - lag:6 - lag + span]
        gate = (short[:, 1] * short[:, 2]).astype(jnp.bfloat16)
        query = short[127:, 0]
        medium = fft_causal(gate.astype(jnp.float32), mix_taps, rows)
        filt = jnp.zeros((rows, D), jnp.float32)
        inflow = jnp.zeros((rows, D), jnp.float32)
        flipped = medium[::-1]
        end_re = []
        end_im = []
        for mode in range(MODES):
            mag = jnp.exp(-pole_rate[mode][None] * steps)
            cosk = mag * jnp.cos(pole_angle[mode][None] * steps)
            sink = mag * jnp.sin(pole_angle[mode][None] * steps)
            filt = filt + res_re[mode][None] * cosk - res_im[mode][None] * sink
            end_re.append(lax.optimization_barrier(jnp.sum(flipped * cosk, 0)))
            end_im.append(lax.optimization_barrier(jnp.sum(flipped * sink, 0)))
            later = steps + 1.0
            mag1 = jnp.exp(-pole_rate[mode][None] * later)
            cos1 = mag1 * jnp.cos(pole_angle[mode][None] * later)
            sin1 = mag1 * jnp.sin(pole_angle[mode][None] * later)
            are = res_re[mode] * st_re[mode] - res_im[mode] * st_im[mode]
            aim = res_re[mode] * st_im[mode] + res_im[mode] * st_re[mode]
            inflow = inflow + are[None] * cos1 - aim[None] * sin1
        intra = fft_causal(medium, filt, rows)
        longf = intra + inflow + skip[None] * medium
        hidden = (query * longf).astype(jnp.bfloat16)
        out = jnp.dot(hidden, out_weight, preferred_element_type=jnp.float32).astype(jnp.bfloat16)
        e_re = jnp.stack(end_re, 0)
        e_im = jnp.stack(end_im, 0)
        new_re = dec_re * st_re - dec_im * st_im + e_re
        new_im = dec_re * st_im + dec_im * st_re + e_im
        return ((block[rows - 133:], new_re, new_im), out)
    init = (jnp.zeros((133, 3, D), jnp.bfloat16), jnp.zeros((MODES, D), jnp.float32), jnp.zeros((MODES, D), jnp.float32))
    final, outs = lax.scan(one_block, init, blocks)
    return outs.reshape(TOKENS, DOUT)
```

```python
import jax
import jax.numpy as jnp
import ml_dtypes
import numpy as np
from jax import lax
from jax.experimental import pallas as pl
from jax.experimental.pallas import tpu as pltpu
from jax.sharding import PartitionSpec as P

F32 = jnp.float32
BF16 = jnp.bfloat16
AXES = ("ctx", "tp")
GROUP = 4
BIT_CORE, BIT_Y, BIT_PART = 1, 2, 16
SLOT_BITS = (0, 4, 8, 12)
VMEM = pl.BlockSpec(memory_space=pltpu.VMEM)
SMEM = pl.BlockSpec(memory_space=pltpu.SMEM)


def swap(block, bits):
    return lax.ppermute(block, AXES, [(i, i ^ bits) for i in range(32)])


def split_const(mat):
    hi = mat.astype(ml_dtypes.bfloat16)
    lo = (mat - hi.astype(np.float64)).astype(ml_dtypes.bfloat16)
    return hi, lo


def odd_dft(size, rows_in):
    freq = 2 * np.pi * (np.arange(size // 2) + 0.5) / size
    ang = freq[:, None] * np.arange(rows_in)
    return np.concatenate([np.cos(ang), -np.sin(ang)], 0)


def odd_idft(size, rows_out):
    freq = 2 * np.pi * (np.arange(size // 2) + 0.5) / size
    ang = np.asarray(rows_out)[:, None] * freq
    return np.concatenate([np.cos(ang), -np.sin(ang)], 1) * (2.0 / size)


def mm(a, b):
    return jnp.dot(a, b, preferred_element_type=F32)


def split(x):
    hi = x.astype(BF16)
    return hi, (x - hi.astype(F32)).astype(BF16)


def mm3(hi, lo, x):
    xh, xl = split(x)
    return mm(hi, xh) + mm(lo, xh) + mm(hi, xl)


def cmul(spec, filt):
    half = spec.shape[0] // 2
    a, b, c, d = spec[:half], spec[half:], filt[:half], filt[half:]
    return jnp.concatenate([a * c - b * d, a * d + b * c], 0)


def params(**kw):
    return pltpu.CompilerParams(vmem_limit_bytes=56 * 1024 * 1024, **kw)


def filters_kernel(rows, modes, taps_ref, rate_ref, angle_ref, res_ref, skip_ref, cmh, cml, clh, cll,
                   spec_ref, lspec_ref, qre_ref, qim_ref, par_ref):
    width = taps_ref.shape[1]
    ntap = taps_ref.shape[0]
    spec_ref[...] = mm3(cmh[:, :ntap], cml[:, :ntap], taps_ref[...])
    rate, angle = rate_ref[...], angle_ref[...]
    amp = jnp.sqrt(1.0 - jnp.exp(-2.0 * rate))
    rre, rim = res_ref[0] * amp, res_ref[1] * amp

    def power(n):
        mag = jnp.exp(-rate * n)
        return mag * jnp.cos(angle * n), mag * jnp.sin(angle * n)

    p1, p8, pend = power(1.0), power(8.0), power(float(rows))
    par_ref[0], par_ref[1] = rre * p1[0] - rim * p1[1], rre * p1[1] + rim * p1[0]
    par_ref[2], par_ref[3] = pend
    steps = lax.broadcasted_iota(jnp.int32, (8, width), 0).astype(F32)
    filt = [jnp.zeros((8, width), F32) for _ in range(rows // 8)]
    for m in range(modes):
        ang = angle[m:m + 1] * steps
        mag = jnp.exp(-rate[m:m + 1] * steps)
        cre, cim = mag * jnp.cos(ang), mag * jnp.sin(ang)
        sre, sim = p8[0][m:m + 1], p8[1][m:m + 1]
        wre, wim = rre[m:m + 1], rim[m:m + 1]
        for j in range(rows // 8):
            qre_ref[m, j * 8:j * 8 + 8] = cre
            qim_ref[m, j * 8:j * 8 + 8] = cim
            filt[j] = filt[j] + wre * cre - wim * cim
            cre, cim = cre * sre - cim * sim, cre * sim + cim * sre
    first = lax.broadcasted_iota(jnp.int32, (8, width), 0) == 0
    filt[0] = filt[0] + jnp.where(first, skip_ref[...], 0.0)
    lspec_ref[...] = mm3(clh[...], cll[...], jnp.concatenate(filt, 0))


def short_conv(ext_ref, taps, total):
    out = taps[0:1] * ext_ref[8:8 + total]
    for lag in range(1, 7):
        out = out + taps[lag:lag + 1] * ext_ref[8 - lag:8 - lag + total]
    return out


def gate_kernel(rows, g_ref, t_ref, s0, s1, s2, s3, gate_ref, msg_ref, head_ref, kx, vx):
    g = g_ref[0]
    total = GROUP * rows
    kx[:8] = jnp.zeros_like(kx[:8])
    vx[:8] = jnp.zeros_like(vx[:8])
    for m, s in enumerate((s0, s1, s2, s3)):
        at = pl.ds(pl.multiple_of((g ^ m) * rows + 8, 8), rows)
        kx[at, :] = s[0].astype(F32)
        vx[at, :] = s[1].astype(F32)
    sk = short_conv(kx, t_ref[1], total)
    sv = short_conv(vx, t_ref[2], total)
    gate = (sk * sv).astype(BF16)
    gate_ref[...] = gate
    head_ref[0], head_ref[1] = sk[:8], sv[:8]
    msg_ref[:128] = gate[total - 128:]
    tails = jnp.concatenate([kx[total:total + 8], vx[total:total + 8]], 0)
    msg_ref[128:144] = tails.astype(BF16)


def tail_part(tail, taps):
    ext = jnp.concatenate([tail, jnp.zeros_like(tail)], 0)
    out = taps[1:2] * ext[7:15]
    for lag in range(2, 7):
        out = out + taps[lag:lag + 1] * ext[8 - lag:16 - lag]
    return out


def medium_kernel(rows, modes, g_ref, t_ref, gate_ref, msg_ref, head_ref, spec_ref, qre_ref, qim_ref, par_ref,
                  cmh, cml, imh, iml, q0, q1, q2, q3,
                  med_ref, st_ref, out_ref, gx, flip, er, ei):
    g, part = g_ref[0], g_ref[1]
    width = gate_ref.shape[1]
    total = GROUP * rows
    live = (part > 0).astype(F32)
    gx[:128] = (msg_ref[:128].astype(F32) * live).astype(BF16)
    tails = msg_ref[128:144].astype(F32) * live
    sk = head_ref[0] + tail_part(tails[:8], t_ref[1])
    sv = head_ref[1] + tail_part(tails[8:], t_ref[2])
    gx[128:128 + total] = gate_ref[...]
    gx[128:144] = jnp.concatenate([(sk * sv).astype(BF16).astype(F32), gate_ref[:16].astype(F32)[8:]], 0).astype(BF16)
    for b in range(GROUP):
        gb = gx[b * rows:b * rows + rows + 128]
        y = cmul(mm(cmh[...], gb) + mm(cml[...], gb), spec_ref[...])
        both = mm3(imh[...], iml[...], y)
        med_ref[b] = both[:rows]
        flip[b] = both[rows:]
    lanes = width // 128
    per = 4
    for lt in range(lanes):
        ls = slice(lt * 128, lt * 128 + 128)
        for m0 in range(0, modes, per):
            def step(j, acc):
                at = pl.ds(pl.multiple_of(j * 8, 8), 8)
                x = [flip[b, at, ls] for b in range(GROUP)]
                out = []
                for i in range(per):
                    qr, qi = qre_ref[m0 + i, at, ls], qim_ref[m0 + i, at, ls]
                    for b in range(GROUP):
                        k = (i * GROUP + b) * 2
                        out += [acc[k] + x[b] * qr, acc[k + 1] + x[b] * qi]
                return tuple(out)
            acc = lax.fori_loop(0, rows // 8, step, (jnp.zeros((8, 128), F32),) * (2 * GROUP * per), unroll=4)
            for i in range(per):
                for b in range(GROUP):
                    k = (i * GROUP + b) * 2
                    er[b, m0 + i:m0 + i + 1, ls] = jnp.sum(acc[k], 0, keepdims=True)
                    ei[b, m0 + i:m0 + i + 1, ls] = jnp.sum(acc[k + 1], 0, keepdims=True)
    dre, dim = par_ref[2], par_ref[3]
    sre = jnp.zeros((modes, width), F32)
    sim = sre
    for b in range(GROUP):
        st_ref[b, 0], st_ref[b, 1] = sre, sim
        sre, sim = dre * sre - dim * sim + er[b], dre * sim + dim * sre + ei[b]
    out_ref[:modes] = sre
    out_ref[modes:2 * modes] = sim
    for m, q in enumerate((q0, q1, q2, q3)):
        @pl.when((g ^ m) == GROUP - 1)
        def _():
            out_ref[2 * modes:] = q[rows - 16:].astype(F32)[8:]


def intra_kernel(rows, g_ref, t_ref, med_ref, lspec_ref, clh, cll, ilh, ill, q0, q1, q2, q3, intra_ref, query_ref, qx):
    g = g_ref[0]
    for b in range(GROUP):
        y = cmul(mm3(clh[...], cll[...], med_ref[b]), lspec_ref[...])
        intra_ref[b] = mm3(ilh[...], ill[...], y)
    qx[:8] = jnp.zeros_like(qx[:8])
    for m, q in enumerate((q0, q1, q2, q3)):
        qx[pl.ds(pl.multiple_of((g ^ m) * rows + 8, 8), rows), :] = q[...].astype(F32)
    query_ref[...] = short_conv(qx, t_ref[0], GROUP * rows)


def hidden_kernel(rows, modes, g_ref, t_ref, in_ref, st_ref, par_ref, qre_ref, qim_ref, intra_ref, query_ref, hid_ref, amp):
    part = g_ref[1]
    live = (part > 0).astype(F32)
    width = query_ref.shape[1]
    rin, iin = in_ref[:modes] * live, in_ref[modes:2 * modes] * live
    rre, rim, dre, dim = par_ref[0], par_ref[1], par_ref[2], par_ref[3]
    for b in range(GROUP):
        sre, sim = st_ref[b, 0] + rin, st_ref[b, 1] + iin
        are, aim = rre * sre - rim * sim, rre * sim + rim * sre
        for m in range(modes):
            amp[b, m, 0] = jnp.broadcast_to(are[m:m + 1], (8, width))
            amp[b, m, 1] = jnp.broadcast_to(aim[m:m + 1], (8, width))
        rin, iin = dre * rin - dim * iin, dre * iin + dim * rin
    query_ref_head = query_ref[:8] + tail_part(in_ref[2 * modes:] * live, t_ref[0])
    query_ref[:8] = query_ref_head
    for lt in range(width // 128):
        ls = slice(lt * 128, lt * 128 + 128)

        def step(j, carry):
            at = [pl.ds(pl.multiple_of(j * 16 + 8 * i, 8), 8) for i in range(2)]
            acc = [[intra_ref[b, at[i], ls] for i in range(2)] for b in range(GROUP)]
            for m in range(modes):
                qr = [qre_ref[m, at[i], ls] for i in range(2)]
                qi = [qim_ref[m, at[i], ls] for i in range(2)]
                for b in range(GROUP):
                    ar, ai = amp[b, m, 0, :, ls], amp[b, m, 1, :, ls]
                    for i in range(2):
                        acc[b][i] = acc[b][i] + ar * qr[i] - ai * qi[i]
            for b in range(GROUP):
                row = pl.multiple_of(b * rows + j * 16, 16)
                long = jnp.concatenate(acc[b], 0)
                hid_ref[pl.ds(row, 16), ls] = (query_ref[pl.ds(row, 16), ls] * long).astype(BF16)
            return carry

        lax.fori_loop(0, rows // 16, step, 0)


def project_kernel(g_ref, h0, h1, h2, h3, wa_ref, wb_ref, keep_ref, send_ref):
    g, same, core = g_ref[0], g_ref[2], g_ref[3]
    quarter = h0.shape[1]
    half = wa_ref.shape[1] // 2
    mine = pl.ds(pl.multiple_of(core * half, half), half)
    other = pl.ds(pl.multiple_of((1 - core) * half, half), half)
    accs = [None] * 4
    for m, h in enumerate((h0, h1, h2, h3)):
        at = pl.ds(pl.multiple_of((g ^ m) * quarter, quarter), quarter)
        x = h[...]
        for n, cols in enumerate((mine, other)):
            a, b = wa_ref[at, cols], wb_ref[at, cols]
            for k, w in enumerate((a, b)):
                d = mm(x, w)
                accs[2 * k + n] = d if m == 0 else accs[2 * k + n] + d
    own = same > 0
    keep_ref[0] = jnp.where(own, accs[0], accs[2])
    keep_ref[1] = jnp.where(own, accs[2], accs[0])
    send_ref[0] = jnp.where(own, accs[1], accs[3]).astype(BF16)
    send_ref[1] = jnp.where(own, accs[3], accs[1]).astype(BF16)


def call(kernel, outs, args, scratch=(), flops=10**8):
    return pl.pallas_call(
        kernel,
        out_shape=tuple(jax.ShapeDtypeStruct(s, d) for s, d in outs),
        in_specs=[SMEM] + [VMEM] * (len(args) - 1),
        out_specs=(VMEM,) * len(outs),
        scratch_shapes=[pltpu.VMEM(s, d) for s, d in scratch],
        compiler_params=params(),
    )(*args)


def fast_body(streams, short_taps, mix_taps, pole_rate, pole_angle, residue, skip, out_weight):
    rows, _, width = streams.shape
    modes = pole_rate.shape[0]
    ntap = mix_taps.shape[0]
    quarter = width // GROUP
    total = GROUP * rows
    ctx, tp = lax.axis_index("ctx"), lax.axis_index("tp")
    g, part = ctx % GROUP, ctx // GROUP
    core, y = tp % 2, tp // 2
    scal = jnp.stack([g, part, (y == part).astype(jnp.int32), core]).astype(jnp.int32)

    def columns(x, slot=0):
        return lax.dynamic_slice_in_dim(x, (g ^ slot) * quarter, quarter, x.ndim - 1)

    kv = [columns(streams[:, 1:], m).transpose(1, 0, 2) for m in range(GROUP)]
    qs = [columns(streams[:, 0], m) for m in range(GROUP)]
    kv = [kv[0]] + [swap(kv[m], SLOT_BITS[m]) for m in (1, 2, 3)]
    qs = [qs[0]] + [swap(qs[m], SLOT_BITS[m]) for m in (1, 2, 3)]

    size_m, size_l = rows + ntap, 2 * rows
    cmh, cml = split_const(odd_dft(size_m, size_m))
    back = np.concatenate([np.arange(ntap, size_m), np.arange(ntap, size_m)[::-1]])
    imh, iml = split_const(odd_idft(size_m, back))
    clh, cll = split_const(odd_dft(size_l, rows))
    ilh, ill = split_const(odd_idft(size_l, np.arange(rows)))

    taps = columns(short_taps).transpose(1, 0, 2)
    args = (columns(mix_taps), columns(pole_rate), columns(pole_angle), columns(residue), columns(skip)[None], cmh, cml, clh, cll)
    spec, lspec, qre, qim, par = pl.pallas_call(
        lambda *refs: filters_kernel(rows, modes, *refs),
        out_shape=tuple(jax.ShapeDtypeStruct(s, F32) for s in (
            (size_m, quarter), (size_l, quarter), (modes, rows, quarter), (modes, rows, quarter), (4, modes, quarter))),
        in_specs=[VMEM] * len(args),
        out_specs=(VMEM,) * 5,
        compiler_params=params(),
    )(*args)

    gate, msg, head = call(
        lambda *refs: gate_kernel(rows, *refs),
        [((total, quarter), BF16), ((144, quarter), BF16), ((2, 8, quarter), F32)],
        (scal, taps, *kv),
        [((total + 8, quarter), F32)] * 2,
    )
    msg = swap(msg, BIT_PART)
    med, st, out = call(
        lambda *refs: medium_kernel(rows, modes, *refs),
        [((GROUP, rows, quarter), F32), ((GROUP, 2, modes, quarter), F32), ((2 * modes + 8, quarter), F32)],
        (scal, taps, gate, msg, head, spec, qre, qim, par, cmh, cml, imh, iml, *qs),
        [((total + 128, quarter), BF16), ((GROUP, rows, quarter), F32), ((GROUP, modes, quarter), F32), ((GROUP, modes, quarter), F32)],
    )
    state_in = swap(out, BIT_PART)
    intra, query = call(
        lambda *refs: intra_kernel(rows, *refs),
        [((GROUP, rows, quarter), F32), ((total, quarter), F32)],
        (scal, taps, med, lspec, clh, cll, ilh, ill, *qs),
        [((total + 8, quarter), F32)],
    )
    (hidden,) = call(
        lambda *refs: hidden_kernel(rows, modes, *refs),
        [((total, quarter), BF16)],
        (scal, taps, state_in, st, par, qre, qim, intra, query),
        [((GROUP, modes, 2, 8, quarter), F32)],
    )
    hid = [hidden] + [swap(hidden, SLOT_BITS[m]) for m in (1, 2, 3)]
    far_weight = swap(out_weight, BIT_PART)
    half = out_weight.shape[1] // 2
    keep, send = call(
        project_kernel,
        [((2, total, half), F32), ((2, total, half), BF16)],
        (scal, *hid, out_weight, far_weight),
    )
    chip = keep + swap(send, BIT_CORE).astype(F32)
    both = (chip[0] + swap(chip[1].astype(BF16), BIT_Y).astype(F32)).astype(BF16)
    blocks = [lax.dynamic_slice_in_dim(both, (g ^ m) * rows, rows, 0) for m in range(GROUP)]
    got = [blocks[0]] + [swap(blocks[m], SLOT_BITS[m]) for m in (1, 2, 3)]
    stay = (g // 2) == core
    near = [jnp.where(stay, got[0], got[2]), jnp.where(stay, got[1], got[3])]
    away = jnp.stack([jnp.where(stay, got[2], got[0]), jnp.where(stay, got[3], got[1])])
    far = swap(away, BIT_CORE)
    even = g % 2 == 0
    near = [jnp.where(even, near[0], near[1]), jnp.where(even, near[1], near[0])]
    far = [jnp.where(even, far[0], far[1]), jnp.where(even, far[1], far[0])]
    first = core == 0
    pieces = []
    for x in range(2):
        pieces += [jnp.where(first, near[x], far[x]), jnp.where(first, far[x], near[x])]
    return jnp.concatenate(pieces, 1)


def from_behind(block, axis, distance):
    devices = range(lax.axis_size(axis))
    route = [(i - distance, i) for i in devices if i - distance in devices]
    return lax.ppermute(block, axis, route)


def depthwise(ext, taps):
    width = taps.shape[1]
    kernel = taps[::-1][:, None, :]
    out = lax.conv_general_dilated(
        ext[None],
        kernel,
        (1,),
        "VALID",
        dimension_numbers=("NWC", "WIO", "NWC"),
        feature_group_count=width,
        precision=lax.Precision.HIGHEST,
    )
    return out[0]


def general_body(streams, short_taps, mix_taps, pole_rate, pole_angle, residue, skip, out_weight):
    rows, three, width = streams.shape
    modes = pole_rate.shape[0]
    short = short_taps.reshape(7, three * width)
    rim = from_behind(streams[rows - 6 :], "ctx", 1)
    ext = jnp.concatenate([rim, streams], 0).astype(jnp.float32).reshape(rows + 6, three * width)
    conv = depthwise(ext, short).reshape(rows, three, width)
    gate = (conv[:, 1] * conv[:, 2]).astype(jnp.bfloat16)
    gate_rim = from_behind(gate[rows - 127 :], "ctx", 1)
    gate_ext = jnp.concatenate([gate_rim, gate], 0)
    query = conv[:, 0]
    medium = depthwise(gate_ext.astype(jnp.float32), mix_taps)
    amp = jnp.sqrt(1.0 - jnp.exp(-2.0 * pole_rate))
    res_re = residue[0] * amp
    res_im = residue[1] * amp
    steps = jnp.arange(rows).astype(jnp.float32)[:, None]
    flipped = medium[::-1]

    def first_pass(mode, carry):
        filt, end_re, end_im = carry
        rate = pole_rate[mode][None]
        angle = pole_angle[mode][None]
        mag = jnp.exp(-rate * steps)
        cosk = mag * jnp.cos(angle * steps)
        sink = mag * jnp.sin(angle * steps)
        filt = filt + res_re[mode][None] * cosk - res_im[mode][None] * sink
        end_re = end_re.at[mode].set(jnp.sum(flipped * cosk, 0))
        end_im = end_im.at[mode].set(jnp.sum(flipped * sink, 0))
        return (filt, end_re, end_im)

    zero_state = jnp.zeros((modes, width), jnp.float32)
    filt, end_re, end_im = lax.fori_loop(
        0, modes, first_pass, (jnp.zeros((rows, width), jnp.float32), zero_state, zero_state)
    )
    dec_mag = jnp.exp(-pole_rate * rows)
    dec_re = dec_mag * jnp.cos(pole_angle * rows)
    dec_im = dec_mag * jnp.sin(pole_angle * rows)

    def relay_step(turn, received):
        in_re, in_im = received
        out_re = dec_re * in_re - dec_im * in_im + end_re
        out_im = dec_re * in_im + dec_im * in_re + end_im
        return from_behind((out_re, out_im), "ctx", 1)

    st_re, st_im = lax.fori_loop(0, lax.axis_size("ctx") - 1, relay_step, (zero_state, zero_state))
    later = steps + 1.0

    def second_pass(mode, inflow):
        rate = pole_rate[mode][None]
        angle = pole_angle[mode][None]
        mag = jnp.exp(-rate * later)
        cos1 = mag * jnp.cos(angle * later)
        sin1 = mag * jnp.sin(angle * later)
        are = res_re[mode] * st_re[mode] - res_im[mode] * st_im[mode]
        aim = res_re[mode] * st_im[mode] + res_im[mode] * st_re[mode]
        return inflow + are[None] * cos1 - aim[None] * sin1

    inflow = lax.fori_loop(0, modes, second_pass, jnp.zeros((rows, width), jnp.float32))
    padded = jnp.concatenate([jnp.zeros((rows - 1, width), jnp.float32), medium], 0)
    intra = depthwise(padded, filt)
    longf = intra + inflow + skip[None] * medium
    hidden = (query * longf).astype(jnp.bfloat16)
    partial_out = jnp.dot(
        hidden,
        lax.all_gather(out_weight, "ctx", axis=1, tiled=True),
        preferred_element_type=jnp.float32,
    )
    return lax.psum_scatter(partial_out, "tp", scatter_dimension=1, tiled=True).astype(jnp.bfloat16)


def solution(mesh):
    fast = dict(mesh.shape) == {"ctx": 8, "tp": 4}
    return jax.shard_map(
        fast_body if fast else general_body,
        mesh=mesh,
        in_specs=(
            P("ctx", None, "tp"),
            P(None, None, "tp"),
            P(None, "tp"),
            P(None, "tp"),
            P(None, "tp"),
            P(None, None, "tp"),
            P("tp"),
            P("tp", "ctx"),
        ),
        out_specs=P("ctx", "tp"),
        check_vma=False,
    )
```

```python
import jax
import jax.numpy as jnp
import ml_dtypes
import numpy as np
from jax import lax
from jax.experimental import pallas as pl
from jax.experimental.pallas import tpu as pltpu
from jax.sharding import PartitionSpec as P

F32 = jnp.float32
BF16 = jnp.bfloat16
AXES = ("ctx", "tp")
GROUP = 4
BIT_CORE, BIT_PART = 1, 16
EARLY = 6
SLOT_BITS = (0, 4, 8, 12)
VMEM = pl.BlockSpec(memory_space=pltpu.VMEM)
SMEM = pl.BlockSpec(memory_space=pltpu.SMEM)


def swap(block, bits):
    return lax.ppermute(block, AXES, [(i, i ^ bits) for i in range(32)])


def homeward(a, b, c):
    route = []
    for i in range(32):
        high, low, y, core = i >> 3 & 1, i >> 2 & 1, i >> 1 & 1, i & 1
        route.append((i, (i & 16) + (core ^ a) * 8 + (low ^ b) * 4 + (y ^ c) * 2 + high))
    return route


def split_const(mat):
    hi = mat.astype(ml_dtypes.bfloat16)
    lo = (mat - hi.astype(np.float64)).astype(ml_dtypes.bfloat16)
    return hi, lo


def odd_dft(size, rows_in):
    freq = 2 * np.pi * (np.arange(size // 2) + 0.5) / size
    ang = freq[:, None] * np.arange(rows_in)
    return np.concatenate([np.cos(ang), -np.sin(ang)], 0)


def odd_idft(size, rows_out):
    freq = 2 * np.pi * (np.arange(size // 2) + 0.5) / size
    ang = np.asarray(rows_out)[:, None] * freq
    return np.concatenate([np.cos(ang), -np.sin(ang)], 1) * (2.0 / size)


def mm(a, b):
    return jnp.dot(a, b, preferred_element_type=F32)


def split(x):
    hi = x.astype(BF16)
    return hi, (x - hi.astype(F32)).astype(BF16)


def mm3(hi, lo, x):
    xh, xl = split(x)
    return mm(hi, xh) + mm(lo, xh) + mm(hi, xl)


def cmul(spec, filt):
    half = spec.shape[0] // 2
    a, b, c, d = spec[:half], spec[half:], filt[:half], filt[half:]
    return jnp.concatenate([a * c - b * d, a * d + b * c], 0)


class View:
    def __init__(self, ref, top, high, wide):
        self.ref, self.top, self.high, self.wide = ref, top, high, wide

    def __getitem__(self, key):
        wide = self.wide if key is Ellipsis else key[1].stop
        return self.ref[self.top:self.top + self.high, :wide]


def views(consts, rows, size):
    out, top = [], 0
    for high, wide in ((size, size), (2 * rows, size), (2 * rows, rows), (rows, 2 * rows)):
        for _ in range(2):
            out.append(View(consts, top, high, wide))
            top += high
    return out


def params(**kw):
    return pltpu.CompilerParams(vmem_limit_bytes=16 * 1024 * 1024, **kw)


def filters_kernel(rows, modes, g_ref, taps_ref, rate_all, angle_all, res_all, skip_all, short_all, consts,
                   spec_ref, lspec_ref, qre_ref, qim_ref, par_ref, short_ref):
    width = spec_ref.shape[1]
    ntap = taps_ref.shape[0]
    cmh, cml, _, _, clh, cll, _, _ = views(consts, rows, spec_ref.shape[0])
    at = pl.ds(pl.multiple_of(g_ref[0] * width, width), width)
    spec_ref[...] = mm3(cmh[:, :ntap], cml[:, :ntap], taps_ref[:, at])
    short_ref[...] = short_all[:, :, at]
    rate_ref, angle_ref, res_ref, skip_ref = rate_all[:, at], angle_all[:, at], res_all[:, :, at], skip_all[:, at]
    rate, angle = rate_ref[...], angle_ref[...]
    amp = jnp.sqrt(1.0 - jnp.exp(-2.0 * rate))
    rre, rim = res_ref[0] * amp, res_ref[1] * amp

    def power(n):
        mag = jnp.exp(-rate * n)
        return mag * jnp.cos(angle * n), mag * jnp.sin(angle * n)

    p1, p8, pend = power(1.0), power(8.0), power(float(rows))
    par_ref[0], par_ref[1] = rre * p1[0] - rim * p1[1], rre * p1[1] + rim * p1[0]
    par_ref[2], par_ref[3] = pend
    steps = lax.broadcasted_iota(jnp.int32, (8, width), 0).astype(F32)
    filt = [jnp.zeros((8, width), F32) for _ in range(rows // 8)]
    for m in range(modes):
        ang = angle[m:m + 1] * steps
        mag = jnp.exp(-rate[m:m + 1] * steps)
        cre, cim = mag * jnp.cos(ang), mag * jnp.sin(ang)
        sre, sim = p8[0][m:m + 1], p8[1][m:m + 1]
        wre, wim = rre[m:m + 1], rim[m:m + 1]
        for j in range(rows // 8):
            qre_ref[m, j * 8:j * 8 + 8] = cre
            qim_ref[m, j * 8:j * 8 + 8] = cim
            filt[j] = filt[j] + wre * cre - wim * cim
            cre, cim = cre * sre - cim * sim, cre * sim + cim * sre
    first = lax.broadcasted_iota(jnp.int32, (8, width), 0) == 0
    filt[0] = filt[0] + jnp.where(first, skip_ref[...], 0.0)
    lspec_ref[...] = mm3(clh[...], cll[...], jnp.concatenate(filt, 0))


def prepare_kernel(rows, g_ref, x_ref, t_ref, o0, o1, o2, o3, kx, vx, gate):
    outs = (o0, o1, o2, o3)
    g = g_ref[0]
    quarter = o0.shape[1]
    for lt in range(x_ref.shape[2] // 128):
        ls = slice(lt * 128, lt * 128 + 128)
        for src, ext in ((1, kx), (2, vx)):
            ext[lt, :8] = jnp.zeros((8, 128), F32)
            ext[lt, 8:] = x_ref[src, :, ls].astype(F32)
        tk = [jnp.broadcast_to(t_ref[1, j:j + 1, ls], (8, 128)) for j in range(7)]
        tv = [jnp.broadcast_to(t_ref[2, j:j + 1, ls], (8, 128)) for j in range(7)]
        for r in range(0, rows, 16):
            both = []
            for h in (0, 8):
                sk, sv = tk[0] * kx[lt, 8 + r + h:16 + r + h], tv[0] * vx[lt, 8 + r + h:16 + r + h]
                for j in range(1, 7):
                    o = 8 + r + h - j
                    sk, sv = sk + tk[j] * kx[lt, o:o + 8], sv + tv[j] * vx[lt, o:o + 8]
                both.append(sk * sv)
            gate[r:r + 16, ls] = jnp.concatenate(both, 0).astype(BF16)
    for m, out in enumerate(outs):
        at = pl.ds(pl.multiple_of((g ^ m) * quarter, quarter), quarter)
        out[:rows] = gate[:, at]
        out[rows:2 * rows] = x_ref[0, :, at]
        for i in (1, 2):
            ends = [x_ref[i, :16, at].astype(F32)[:8], x_ref[i, rows - 16:, at].astype(F32)[8:]]
            row = 2 * rows + 16 * (i - 1)
            out[row:row + 16] = jnp.concatenate(ends, 0).astype(BF16)


def first_gates(before, ends, taps):
    out = []
    for i in (0, 1):
        ext = jnp.concatenate([before[16 * i + 8:16 * i + 16], ends[16 * i:16 * i + 8]], 0)
        t = taps[1 + i]
        acc = t[0:1] * ext[8:16]
        for j in range(1, 7):
            acc = acc + t[j:j + 1] * ext[8 - j:16 - j]
        out.append(acc)
    return out[0] * out[1]


def tail_part(tail, taps):
    ext = jnp.concatenate([tail, jnp.zeros_like(tail)], 0)
    out = taps[1:2] * ext[7:15]
    for lag in range(2, 7):
        out = out + taps[lag:lag + 1] * ext[8 - lag:16 - lag]
    return out


def end_states(rows, modes, per, flip, blocks, qre_ref, qim_ref, er, ei, width):
    for lt in range(width // 128):
        ls = slice(lt * 128, lt * 128 + 128)
        for m0 in range(0, modes, per):
            def step(j, acc):
                at = pl.ds(pl.multiple_of(j * 8, 8), 8)
                x = [flip[b, at, ls] for b in blocks]
                out = []
                for i in range(per):
                    qr, qi = qre_ref[m0 + i, at, ls], qim_ref[m0 + i, at, ls]
                    for b in range(len(blocks)):
                        k = (i * len(blocks) + b) * 2
                        out += [acc[k] + x[b] * qr, acc[k + 1] + x[b] * qi]
                return tuple(out)
            acc = lax.fori_loop(0, rows // 8, step, (jnp.zeros((8, 128), F32),) * (2 * len(blocks) * per), unroll=4)
            for i in range(per):
                for b in range(len(blocks)):
                    k = (i * len(blocks) + b) * 2
                    er[b, m0 + i:m0 + i + 1, ls] = jnp.sum(acc[k], 0, keepdims=True)
                    ei[b, m0 + i:m0 + i + 1, ls] = jnp.sum(acc[k + 1], 0, keepdims=True)


def medium_of(gates, spec, cmh, cml, imh, iml):
    return mm3(imh[...], iml[...], cmul(mm(cmh[...], gates) + mm(cml[...], gates), spec))


def medium_kernel(rows, modes, g_ref, t_ref, spec_ref, qre_ref, qim_ref, par_ref,
                  consts, q0, q1, q2, q3,
                  med_ref, st_ref, out_ref, rim_ref, gate_ref, ends_ref, gx, flip, er, ei, ends):
    g = g_ref[0]
    cmh, cml, imh, iml = views(consts, rows, spec_ref.shape[0])[:4]
    width = gate_ref.shape[1]
    gx[:128] = jnp.zeros_like(gx[:128])
    for m, msg in enumerate((q0, q1, q2, q3)):
        gx[pl.ds(pl.multiple_of(128 + (g ^ m) * rows, 16), rows), :] = msg[:rows]
        ends[g ^ m] = msg[2 * rows:2 * rows + 32].astype(F32)
    gate_ref[...] = gx[128:128 + rows]
    ends_ref[...] = ends[0]
    rim_ref[:128] = gx[GROUP * rows:]
    rim_ref[128:160] = ends[GROUP - 1].astype(BF16)
    for b in range(1, GROUP):
        top = 128 + b * rows
        head = first_gates(ends[b - 1], ends[b], t_ref)
        gx[top:top + 16] = jnp.concatenate([head, gx[top:top + 16].astype(F32)[8:]], 0).astype(BF16)
    for b in range(GROUP):
        both = medium_of(gx[b * rows:b * rows + rows + 128], spec_ref[...], cmh, cml, imh, iml)
        med_ref[b] = both[:rows]
        flip[b] = both[rows:]
    end_states(rows, modes, 4, flip, range(GROUP), qre_ref, qim_ref, er, ei, width)
    dre, dim = par_ref[2], par_ref[3]
    sre = jnp.zeros((modes, width), F32)
    sim = sre
    for b in range(GROUP):
        st_ref[b, 0], st_ref[b, 1] = er[b], ei[b]
        sre, sim = dre * sre - dim * sim + er[b], dre * sim + dim * sre + ei[b]
    out_ref[:modes] = sre
    out_ref[modes:2 * modes] = sim
    for m, q in enumerate((q0, q1, q2, q3)):
        @pl.when((g ^ m) == GROUP - 1)
        def _():
            out_ref[2 * modes:] = q[2 * rows - 16:2 * rows].astype(F32)[8:]


def intra_kernel(rows, g_ref, t_ref, med_ref, lspec_ref, consts, q0, q1, q2, q3, intra_ref, query_ref, qx):
    g = g_ref[0]
    _, _, _, _, clh, cll, ilh, ill = views(consts, rows, med_ref.shape[1] + 128)
    for b in range(1, GROUP):
        intra_ref[b - 1] = mm3(ilh[...], ill[...], cmul(mm3(clh[...], cll[...], med_ref[b]), lspec_ref[...]))
    total = GROUP * rows
    for lt in range(query_ref.shape[1] // 128):
        ls = slice(lt * 128, lt * 128 + 128)
        qx[lt, :8] = jnp.zeros((8, 128), F32)
        for m, q in enumerate((q0, q1, q2, q3)):
            qx[lt, pl.ds(pl.multiple_of((g ^ m) * rows + 8, 8), rows), :] = q[rows:2 * rows, ls].astype(F32)
        t = [jnp.broadcast_to(t_ref[0, j:j + 1, ls], (8, 128)) for j in range(7)]
        for r in range(0, total, 8):
            acc = t[0] * qx[lt, 8 + r:16 + r]
            for j in range(1, 7):
                acc = acc + t[j] * qx[lt, 8 + r - j:16 + r - j]
            query_ref[r:r + 8, ls] = acc


def hidden_kernel(rows, modes, g_ref, t_ref, in_ref, rim_ref, gate_ref, ends_ref, spec_ref, lspec_ref, st_ref, par_ref,
                  qre_ref, qim_ref, later_ref, query_ref, consts,
                  hid_ref, amp, gx, flip, er, ei, intra):
    part = g_ref[1]
    live = (part > 0).astype(F32)
    width = query_ref.shape[1]
    cmh, cml, imh, iml, clh, cll, ilh, ill = views(consts, rows, gx.shape[0])
    gx[:128] = (rim_ref[:128].astype(F32) * live).astype(BF16)
    head = first_gates(rim_ref[128:160].astype(F32) * live, ends_ref[...], t_ref)
    gx[128:] = gate_ref[...]
    gx[128:144] = jnp.concatenate([head, gate_ref[:16].astype(F32)[8:]], 0).astype(BF16)
    both = medium_of(gx[...], spec_ref[...], cmh, cml, imh, iml)
    flip[0] = both[rows:]
    intra[0] = mm3(ilh[...], ill[...], cmul(mm3(clh[...], cll[...], both[:rows]), lspec_ref[...]))
    end_states(rows, modes, 8, flip, range(1), qre_ref, qim_ref, er, ei, width)
    sre, sim = in_ref[:modes] * live, in_ref[modes:2 * modes] * live
    rre, rim, dre, dim = par_ref[0], par_ref[1], par_ref[2], par_ref[3]
    for b in range(GROUP):
        are, aim = rre * sre - rim * sim, rre * sim + rim * sre
        for m in range(modes):
            amp[b, m, 0] = jnp.broadcast_to(are[m:m + 1], (8, width))
            amp[b, m, 1] = jnp.broadcast_to(aim[m:m + 1], (8, width))
        ere, eim = (er[0], ei[0]) if b == 0 else (st_ref[b, 0], st_ref[b, 1])
        sre, sim = dre * sre - dim * sim + ere, dre * sim + dim * sre + eim
    query_ref[:8] = query_ref[:8] + tail_part(in_ref[2 * modes:] * live, t_ref[0])
    for lt in range(width // 128):
        ls = slice(lt * 128, lt * 128 + 128)

        def step(j, carry):
            at = [pl.ds(pl.multiple_of(j * 16 + 8 * i, 8), 8) for i in range(2)]
            acc = [[intra[0, at[i], ls] for i in range(2)]]
            acc += [[later_ref[b, at[i], ls] for i in range(2)] for b in range(GROUP - 1)]
            for m in range(modes):
                qr = [qre_ref[m, at[i], ls] for i in range(2)]
                qi = [qim_ref[m, at[i], ls] for i in range(2)]
                for b in range(GROUP):
                    ar, ai = amp[b, m, 0, :, ls], amp[b, m, 1, :, ls]
                    for i in range(2):
                        acc[b][i] = acc[b][i] + ar * qr[i] - ai * qi[i]
            for b in range(GROUP):
                row = pl.multiple_of(b * rows + j * 16, 16)
                long = jnp.concatenate(acc[b], 0)
                hid_ref[pl.ds(row, 16), ls] = (query_ref[pl.ds(row, 16), ls] * long).astype(BF16)
            return carry

        lax.fori_loop(0, rows // 16, step, 0)


def project_kernel(g_ref, h0, h1, h2, h3, wa_ref, *rest):
    far, (keep_ref, send_ref, wb_ref) = rest[:-3], rest[-3:]
    g, same, core = g_ref[0], g_ref[2], g_ref[3]
    quarter = h0.shape[1]
    half = wa_ref.shape[1] // 2
    top = 0
    for part in far:
        wb_ref[top:top + part.shape[0]] = part[...]
        top += part.shape[0]
    mine = pl.ds(pl.multiple_of(core * half, half), half)
    other = pl.ds(pl.multiple_of((1 - core) * half, half), half)
    accs = [None] * 4
    for m, h in enumerate((h0, h1, h2, h3)):
        at = pl.ds(pl.multiple_of((g ^ m) * quarter, quarter), quarter)
        x = h[...]
        for n, cols in enumerate((mine, other)):
            a, b = wa_ref[at, cols], wb_ref[at, cols]
            for k, w in enumerate((a, b)):
                d = mm(x, w)
                accs[2 * k + n] = d if m == 0 else accs[2 * k + n] + d
    own = same > 0
    keep_ref[0] = jnp.where(own, accs[0], accs[2])
    keep_ref[1] = jnp.where(own, accs[2], accs[0])
    send_ref[0] = jnp.where(own, accs[1], accs[3]).astype(BF16)
    send_ref[1] = jnp.where(own, accs[3], accs[1]).astype(BF16)


def sort_kernel(rows, g_ref, keep_ref, got_ref, *outs):
    low, core = g_ref[4], g_ref[3]
    for n, out in enumerate(outs):
        a, b, c = n >> 2 & 1, n >> 1 & 1, n & 1
        block = 2 * (core ^ a) + (low ^ b)
        at = pl.ds(pl.multiple_of(block * rows, rows), rows)
        out[...] = (keep_ref[c, at, :] + got_ref[c, at, :].astype(F32)).astype(BF16)


def gather_kernel(g_ref, *refs):
    out_ref = refs[-1]
    low, high = g_ref[4], g_ref[5]
    width = refs[0].shape[1]
    for n in range(4):
        a, b = n >> 1, n & 1
        at = pl.ds(pl.multiple_of((2 * (low ^ b) + (high ^ a)) * width, width), width)
        out_ref[:, at] = (refs[2 * n][...].astype(F32) + refs[2 * n + 1][...].astype(F32)).astype(BF16)


def call(us, kernel, outs, args, scratch=()):
    return pl.pallas_call(
        kernel,
        out_shape=tuple(jax.ShapeDtypeStruct(s, d) for s, d in outs),
        in_specs=[SMEM] + [VMEM] * (len(args) - 1),
        out_specs=(VMEM,) * len(outs),
        scratch_shapes=[pltpu.VMEM(s, d) for s, d in scratch],
        compiler_params=params(),
        cost_estimate=pl.CostEstimate(flops=int(us * 1.15e9), bytes_accessed=int(us * 3.69e6), transcendentals=0),
    )(*args)


def fast_body(streams, short_taps, mix_taps, pole_rate, pole_angle, residue, skip, out_weight):
    rows, _, width = streams.shape
    modes = pole_rate.shape[0]
    ntap = mix_taps.shape[0]
    quarter = width // GROUP
    total = GROUP * rows
    ctx, tp = lax.axis_index("ctx"), lax.axis_index("tp")
    g, part = ctx % GROUP, ctx // GROUP
    core, y = tp % 2, tp // 2
    scal = jnp.stack([g, part, (y == part).astype(jnp.int32), core, g % 2, g // 2]).astype(jnp.int32)

    cut = width * EARLY // 16
    size_m = rows + ntap
    back = np.concatenate([np.arange(ntap, size_m), np.arange(ntap, size_m)[::-1]])
    mats = [odd_dft(size_m, size_m), odd_idft(size_m, back), odd_dft(2 * rows, rows), odd_idft(2 * rows, np.arange(rows))]
    consts = np.concatenate([
        np.pad(half, ((0, 0), (0, 2 * rows - half.shape[1]))) for mat in mats for half in split_const(mat)], 0)

    short_taps = short_taps.transpose(1, 0, 2)
    msgs = call(
        1.5,
        lambda *refs: prepare_kernel(rows, *refs),
        [((2 * rows + 32, quarter), BF16)] * GROUP,
        (scal, streams.transpose(1, 0, 2), short_taps),
        [((width // 128, rows + 8, 128), F32)] * 2 + [((rows, width), BF16)],
    )
    ahead, msgs = lax.optimization_barrier((out_weight[:cut], msgs))
    early = swap(ahead, BIT_PART)
    msgs = [msgs[0]] + [swap(msgs[m], SLOT_BITS[m]) for m in (1, 2, 3)]
    spec, lspec, qre, qim, par, taps = call(
        2.5,
        lambda *refs: filters_kernel(rows, modes, *refs),
        [(s, F32) for s in ((size_m, quarter), (2 * rows, quarter), (modes, rows, quarter), (modes, rows, quarter),
                            (4, modes, quarter), (3, 7, quarter))],
        (scal, mix_taps, pole_rate, pole_angle, residue, skip[None], short_taps, consts),
    )
    med, st, out, rim, gate, ends = call(
        5.4,
        lambda *refs: medium_kernel(rows, modes, *refs),
        [((GROUP, rows, quarter), F32), ((GROUP, 2, modes, quarter), F32), ((2 * modes + 8, quarter), F32),
         ((160, quarter), BF16), ((rows, quarter), BF16), ((32, quarter), F32)],
        (scal, taps, spec, qre, qim, par, consts, *msgs),
        [((total + 128, quarter), BF16), ((GROUP, rows, quarter), F32), ((GROUP, modes, quarter), F32), ((GROUP, modes, quarter), F32),
         ((GROUP, 32, quarter), F32)],
    )
    out, rim, early = lax.optimization_barrier((out, rim, early))
    state_in, rim_in = swap(out, BIT_PART), swap(rim, BIT_PART)
    late, state_in, rim_in = lax.optimization_barrier((out_weight[cut:], state_in, rim_in))
    far_weight = [early, swap(late, BIT_PART)]
    later, query = call(
        3.1,
        lambda *refs: intra_kernel(rows, *refs),
        [((GROUP - 1, rows, quarter), F32), ((total, quarter), F32)],
        (scal, taps, med, lspec, consts, *msgs),
        [((quarter // 128, total + 8, 128), F32)],
    )
    (hidden,) = call(
        5.2,
        lambda *refs: hidden_kernel(rows, modes, *refs),
        [((total, quarter), BF16)],
        (scal, taps, state_in, rim_in, gate, ends, spec, lspec, st, par, qre, qim, later, query, consts),
        [((GROUP, modes, 2, 8, quarter), F32), ((rows + 128, quarter), BF16), ((1, rows, quarter), F32),
         ((1, modes, quarter), F32), ((1, modes, quarter), F32), ((1, rows, quarter), F32)],
    )
    hid = [hidden] + [swap(hidden, SLOT_BITS[m]) for m in (1, 2, 3)]
    half = out_weight.shape[1] // 2
    keep, send = call(
        2.2,
        project_kernel,
        [((2, total, half), F32), ((2, total, half), BF16)],
        (scal, *hid, out_weight, *far_weight),
        [((width, 2 * half), BF16)],
    )
    blocks = call(
        0.7,
        lambda *refs: sort_kernel(rows, *refs),
        [((rows, half), BF16)] * 8,
        (scal, keep, swap(send, BIT_CORE)),
    )
    blocks = [lax.ppermute(block, AXES, homeward(n >> 2 & 1, n >> 1 & 1, n & 1)) for n, block in enumerate(blocks)]
    (mixed,) = call(1.3, gather_kernel, [((rows, 4 * half), BF16)], (scal, *blocks))
    return mixed


def from_behind(block, axis, distance):
    devices = range(lax.axis_size(axis))
    route = [(i - distance, i) for i in devices if i - distance in devices]
    return lax.ppermute(block, axis, route)


def depthwise(ext, taps):
    width = taps.shape[1]
    kernel = taps[::-1][:, None, :]
    out = lax.conv_general_dilated(
        ext[None],
        kernel,
        (1,),
        "VALID",
        dimension_numbers=("NWC", "WIO", "NWC"),
        feature_group_count=width,
        precision=lax.Precision.HIGHEST,
    )
    return out[0]


def general_body(streams, short_taps, mix_taps, pole_rate, pole_angle, residue, skip, out_weight):
    rows, three, width = streams.shape
    modes = pole_rate.shape[0]
    short = short_taps.reshape(7, three * width)
    rim = from_behind(streams[rows - 6 :], "ctx", 1)
    ext = jnp.concatenate([rim, streams], 0).astype(jnp.float32).reshape(rows + 6, three * width)
    conv = depthwise(ext, short).reshape(rows, three, width)
    gate = (conv[:, 1] * conv[:, 2]).astype(jnp.bfloat16)
    gate_rim = from_behind(gate[rows - 127 :], "ctx", 1)
    gate_ext = jnp.concatenate([gate_rim, gate], 0)
    query = conv[:, 0]
    medium = depthwise(gate_ext.astype(jnp.float32), mix_taps)
    amp = jnp.sqrt(1.0 - jnp.exp(-2.0 * pole_rate))
    res_re = residue[0] * amp
    res_im = residue[1] * amp
    steps = jnp.arange(rows).astype(jnp.float32)[:, None]
    flipped = medium[::-1]

    def first_pass(mode, carry):
        filt, end_re, end_im = carry
        rate = pole_rate[mode][None]
        angle = pole_angle[mode][None]
        mag = jnp.exp(-rate * steps)
        cosk = mag * jnp.cos(angle * steps)
        sink = mag * jnp.sin(angle * steps)
        filt = filt + res_re[mode][None] * cosk - res_im[mode][None] * sink
        end_re = end_re.at[mode].set(jnp.sum(flipped * cosk, 0))
        end_im = end_im.at[mode].set(jnp.sum(flipped * sink, 0))
        return (filt, end_re, end_im)

    zero_state = jnp.zeros((modes, width), jnp.float32)
    filt, end_re, end_im = lax.fori_loop(
        0, modes, first_pass, (jnp.zeros((rows, width), jnp.float32), zero_state, zero_state)
    )
    dec_mag = jnp.exp(-pole_rate * rows)
    dec_re = dec_mag * jnp.cos(pole_angle * rows)
    dec_im = dec_mag * jnp.sin(pole_angle * rows)

    def relay_step(turn, received):
        in_re, in_im = received
        out_re = dec_re * in_re - dec_im * in_im + end_re
        out_im = dec_re * in_im + dec_im * in_re + end_im
        return from_behind((out_re, out_im), "ctx", 1)

    st_re, st_im = lax.fori_loop(0, lax.axis_size("ctx") - 1, relay_step, (zero_state, zero_state))
    later = steps + 1.0

    def second_pass(mode, inflow):
        rate = pole_rate[mode][None]
        angle = pole_angle[mode][None]
        mag = jnp.exp(-rate * later)
        cos1 = mag * jnp.cos(angle * later)
        sin1 = mag * jnp.sin(angle * later)
        are = res_re[mode] * st_re[mode] - res_im[mode] * st_im[mode]
        aim = res_re[mode] * st_im[mode] + res_im[mode] * st_re[mode]
        return inflow + are[None] * cos1 - aim[None] * sin1

    inflow = lax.fori_loop(0, modes, second_pass, jnp.zeros((rows, width), jnp.float32))
    padded = jnp.concatenate([jnp.zeros((rows - 1, width), jnp.float32), medium], 0)
    intra = depthwise(padded, filt)
    longf = intra + inflow + skip[None] * medium
    hidden = (query * longf).astype(jnp.bfloat16)
    partial_out = jnp.dot(
        hidden,
        lax.all_gather(out_weight, "ctx", axis=1, tiled=True),
        preferred_element_type=jnp.float32,
    )
    return lax.psum_scatter(partial_out, "tp", scatter_dimension=1, tiled=True).astype(jnp.bfloat16)


def solution(mesh):
    fast = dict(mesh.shape) == {"ctx": 8, "tp": 4}
    return jax.shard_map(
        fast_body if fast else general_body,
        mesh=mesh,
        in_specs=(
            P("ctx", None, "tp"),
            P(None, None, "tp"),
            P(None, "tp"),
            P(None, "tp"),
            P(None, "tp"),
            P(None, None, "tp"),
            P("tp"),
            P("tp", "ctx"),
        ),
        out_specs=P("ctx", "tp"),
        check_vma=False,
    )
```

```python
import jax
import jax.numpy as jnp
import ml_dtypes
import numpy as np
from jax import lax
from jax.experimental import pallas as pl
from jax.experimental.pallas import tpu as pltpu
from jax.sharding import PartitionSpec as P

F32 = jnp.float32
BF16 = jnp.bfloat16
AXES = ("ctx", "tp")
GROUP = 4
BIT_CORE, BIT_PART, BITS_FAR = 1, 16, 24
EARLY = 9
SLOT_BITS = (0, 4, 8, 12)
VMEM = pl.BlockSpec(memory_space=pltpu.VMEM)
SMEM = pl.BlockSpec(memory_space=pltpu.SMEM)


def swap(block, bits):
    return lax.ppermute(block, AXES, [(i, i ^ bits) for i in range(32)])


def homeward(a, b, c):
    route = []
    for i in range(32):
        high, low, y, core = i >> 3 & 1, i >> 2 & 1, i >> 1 & 1, i & 1
        part, row = i >> 4, y ^ c
        route.append((i, part * 16 + (core ^ a) * 8 + (low ^ b) * 4 + row * 2 + (high ^ part ^ row)))
    return route


def outer(i):
    return (i >> 4) == (i >> 3 & 1)


def far_swap(block, ends):
    return lax.ppermute(block, AXES, [(i, i ^ BITS_FAR) for i in range(32) if outer(i) == ends])


def split_const(mat):
    hi = mat.astype(ml_dtypes.bfloat16)
    lo = (mat - hi.astype(np.float64)).astype(ml_dtypes.bfloat16)
    return hi, lo


def odd_dft(size, rows_in):
    freq = 2 * np.pi * (np.arange(size // 2) + 0.5) / size
    ang = freq[:, None] * np.arange(rows_in)
    return np.concatenate([np.cos(ang), -np.sin(ang)], 0)


def odd_idft(size, rows_out):
    freq = 2 * np.pi * (np.arange(size // 2) + 0.5) / size
    ang = np.asarray(rows_out)[:, None] * freq
    return np.concatenate([np.cos(ang), -np.sin(ang)], 1) * (2.0 / size)


def mm(a, b):
    return jnp.dot(a, b, preferred_element_type=F32)


def split(x):
    hi = x.astype(BF16)
    return hi, (x - hi.astype(F32)).astype(BF16)


def mm3(hi, lo, x):
    xh, xl = split(x)
    return mm(hi, xh) + mm(lo, xh) + mm(hi, xl)


def cmul(spec, filt):
    half = spec.shape[0] // 2
    a, b, c, d = spec[:half], spec[half:], filt[:half], filt[half:]
    return jnp.concatenate([a * c - b * d, a * d + b * c], 0)


class View:
    def __init__(self, ref, top, high, wide):
        self.ref, self.top, self.high, self.wide = ref, top, high, wide

    def __getitem__(self, key):
        wide = self.wide if key is Ellipsis else key[1].stop
        return self.ref[self.top:self.top + self.high, :wide]


def views(consts, rows, size):
    out, top = [], 0
    for high, wide in ((size, size), (2 * rows, size), (2 * rows, rows), (rows, 2 * rows)):
        for _ in range(2):
            out.append(View(consts, top, high, wide))
            top += high
    return out


def params(**kw):
    return pltpu.CompilerParams(vmem_limit_bytes=16 * 1024 * 1024, **kw)


def filters_kernel(rows, modes, g_ref, taps_ref, rate_all, angle_all, res_all, skip_all, short_all, consts,
                   spec_ref, lspec_ref, qre_ref, qim_ref, par_ref, short_ref):
    width = spec_ref.shape[1]
    ntap = taps_ref.shape[0]
    cmh, cml, _, _, clh, cll, _, _ = views(consts, rows, spec_ref.shape[0])
    at = pl.ds(pl.multiple_of(g_ref[0] * width, width), width)
    spec_ref[...] = mm3(cmh[:, :ntap], cml[:, :ntap], taps_ref[:, at])
    short_ref[...] = short_all[:, :, at]
    rate_ref, angle_ref, res_ref, skip_ref = rate_all[:, at], angle_all[:, at], res_all[:, :, at], skip_all[:, at]
    rate, angle = rate_ref[...], angle_ref[...]
    amp = jnp.sqrt(1.0 - jnp.exp(-2.0 * rate))
    rre, rim = res_ref[0] * amp, res_ref[1] * amp

    def power(n):
        mag = jnp.exp(-rate * n)
        return mag * jnp.cos(angle * n), mag * jnp.sin(angle * n)

    p1, p8, pend = power(1.0), power(8.0), power(float(rows))
    par_ref[0], par_ref[1] = rre * p1[0] - rim * p1[1], rre * p1[1] + rim * p1[0]
    par_ref[2], par_ref[3] = pend
    steps = lax.broadcasted_iota(jnp.int32, (8, width), 0).astype(F32)
    filt = [jnp.zeros((8, width), F32) for _ in range(rows // 8)]
    for m in range(modes):
        ang = angle[m:m + 1] * steps
        mag = jnp.exp(-rate[m:m + 1] * steps)
        cre, cim = mag * jnp.cos(ang), mag * jnp.sin(ang)
        sre, sim = p8[0][m:m + 1], p8[1][m:m + 1]
        wre, wim = rre[m:m + 1], rim[m:m + 1]
        for j in range(rows // 8):
            qre_ref[m, j * 8:j * 8 + 8] = cre
            qim_ref[m, j * 8:j * 8 + 8] = cim
            filt[j] = filt[j] + wre * cre - wim * cim
            cre, cim = cre * sre - cim * sim, cre * sim + cim * sre
    first = lax.broadcasted_iota(jnp.int32, (8, width), 0) == 0
    filt[0] = filt[0] + jnp.where(first, skip_ref[...], 0.0)
    lspec_ref[...] = mm3(clh[...], cll[...], jnp.concatenate(filt, 0))


def prepare_kernel(rows, g_ref, x_hbm, t_hbm, o0, o1, o2, o3, p0, p1, p2, p3, x_ref, t_ref, kx, vx, gate, sems):
    outs, queries = (o0, o1, o2, o3), (p0, p1, p2, p3)
    g = g_ref[0]
    quarter = o0.shape[1]
    tiles = x_ref.shape[2] // 128
    short = pltpu.make_async_copy(t_hbm, t_ref, sems.at[tiles])
    short.start()
    loads = []
    for lt in range(tiles):
        ls = slice(lt * 128, lt * 128 + 128)
        loads.append(pltpu.make_async_copy(x_hbm.at[:, :, ls], x_ref.at[:, :, ls], sems.at[lt]))
        loads[-1].start()
    short.wait()
    for lt in range(tiles):
        ls = slice(lt * 128, lt * 128 + 128)
        loads[lt].wait()
        for src, ext in ((1, kx), (2, vx)):
            ext[lt, :8] = jnp.zeros((8, 128), F32)
            ext[lt, 8:] = x_ref[src, :, ls].astype(F32)
        tk = [jnp.broadcast_to(t_ref[1, j:j + 1, ls], (8, 128)) for j in range(7)]
        tv = [jnp.broadcast_to(t_ref[2, j:j + 1, ls], (8, 128)) for j in range(7)]
        for r in range(0, rows, 16):
            both = []
            for h in (0, 8):
                sk, sv = tk[0] * kx[lt, 8 + r + h:16 + r + h], tv[0] * vx[lt, 8 + r + h:16 + r + h]
                for j in range(1, 7):
                    o = 8 + r + h - j
                    sk, sv = sk + tk[j] * kx[lt, o:o + 8], sv + tv[j] * vx[lt, o:o + 8]
                both.append(sk * sv)
            gate[r:r + 16, ls] = jnp.concatenate(both, 0).astype(BF16)
    for m, (out, query) in enumerate(zip(outs, queries)):
        at = pl.ds(pl.multiple_of((g ^ m) * quarter, quarter), quarter)
        out[:rows] = gate[:, at]
        for i in (1, 2):
            ends = [x_ref[i, :16, at].astype(F32)[:8], x_ref[i, rows - 16:, at].astype(F32)[8:]]
            row = rows + 16 * (i - 1)
            out[row:row + 16] = jnp.concatenate(ends, 0).astype(BF16)
        out[rows + 32:rows + 48] = x_ref[0, rows - 16:, at]
        query[...] = x_ref[0, :, at]


def first_gates(before, ends, taps):
    out = []
    for i in (0, 1):
        ext = jnp.concatenate([before[16 * i + 8:16 * i + 16], ends[16 * i:16 * i + 8]], 0)
        t = taps[1 + i]
        acc = t[0:1] * ext[8:16]
        for j in range(1, 7):
            acc = acc + t[j:j + 1] * ext[8 - j:16 - j]
        out.append(acc)
    return out[0] * out[1]


def tail_part(tail, taps):
    ext = jnp.concatenate([tail, jnp.zeros_like(tail)], 0)
    out = taps[1:2] * ext[7:15]
    for lag in range(2, 7):
        out = out + taps[lag:lag + 1] * ext[8 - lag:16 - lag]
    return out


def end_states(rows, modes, per, flip, blocks, qre_ref, qim_ref, er, ei, width):
    for lt in range(width // 128):
        ls = slice(lt * 128, lt * 128 + 128)
        for m0 in range(0, modes, per):
            def step(j, acc):
                at = pl.ds(pl.multiple_of(j * 8, 8), 8)
                x = [flip[b, at, ls] for b in blocks]
                out = []
                for i in range(per):
                    qr, qi = qre_ref[m0 + i, at, ls], qim_ref[m0 + i, at, ls]
                    for b in range(len(blocks)):
                        k = (i * len(blocks) + b) * 2
                        out += [acc[k] + x[b] * qr, acc[k + 1] + x[b] * qi]
                return tuple(out)
            acc = lax.fori_loop(0, rows // 8, step, (jnp.zeros((8, 128), F32),) * (2 * len(blocks) * per), unroll=10 if len(blocks) > 1 else 20)
            for i in range(per):
                for b in range(len(blocks)):
                    k = (i * len(blocks) + b) * 2
                    er[b, m0 + i:m0 + i + 1, ls] = jnp.sum(acc[k], 0, keepdims=True)
                    ei[b, m0 + i:m0 + i + 1, ls] = jnp.sum(acc[k + 1], 0, keepdims=True)


def medium_of(gates, spec, cmh, cml, imh, iml):
    return mm3(imh[...], iml[...], cmul(mm(cmh[...], gates) + mm(cml[...], gates), spec))


def medium_kernel(rows, modes, g_ref, t_ref, spec_ref, qre_ref, qim_ref, par_ref,
                  consts, q0, q1, q2, q3,
                  med_ref, st_ref, out_ref, rim_ref, gate_ref, ends_ref, gx, flip, er, ei, ends):
    g = g_ref[0]
    cmh, cml, imh, iml = views(consts, rows, spec_ref.shape[0])[:4]
    width = gate_ref.shape[1]
    gx[:128] = jnp.zeros_like(gx[:128])
    for m, msg in enumerate((q0, q1, q2, q3)):
        gx[pl.ds(pl.multiple_of(128 + (g ^ m) * rows, 16), rows), :] = msg[:rows]
        ends[g ^ m] = msg[rows:rows + 32].astype(F32)
    gate_ref[...] = gx[128:128 + rows]
    ends_ref[...] = ends[0]
    rim_ref[:128] = gx[GROUP * rows:]
    rim_ref[128:160] = ends[GROUP - 1].astype(BF16)
    for b in range(1, GROUP):
        top = 128 + b * rows
        head = first_gates(ends[b - 1], ends[b], t_ref)
        gx[top:top + 16] = jnp.concatenate([head, gx[top:top + 16].astype(F32)[8:]], 0).astype(BF16)
    ext = jnp.concatenate([gx[b * rows:b * rows + rows + 128] for b in range(GROUP)], 1)
    both = medium_of(ext, jnp.concatenate([spec_ref[...]] * GROUP, 1), cmh, cml, imh, iml)
    for b in range(GROUP):
        med_ref[b] = both[:rows, b * width:(b + 1) * width]
        flip[b] = both[rows:, b * width:(b + 1) * width]
    end_states(rows, modes, 4, flip, range(GROUP), qre_ref, qim_ref, er, ei, width)
    dre, dim = par_ref[2], par_ref[3]
    sre = jnp.zeros((modes, width), F32)
    sim = sre
    for b in range(GROUP):
        st_ref[b, 0], st_ref[b, 1] = er[b], ei[b]
        sre, sim = dre * sre - dim * sim + er[b], dre * sim + dim * sre + ei[b]
    out_ref[:modes] = sre
    out_ref[modes:2 * modes] = sim
    for m, q in enumerate((q0, q1, q2, q3)):
        @pl.when((g ^ m) == GROUP - 1)
        def _():
            out_ref[2 * modes:] = q[rows + 32:].astype(F32)[8:]


def intra_kernel(rows, g_ref, t_ref, med_ref, lspec_ref, consts, q0, q1, q2, q3, intra_ref, query_ref, qx):
    g = g_ref[0]
    _, _, _, _, clh, cll, ilh, ill = views(consts, rows, med_ref.shape[1] + 128)
    for b in range(1, GROUP):
        intra_ref[b - 1] = mm3(ilh[...], ill[...], cmul(mm3(clh[...], cll[...], med_ref[b]), lspec_ref[...]))
    total = GROUP * rows
    for lt in range(query_ref.shape[1] // 128):
        ls = slice(lt * 128, lt * 128 + 128)
        qx[lt, :8] = jnp.zeros((8, 128), F32)
        for m, q in enumerate((q0, q1, q2, q3)):
            qx[lt, pl.ds(pl.multiple_of((g ^ m) * rows + 8, 8), rows), :] = q[:, ls].astype(F32)
        t = [jnp.broadcast_to(t_ref[0, j:j + 1, ls], (8, 128)) for j in range(7)]
        for r in range(0, total, 8):
            acc = t[0] * qx[lt, 8 + r:16 + r]
            for j in range(1, 7):
                acc = acc + t[j] * qx[lt, 8 + r - j:16 + r - j]
            query_ref[r:r + 8, ls] = acc


def hidden_kernel(rows, modes, g_ref, t_ref, in_ref, rim_ref, gate_ref, ends_ref, spec_ref, lspec_ref, st_ref, par_ref,
                  qre_ref, qim_ref, later_ref, query_ref, consts,
                  hid_ref, amp, gx, flip, er, ei, intra):
    part = g_ref[1]
    live = (part > 0).astype(F32)
    width = query_ref.shape[1]
    cmh, cml, imh, iml, clh, cll, ilh, ill = views(consts, rows, gx.shape[0])
    gx[:128] = (rim_ref[:128].astype(F32) * live).astype(BF16)
    head = first_gates(rim_ref[128:160].astype(F32) * live, ends_ref[...], t_ref)
    gx[128:] = gate_ref[...]
    gx[128:144] = jnp.concatenate([head, gate_ref[:16].astype(F32)[8:]], 0).astype(BF16)
    both = medium_of(gx[...], spec_ref[...], cmh, cml, imh, iml)
    flip[0] = both[rows:]
    intra[0] = mm3(ilh[...], ill[...], cmul(mm3(clh[...], cll[...], both[:rows]), lspec_ref[...]))
    end_states(rows, modes, 8, flip, range(1), qre_ref, qim_ref, er, ei, width)
    sre, sim = in_ref[:modes] * live, in_ref[modes:2 * modes] * live
    rre, rim, dre, dim = par_ref[0], par_ref[1], par_ref[2], par_ref[3]
    for b in range(GROUP):
        are, aim = rre * sre - rim * sim, rre * sim + rim * sre
        for m in range(modes):
            amp[b, m, 0] = jnp.broadcast_to(are[m:m + 1], (8, width))
            amp[b, m, 1] = jnp.broadcast_to(aim[m:m + 1], (8, width))
        ere, eim = (er[0], ei[0]) if b == 0 else (st_ref[b, 0], st_ref[b, 1])
        sre, sim = dre * sre - dim * sim + ere, dre * sim + dim * sre + eim
    query_ref[:8] = query_ref[:8] + tail_part(in_ref[2 * modes:] * live, t_ref[0])
    for lt in range(width // 128):
        ls = slice(lt * 128, lt * 128 + 128)

        def step(j, carry):
            at = [pl.ds(pl.multiple_of(j * 16 + 8 * i, 8), 8) for i in range(2)]
            acc = [[intra[0, at[i], ls] for i in range(2)]]
            acc += [[later_ref[b, at[i], ls] for i in range(2)] for b in range(GROUP - 1)]
            for m in range(modes):
                qr = [qre_ref[m, at[i], ls] for i in range(2)]
                qi = [qim_ref[m, at[i], ls] for i in range(2)]
                for b in range(GROUP):
                    ar, ai = amp[b, m, 0, :, ls], amp[b, m, 1, :, ls]
                    for i in range(2):
                        acc[b][i] = acc[b][i] + ar * qr[i] - ai * qi[i]
            for b in range(GROUP):
                row = pl.multiple_of(b * rows + j * 16, 16)
                long = jnp.concatenate(acc[b], 0)
                hid_ref[pl.ds(row, 16), ls] = (query_ref[pl.ds(row, 16), ls] * long).astype(BF16)
            return carry

        lax.fori_loop(0, rows // 16, step, 0)


def project_kernel(c, g_ref, h0, h1, h2, h3, wa_ref, early, out_late, in_late, keep_ref, send_ref, wb_ref):
    g, own, core, at_end, cut = g_ref[0], g_ref[2] != c, g_ref[3], g_ref[6], early.shape[0]
    quarter = h0.shape[1]
    half = wa_ref.shape[1] // 2
    mine = pl.ds(pl.multiple_of(core * half, half), half)
    other = pl.ds(pl.multiple_of((1 - core) * half, half), half)

    def run(weight):
        keep = send = None
        for m, h in enumerate((h0, h1, h2, h3)):
            at = pl.ds(pl.multiple_of((g ^ m) * quarter, quarter), quarter)
            x = h[...]
            a, b = mm(x, weight[at, mine]), mm(x, weight[at, other])
            keep, send = (a, b) if m == 0 else (keep + a, send + b)
        keep_ref[...] = keep
        send_ref[...] = send.astype(BF16)

    @pl.when(own)
    def _():
        run(wa_ref)

    @pl.when(jnp.logical_not(own))
    def _():
        wb_ref[:cut] = early[...]

        @pl.when(at_end > 0)
        def _():
            wb_ref[cut:] = out_late[...]

        @pl.when(at_end == 0)
        def _():
            wb_ref[cut:] = in_late[...]

        run(wb_ref)


def sort_kernel(rows, g_ref, keep_ref, got_ref, *outs):
    low, core = g_ref[4], g_ref[3]
    for n, out in enumerate(outs):
        block = 2 * (core ^ (n >> 1)) + (low ^ (n & 1))
        at = pl.ds(pl.multiple_of(block * rows, rows), rows)
        out[...] = (keep_ref[at, :] + got_ref[at, :].astype(F32)).astype(BF16)


def gather_kernel(g_ref, *refs):
    out_ref = refs[-1]
    low, high = g_ref[4], g_ref[5]
    width = refs[0].shape[1]
    for n in range(4):
        a, b = n >> 1, n & 1
        at = pl.ds(pl.multiple_of((2 * (low ^ b) + (high ^ a)) * width, width), width)
        out_ref[:, at] = (refs[2 * n][...].astype(F32) + refs[2 * n + 1][...].astype(F32)).astype(BF16)


def call(us, kernel, outs, args, scratch=()):
    return pl.pallas_call(
        kernel,
        out_shape=tuple(jax.ShapeDtypeStruct(s, d) for s, d in outs),
        in_specs=[SMEM] + [VMEM] * (len(args) - 1),
        out_specs=(VMEM,) * len(outs),
        scratch_shapes=[pltpu.VMEM(s, d) for s, d in scratch],
        compiler_params=params(),
        cost_estimate=pl.CostEstimate(flops=int(us * 1.15e9), bytes_accessed=int(us * 3.69e6), transcendentals=0),
    )(*args)


def fast_body(streams, short_taps, mix_taps, pole_rate, pole_angle, residue, skip, out_weight):
    rows, _, width = streams.shape
    modes = pole_rate.shape[0]
    ntap = mix_taps.shape[0]
    quarter = width // GROUP
    total = GROUP * rows
    ctx, tp = lax.axis_index("ctx"), lax.axis_index("tp")
    g, part = ctx % GROUP, ctx // GROUP
    core, y = tp % 2, tp // 2
    scal = jnp.stack([g, part, (y == part).astype(jnp.int32), core, g % 2, g // 2, (part == g // 2).astype(jnp.int32)]).astype(jnp.int32)

    cut = width * EARLY // 16
    size_m = rows + ntap
    back = np.concatenate([np.arange(ntap, size_m), np.arange(ntap, size_m)[::-1]])
    mats = [odd_dft(size_m, size_m), odd_idft(size_m, back), odd_dft(2 * rows, rows), odd_idft(2 * rows, np.arange(rows))]
    consts = np.concatenate([
        np.pad(half, ((0, 0), (0, 2 * rows - half.shape[1]))) for mat in mats for half in split_const(mat)], 0)

    short_taps = short_taps.transpose(1, 0, 2)
    anywhere = pl.BlockSpec(memory_space=pltpu.HBM)
    sent = pl.pallas_call(
        lambda *refs: prepare_kernel(rows, *refs),
        out_shape=tuple(jax.ShapeDtypeStruct((r, quarter), BF16) for r in (rows + 48,) * GROUP + (rows,) * GROUP),
        in_specs=[SMEM, anywhere, anywhere],
        out_specs=(VMEM,) * (2 * GROUP),
        scratch_shapes=[pltpu.VMEM((3, rows, width), BF16), pltpu.VMEM((3, 7, width), F32)]
        + [pltpu.VMEM((width // 128, rows + 8, 128), F32)] * 2
        + [pltpu.VMEM((rows, width), BF16), pltpu.SemaphoreType.DMA((width // 128 + 1,))],
        compiler_params=params(),
        cost_estimate=pl.CostEstimate(flops=int(2e9), bytes_accessed=int(6e6), transcendentals=0),
    )(scal, streams.transpose(1, 0, 2), short_taps)
    msgs, qs = sent[:GROUP], sent[GROUP:]
    early = swap(out_weight[:cut], BITS_FAR)
    msgs = [msgs[0]] + [swap(msgs[m], SLOT_BITS[m]) for m in (1, 2, 3)]
    spec, lspec, qre, qim, par, taps = call(
        0.3,
        lambda *refs: filters_kernel(rows, modes, *refs),
        [(s, F32) for s in ((size_m, quarter), (2 * rows, quarter), (modes, rows, quarter), (modes, rows, quarter),
                            (4, modes, quarter), (3, 7, quarter))],
        (scal, mix_taps, pole_rate, pole_angle, residue, skip[None], short_taps, consts),
    )
    spec, qs = lax.optimization_barrier((spec, qs))
    qs = [qs[0]] + [swap(qs[m], SLOT_BITS[m]) for m in (1, 2, 3)]
    med, st, out, rim, gate, ends = call(
        0.6,
        lambda *refs: medium_kernel(rows, modes, *refs),
        [((GROUP, rows, quarter), F32), ((GROUP, 2, modes, quarter), F32), ((2 * modes + 8, quarter), F32),
         ((160, quarter), BF16), ((rows, quarter), BF16), ((32, quarter), F32)],
        (scal, taps, spec, qre, qim, par, consts, *msgs),
        [((total + 128, quarter), BF16), ((GROUP, rows, quarter), F32), ((GROUP, modes, quarter), F32), ((GROUP, modes, quarter), F32),
         ((GROUP, 32, quarter), F32)],
    )
    out, rim, early = lax.optimization_barrier((out, rim, early))
    state_in, rim_in = swap(out, BIT_PART), swap(rim, BIT_PART)
    later, query = call(
        3.1,
        lambda *refs: intra_kernel(rows, *refs),
        [((GROUP - 1, rows, quarter), F32), ((total, quarter), F32)],
        (scal, taps, med, lspec, consts, *qs),
        [((quarter // 128, total + 8, 128), F32)],
    )
    late, later = lax.optimization_barrier((out_weight[cut:], later))
    out_late = far_swap(late, True)
    (hidden,) = call(
        5.2,
        lambda *refs: hidden_kernel(rows, modes, *refs),
        [((total, quarter), BF16)],
        (scal, taps, state_in, rim_in, gate, ends, spec, lspec, st, par, qre, qim, later, query, consts),
        [((GROUP, modes, 2, 8, quarter), F32), ((rows + 128, quarter), BF16), ((1, rows, quarter), F32),
         ((1, modes, quarter), F32), ((1, modes, quarter), F32), ((1, rows, quarter), F32)],
    )
    hidden, late = lax.optimization_barrier((hidden, out_weight[cut:]))
    in_late = far_swap(late, False)
    hid = [hidden] + [swap(hidden, SLOT_BITS[m]) for m in (1, 2, 3)]
    half = out_weight.shape[1] // 2
    blocks = {}
    for c in (1, 0):
        keep, send = call(
            1.2,
            lambda *refs: project_kernel(c, *refs),
            [((total, half), F32), ((total, half), BF16)],
            (scal, *hid, out_weight, early, out_late, in_late),
            [((width, 2 * half), BF16)],
        )
        send, hid = lax.optimization_barrier((send, hid))
        parts = call(
            0.4,
            lambda *refs: sort_kernel(rows, *refs),
            [((rows, half), BF16)] * GROUP,
            (scal, keep, swap(send, BIT_CORE)),
        )
        for n, part in enumerate(parts):
            blocks[n, c] = lax.ppermute(part, AXES, homeward(n >> 1, n & 1, c))
    blocks = [blocks[n, c] for n in range(GROUP) for c in (0, 1)]
    (mixed,) = call(1.3, gather_kernel, [((rows, 4 * half), BF16)], (scal, *blocks))
    return mixed


def from_behind(block, axis, distance):
    devices = range(lax.axis_size(axis))
    route = [(i - distance, i) for i in devices if i - distance in devices]
    return lax.ppermute(block, axis, route)


def depthwise(ext, taps):
    width = taps.shape[1]
    kernel = taps[::-1][:, None, :]
    out = lax.conv_general_dilated(
        ext[None],
        kernel,
        (1,),
        "VALID",
        dimension_numbers=("NWC", "WIO", "NWC"),
        feature_group_count=width,
        precision=lax.Precision.HIGHEST,
    )
    return out[0]


def general_body(streams, short_taps, mix_taps, pole_rate, pole_angle, residue, skip, out_weight):
    rows, three, width = streams.shape
    modes = pole_rate.shape[0]
    short = short_taps.reshape(7, three * width)
    rim = from_behind(streams[rows - 6 :], "ctx", 1)
    ext = jnp.concatenate([rim, streams], 0).astype(jnp.float32).reshape(rows + 6, three * width)
    conv = depthwise(ext, short).reshape(rows, three, width)
    gate = (conv[:, 1] * conv[:, 2]).astype(jnp.bfloat16)
    gate_rim = from_behind(gate[rows - 127 :], "ctx", 1)
    gate_ext = jnp.concatenate([gate_rim, gate], 0)
    query = conv[:, 0]
    medium = depthwise(gate_ext.astype(jnp.float32), mix_taps)
    amp = jnp.sqrt(1.0 - jnp.exp(-2.0 * pole_rate))
    res_re = residue[0] * amp
    res_im = residue[1] * amp
    steps = jnp.arange(rows).astype(jnp.float32)[:, None]
    flipped = medium[::-1]

    def first_pass(mode, carry):
        filt, end_re, end_im = carry
        rate = pole_rate[mode][None]
        angle = pole_angle[mode][None]
        mag = jnp.exp(-rate * steps)
        cosk = mag * jnp.cos(angle * steps)
        sink = mag * jnp.sin(angle * steps)
        filt = filt + res_re[mode][None] * cosk - res_im[mode][None] * sink
        end_re = end_re.at[mode].set(jnp.sum(flipped * cosk, 0))
        end_im = end_im.at[mode].set(jnp.sum(flipped * sink, 0))
        return (filt, end_re, end_im)

    zero_state = jnp.zeros((modes, width), jnp.float32)
    filt, end_re, end_im = lax.fori_loop(
        0, modes, first_pass, (jnp.zeros((rows, width), jnp.float32), zero_state, zero_state)
    )
    dec_mag = jnp.exp(-pole_rate * rows)
    dec_re = dec_mag * jnp.cos(pole_angle * rows)
    dec_im = dec_mag * jnp.sin(pole_angle * rows)

    def relay_step(turn, received):
        in_re, in_im = received
        out_re = dec_re * in_re - dec_im * in_im + end_re
        out_im = dec_re * in_im + dec_im * in_re + end_im
        return from_behind((out_re, out_im), "ctx", 1)

    st_re, st_im = lax.fori_loop(0, lax.axis_size("ctx") - 1, relay_step, (zero_state, zero_state))
    later = steps + 1.0

    def second_pass(mode, inflow):
        rate = pole_rate[mode][None]
        angle = pole_angle[mode][None]
        mag = jnp.exp(-rate * later)
        cos1 = mag * jnp.cos(angle * later)
        sin1 = mag * jnp.sin(angle * later)
        are = res_re[mode] * st_re[mode] - res_im[mode] * st_im[mode]
        aim = res_re[mode] * st_im[mode] + res_im[mode] * st_re[mode]
        return inflow + are[None] * cos1 - aim[None] * sin1

    inflow = lax.fori_loop(0, modes, second_pass, jnp.zeros((rows, width), jnp.float32))
    padded = jnp.concatenate([jnp.zeros((rows - 1, width), jnp.float32), medium], 0)
    intra = depthwise(padded, filt)
    longf = intra + inflow + skip[None] * medium
    hidden = (query * longf).astype(jnp.bfloat16)
    partial_out = jnp.dot(
        hidden,
        lax.all_gather(out_weight, "ctx", axis=1, tiled=True),
        preferred_element_type=jnp.float32,
    )
    return lax.psum_scatter(partial_out, "tp", scatter_dimension=1, tiled=True).astype(jnp.bfloat16)


def solution(mesh):
    fast = dict(mesh.shape) == {"ctx": 8, "tp": 4}
    return jax.shard_map(
        fast_body if fast else general_body,
        mesh=mesh,
        in_specs=(
            P("ctx", None, "tp"),
            P(None, None, "tp"),
            P(None, "tp"),
            P(None, "tp"),
            P(None, "tp"),
            P(None, None, "tp"),
            P("tp"),
            P("tp", "ctx"),
        ),
        out_specs=P("ctx", "tp"),
        check_vma=False,
    )
```

```python
import jax
import jax.numpy as jnp
import ml_dtypes
import numpy as np
from jax import lax
from jax.experimental import pallas as pl
from jax.experimental.pallas import tpu as pltpu
from jax.sharding import PartitionSpec as P

F32 = jnp.float32
BF16 = jnp.bfloat16
AXES = ("ctx", "tp")
GROUP = 4
BIT_CORE, BIT_PART, BITS_FAR = 1, 16, 24
EARLY = 9
SLOT_BITS = (0, 4, 8, 12)
VMEM = pl.BlockSpec(memory_space=pltpu.VMEM)
SMEM = pl.BlockSpec(memory_space=pltpu.SMEM)


def swap(block, bits):
    return lax.ppermute(block, AXES, [(i, i ^ bits) for i in range(32)])


def homeward(a, b, c):
    route = []
    for i in range(32):
        high, low, y, core = i >> 3 & 1, i >> 2 & 1, i >> 1 & 1, i & 1
        part, row = i >> 4, y ^ c
        route.append((i, part * 16 + (core ^ a) * 8 + (low ^ b) * 4 + row * 2 + (high ^ part ^ row)))
    return route


def outer(i):
    return (i >> 4) == (i >> 3 & 1)


def far_swap(block, ends):
    return lax.ppermute(block, AXES, [(i, i ^ BITS_FAR) for i in range(32) if outer(i) == ends])


def split_const(mat):
    hi = mat.astype(ml_dtypes.bfloat16)
    lo = (mat - hi.astype(np.float64)).astype(ml_dtypes.bfloat16)
    return hi, lo


def odd_dft(size, rows_in):
    freq = 2 * np.pi * (np.arange(size // 2) + 0.5) / size
    ang = freq[:, None] * np.arange(rows_in)
    return np.concatenate([np.cos(ang), -np.sin(ang)], 0)


def odd_idft(size, rows_out):
    freq = 2 * np.pi * (np.arange(size // 2) + 0.5) / size
    ang = np.asarray(rows_out)[:, None] * freq
    return np.concatenate([np.cos(ang), -np.sin(ang)], 1) * (2.0 / size)


def mm(a, b):
    return jnp.dot(a, b, preferred_element_type=F32)


def split(x):
    hi = x.astype(BF16)
    return hi, (x - hi.astype(F32)).astype(BF16)


def mm3(hi, lo, x):
    xh, xl = split(x)
    return mm(hi, xh) + mm(lo, xh) + mm(hi, xl)


def cmul(spec, filt):
    half = spec.shape[0] // 2
    a, b, c, d = spec[:half], spec[half:], filt[:half], filt[half:]
    return jnp.concatenate([a * c - b * d, a * d + b * c], 0)


class View:
    def __init__(self, ref, top, high, wide):
        self.ref, self.top, self.high, self.wide = ref, top, high, wide

    def __getitem__(self, key):
        wide = self.wide if key is Ellipsis else key[1].stop
        return self.ref[self.top:self.top + self.high, :wide]


def views(consts, rows, size):
    out, top = [], 0
    for high, wide in ((size, size), (2 * rows, size), (2 * rows, rows), (rows, 2 * rows)):
        for _ in range(2):
            out.append(View(consts, top, high, wide))
            top += high
    return out


def params(**kw):
    return pltpu.CompilerParams(vmem_limit_bytes=16 * 1024 * 1024, **kw)


def filters_kernel(rows, modes, g_ref, taps_ref, rate_all, angle_all, res_all, skip_all, short_all, consts,
                   spec_ref, lspec_ref, qre_ref, qim_ref, par_ref, short_ref):
    width = spec_ref.shape[1]
    ntap = taps_ref.shape[0]
    cmh, cml, _, _, clh, cll, _, _ = views(consts, rows, spec_ref.shape[0])
    at = pl.ds(pl.multiple_of(g_ref[0] * width, width), width)
    spec_ref[...] = mm3(cmh[:, :ntap], cml[:, :ntap], taps_ref[:, at])
    short_ref[...] = short_all[:, :, at]
    rate_ref, angle_ref, res_ref, skip_ref = rate_all[:, at], angle_all[:, at], res_all[:, :, at], skip_all[:, at]
    rate, angle = rate_ref[...], angle_ref[...]
    amp = jnp.sqrt(1.0 - jnp.exp(-2.0 * rate))
    rre, rim = res_ref[0] * amp, res_ref[1] * amp

    def power(n):
        mag = jnp.exp(-rate * n)
        return mag * jnp.cos(angle * n), mag * jnp.sin(angle * n)

    p1, p8, pend = power(1.0), power(8.0), power(float(rows))
    par_ref[0], par_ref[1] = rre * p1[0] - rim * p1[1], rre * p1[1] + rim * p1[0]
    par_ref[2], par_ref[3] = pend
    steps = lax.broadcasted_iota(jnp.int32, (8, width), 0).astype(F32)
    filt = [jnp.zeros((8, width), F32) for _ in range(rows // 8)]
    for m in range(modes):
        ang = angle[m:m + 1] * steps
        mag = jnp.exp(-rate[m:m + 1] * steps)
        cre, cim = mag * jnp.cos(ang), mag * jnp.sin(ang)
        sre, sim = p8[0][m:m + 1], p8[1][m:m + 1]
        wre, wim = rre[m:m + 1], rim[m:m + 1]
        for j in range(rows // 8):
            qre_ref[m, j * 8:j * 8 + 8] = cre
            qim_ref[m, j * 8:j * 8 + 8] = cim
            filt[j] = filt[j] + wre * cre - wim * cim
            cre, cim = cre * sre - cim * sim, cre * sim + cim * sre
    first = lax.broadcasted_iota(jnp.int32, (8, width), 0) == 0
    filt[0] = filt[0] + jnp.where(first, skip_ref[...], 0.0)
    lspec_ref[...] = mm3(clh[...], cll[...], jnp.concatenate(filt, 0))


def prepare_kernel(rows, g_ref, x_hbm, t_hbm, o0, o1, o2, o3, p0, p1, p2, p3, x_ref, t_ref, kx, vx, gate, sems):
    outs, queries = (o0, o1, o2, o3), (p0, p1, p2, p3)
    g = g_ref[0]
    quarter = o0.shape[1]
    tiles = x_ref.shape[2] // 128
    short = pltpu.make_async_copy(t_hbm, t_ref, sems.at[tiles])
    short.start()
    loads = []
    for lt in range(tiles):
        ls = slice(lt * 128, lt * 128 + 128)
        loads.append(pltpu.make_async_copy(x_hbm.at[:, :, ls], x_ref.at[:, :, ls], sems.at[lt]))
        loads[-1].start()
    short.wait()
    for lt in range(tiles):
        ls = slice(lt * 128, lt * 128 + 128)
        loads[lt].wait()
        for src, ext in ((1, kx), (2, vx)):
            ext[lt, :8] = jnp.zeros((8, 128), F32)
            ext[lt, 8:] = x_ref[src, :, ls].astype(F32)
        tk = [jnp.broadcast_to(t_ref[1, j:j + 1, ls], (8, 128)) for j in range(7)]
        tv = [jnp.broadcast_to(t_ref[2, j:j + 1, ls], (8, 128)) for j in range(7)]
        for r in range(0, rows, 16):
            both = []
            for h in (0, 8):
                sk, sv = tk[0] * kx[lt, 8 + r + h:16 + r + h], tv[0] * vx[lt, 8 + r + h:16 + r + h]
                for j in range(1, 7):
                    o = 8 + r + h - j
                    sk, sv = sk + tk[j] * kx[lt, o:o + 8], sv + tv[j] * vx[lt, o:o + 8]
                both.append(sk * sv)
            gate[r:r + 16, ls] = jnp.concatenate(both, 0).astype(BF16)
    for m, (out, query) in enumerate(zip(outs, queries)):
        at = pl.ds(pl.multiple_of((g ^ m) * quarter, quarter), quarter)
        out[:rows] = gate[:, at]
        for i in (1, 2):
            ends = [x_ref[i, :16, at].astype(F32)[:8], x_ref[i, rows - 16:, at].astype(F32)[8:]]
            row = rows + 16 * (i - 1)
            out[row:row + 16] = jnp.concatenate(ends, 0).astype(BF16)
        out[rows + 32:rows + 48] = x_ref[0, rows - 16:, at]
        query[...] = x_ref[0, :, at]


def first_gates(before, ends, taps):
    out = []
    for i in (0, 1):
        ext = jnp.concatenate([before[16 * i + 8:16 * i + 16], ends[16 * i:16 * i + 8]], 0)
        t = taps[1 + i]
        acc = t[0:1] * ext[8:16]
        for j in range(1, 7):
            acc = acc + t[j:j + 1] * ext[8 - j:16 - j]
        out.append(acc)
    return out[0] * out[1]


def tail_part(tail, taps):
    ext = jnp.concatenate([tail, jnp.zeros_like(tail)], 0)
    out = taps[1:2] * ext[7:15]
    for lag in range(2, 7):
        out = out + taps[lag:lag + 1] * ext[8 - lag:16 - lag]
    return out


def end_states(rows, modes, per, flip, blocks, qre_ref, qim_ref, er, ei, width):
    for lt in range(width // 128):
        ls = slice(lt * 128, lt * 128 + 128)
        for m0 in range(0, modes, per):
            def step(j, acc):
                at = pl.ds(pl.multiple_of(j * 8, 8), 8)
                x = [flip[b, at, ls] for b in blocks]
                out = []
                for i in range(per):
                    qr, qi = qre_ref[m0 + i, at, ls], qim_ref[m0 + i, at, ls]
                    for b in range(len(blocks)):
                        k = (i * len(blocks) + b) * 2
                        out += [acc[k] + x[b] * qr, acc[k + 1] + x[b] * qi]
                return tuple(out)
            acc = lax.fori_loop(0, rows // 8, step, (jnp.zeros((8, 128), F32),) * (2 * len(blocks) * per), unroll=10 if len(blocks) > 1 else 20)
            for i in range(per):
                for b in range(len(blocks)):
                    k = (i * len(blocks) + b) * 2
                    er[b, m0 + i:m0 + i + 1, ls] = jnp.sum(acc[k], 0, keepdims=True)
                    ei[b, m0 + i:m0 + i + 1, ls] = jnp.sum(acc[k + 1], 0, keepdims=True)


def medium_of(gates, spec, cmh, cml, imh, iml):
    return mm3(imh[...], iml[...], cmul(mm(cmh[...], gates) + mm(cml[...], gates), spec))


def medium_kernel(rows, modes, g_ref, t_ref, spec_ref, qre_ref, qim_ref, par_ref,
                  consts, q0, q1, q2, q3,
                  med_ref, st_ref, out_ref, rim_ref, gate_ref, ends_ref, gx, flip, er, ei, ends):
    g = g_ref[0]
    cmh, cml, imh, iml = views(consts, rows, spec_ref.shape[0])[:4]
    width = gate_ref.shape[1]
    gx[:128] = jnp.zeros_like(gx[:128])
    for m, msg in enumerate((q0, q1, q2, q3)):
        gx[pl.ds(pl.multiple_of(128 + (g ^ m) * rows, 16), rows), :] = msg[:rows]
        ends[g ^ m] = msg[rows:rows + 32].astype(F32)
    gate_ref[...] = gx[128:128 + rows]
    ends_ref[...] = ends[0]
    rim_ref[:128] = gx[GROUP * rows:]
    rim_ref[128:160] = ends[GROUP - 1].astype(BF16)
    for b in range(1, GROUP):
        top = 128 + b * rows
        head = first_gates(ends[b - 1], ends[b], t_ref)
        gx[top:top + 16] = jnp.concatenate([head, gx[top:top + 16].astype(F32)[8:]], 0).astype(BF16)
    ext = jnp.concatenate([gx[b * rows:b * rows + rows + 128] for b in range(GROUP)], 1)
    both = medium_of(ext, jnp.concatenate([spec_ref[...]] * GROUP, 1), cmh, cml, imh, iml)
    for b in range(GROUP):
        med_ref[b] = both[:rows, b * width:(b + 1) * width]
        flip[b] = both[rows:, b * width:(b + 1) * width]
    end_states(rows, modes, 4, flip, range(GROUP), qre_ref, qim_ref, er, ei, width)
    dre, dim = par_ref[2], par_ref[3]
    sre = jnp.zeros((modes, width), F32)
    sim = sre
    for b in range(GROUP):
        st_ref[b, 0], st_ref[b, 1] = er[b], ei[b]
        sre, sim = dre * sre - dim * sim + er[b], dre * sim + dim * sre + ei[b]
    out_ref[:modes] = sre
    out_ref[modes:2 * modes] = sim
    for m, q in enumerate((q0, q1, q2, q3)):
        @pl.when((g ^ m) == GROUP - 1)
        def _():
            out_ref[2 * modes:] = q[rows + 32:].astype(F32)[8:]


def intra_kernel(rows, g_ref, t_ref, med_ref, lspec_ref, consts, q0, q1, q2, q3, intra_ref, query_ref, qx):
    g = g_ref[0]
    _, _, _, _, clh, cll, ilh, ill = views(consts, rows, med_ref.shape[1] + 128)
    for b in range(1, GROUP):
        intra_ref[b - 1] = mm3(ilh[...], ill[...], cmul(mm3(clh[...], cll[...], med_ref[b]), lspec_ref[...]))
    total = GROUP * rows
    for lt in range(query_ref.shape[1] // 128):
        ls = slice(lt * 128, lt * 128 + 128)
        qx[lt, :8] = jnp.zeros((8, 128), F32)
        for m, q in enumerate((q0, q1, q2, q3)):
            qx[lt, pl.ds(pl.multiple_of((g ^ m) * rows + 8, 8), rows), :] = q[:, ls].astype(F32)
        t = [jnp.broadcast_to(t_ref[0, j:j + 1, ls], (8, 128)) for j in range(7)]
        for r in range(0, total, 8):
            acc = t[0] * qx[lt, 8 + r:16 + r]
            for j in range(1, 7):
                acc = acc + t[j] * qx[lt, 8 + r - j:16 + r - j]
            query_ref[r:r + 8, ls] = acc


def hidden_kernel(rows, modes, g_ref, t_ref, in_ref, rim_ref, gate_ref, ends_ref, spec_ref, lspec_ref, st_ref, par_ref,
                  qre_ref, qim_ref, later_ref, query_ref, consts,
                  hid_ref, amp, gx, flip, er, ei, intra):
    part = g_ref[1]
    live = (part > 0).astype(F32)
    width = query_ref.shape[1]
    cmh, cml, imh, iml, clh, cll, ilh, ill = views(consts, rows, gx.shape[0])
    gx[:128] = (rim_ref[:128].astype(F32) * live).astype(BF16)
    head = first_gates(rim_ref[128:160].astype(F32) * live, ends_ref[...], t_ref)
    gx[128:] = gate_ref[...]
    gx[128:144] = jnp.concatenate([head, gate_ref[:16].astype(F32)[8:]], 0).astype(BF16)
    both = medium_of(gx[...], spec_ref[...], cmh, cml, imh, iml)
    flip[0] = both[rows:]
    intra[0] = mm3(ilh[...], ill[...], cmul(mm3(clh[...], cll[...], both[:rows]), lspec_ref[...]))
    end_states(rows, modes, 8, flip, range(1), qre_ref, qim_ref, er, ei, width)
    sre, sim = in_ref[:modes] * live, in_ref[modes:2 * modes] * live
    rre, rim, dre, dim = par_ref[0], par_ref[1], par_ref[2], par_ref[3]
    for b in range(GROUP):
        are, aim = rre * sre - rim * sim, rre * sim + rim * sre
        for m in range(modes):
            amp[b, m, 0] = jnp.broadcast_to(are[m:m + 1], (8, width))
            amp[b, m, 1] = jnp.broadcast_to(aim[m:m + 1], (8, width))
        ere, eim = (er[0], ei[0]) if b == 0 else (st_ref[b, 0], st_ref[b, 1])
        sre, sim = dre * sre - dim * sim + ere, dre * sim + dim * sre + eim
    query_ref[:8] = query_ref[:8] + tail_part(in_ref[2 * modes:] * live, t_ref[0])
    for lt in range(width // 128):
        ls = slice(lt * 128, lt * 128 + 128)

        def step(j, carry):
            at = [pl.ds(pl.multiple_of(j * 16 + 8 * i, 8), 8) for i in range(2)]
            acc = [[intra[0, at[i], ls] for i in range(2)]]
            acc += [[later_ref[b, at[i], ls] for i in range(2)] for b in range(GROUP - 1)]
            for m in range(modes):
                qr = [qre_ref[m, at[i], ls] for i in range(2)]
                qi = [qim_ref[m, at[i], ls] for i in range(2)]
                for b in range(GROUP):
                    ar, ai = amp[b, m, 0, :, ls], amp[b, m, 1, :, ls]
                    for i in range(2):
                        acc[b][i] = acc[b][i] + ar * qr[i] - ai * qi[i]
            for b in range(GROUP):
                row = pl.multiple_of(b * rows + j * 16, 16)
                long = jnp.concatenate(acc[b], 0)
                hid_ref[pl.ds(row, 16), ls] = (query_ref[pl.ds(row, 16), ls] * long).astype(BF16)
            return carry

        lax.fori_loop(0, rows // 16, step, 0)


def project_kernel(c, g_ref, h0, h1, h2, h3, h4, wa_ref, early, out_late, in_late, keep_ref, send_ref, wb_ref):
    g, own, core, at_end, cut = g_ref[0], g_ref[2] != c, g_ref[3], g_ref[6], early.shape[0]
    quarter = h0.shape[1]
    half = wa_ref.shape[1] // 2
    mine = pl.ds(pl.multiple_of(core * half, half), half)
    other = pl.ds(pl.multiple_of((1 - core) * half, half), half)

    def run(weight):
        keep = send = None
        for m, h in enumerate((h0, h1, h2, None)):
            at = pl.ds(pl.multiple_of((g ^ m) * quarter, quarter), quarter)
            x = h[...] if m < 3 else jnp.concatenate([h3[...], h4[...]], 0)
            a, b = mm(x, weight[at, mine]), mm(x, weight[at, other])
            keep, send = (a, b) if m == 0 else (keep + a, send + b)
        keep_ref[...] = keep
        send_ref[...] = send.astype(BF16)

    @pl.when(own)
    def _():
        run(wa_ref)

    @pl.when(jnp.logical_not(own))
    def _():
        wb_ref[:cut] = early[...]

        @pl.when(at_end > 0)
        def _():
            wb_ref[cut:] = out_late[...]

        @pl.when(at_end == 0)
        def _():
            wb_ref[cut:] = in_late[...]

        run(wb_ref)


def sort_kernel(rows, g_ref, keep_ref, got_ref, *outs):
    low, core = g_ref[4], g_ref[3]
    for n, out in enumerate(outs):
        block = 2 * (core ^ (n >> 1)) + (low ^ (n & 1))
        at = pl.ds(pl.multiple_of(block * rows, rows), rows)
        out[...] = (keep_ref[at, :] + got_ref[at, :].astype(F32)).astype(BF16)


def gather_kernel(g_ref, *refs):
    out_ref = refs[-1]
    low, high = g_ref[4], g_ref[5]
    width = refs[0].shape[1]
    for n in range(4):
        a, b = n >> 1, n & 1
        at = pl.ds(pl.multiple_of((2 * (low ^ b) + (high ^ a)) * width, width), width)
        out_ref[:, at] = (refs[2 * n][...].astype(F32) + refs[2 * n + 1][...].astype(F32)).astype(BF16)


def call(us, kernel, outs, args, scratch=()):
    return pl.pallas_call(
        kernel,
        out_shape=tuple(jax.ShapeDtypeStruct(s, d) for s, d in outs),
        in_specs=[SMEM] + [VMEM] * (len(args) - 1),
        out_specs=(VMEM,) * len(outs),
        scratch_shapes=[pltpu.VMEM(s, d) for s, d in scratch],
        compiler_params=params(),
        cost_estimate=pl.CostEstimate(flops=int(us * 1.15e9), bytes_accessed=int(us * 3.69e6), transcendentals=0),
    )(*args)


def fast_body(streams, short_taps, mix_taps, pole_rate, pole_angle, residue, skip, out_weight):
    rows, _, width = streams.shape
    modes = pole_rate.shape[0]
    ntap = mix_taps.shape[0]
    quarter = width // GROUP
    total = GROUP * rows
    ctx, tp = lax.axis_index("ctx"), lax.axis_index("tp")
    g, part = ctx % GROUP, ctx // GROUP
    core, y = tp % 2, tp // 2
    scal = jnp.stack([g, part, (y == part).astype(jnp.int32), core, g % 2, g // 2, (part == g // 2).astype(jnp.int32)]).astype(jnp.int32)

    cut = width * EARLY // 16
    size_m = rows + ntap
    back = np.concatenate([np.arange(ntap, size_m), np.arange(ntap, size_m)[::-1]])
    mats = [odd_dft(size_m, size_m), odd_idft(size_m, back), odd_dft(2 * rows, rows), odd_idft(2 * rows, np.arange(rows))]
    consts = np.concatenate([
        np.pad(half, ((0, 0), (0, 2 * rows - half.shape[1]))) for mat in mats for half in split_const(mat)], 0)

    short_taps = short_taps.transpose(1, 0, 2)
    anywhere = pl.BlockSpec(memory_space=pltpu.HBM)
    sent = pl.pallas_call(
        lambda *refs: prepare_kernel(rows, *refs),
        out_shape=tuple(jax.ShapeDtypeStruct((r, quarter), BF16) for r in (rows + 48,) * GROUP + (rows,) * GROUP),
        in_specs=[SMEM, anywhere, anywhere],
        out_specs=(VMEM,) * (2 * GROUP),
        scratch_shapes=[pltpu.VMEM((3, rows, width), BF16), pltpu.VMEM((3, 7, width), F32)]
        + [pltpu.VMEM((width // 128, rows + 8, 128), F32)] * 2
        + [pltpu.VMEM((rows, width), BF16), pltpu.SemaphoreType.DMA((width // 128 + 1,))],
        compiler_params=params(),
        cost_estimate=pl.CostEstimate(flops=int(2e9), bytes_accessed=int(6e6), transcendentals=0),
    )(scal, streams.transpose(1, 0, 2), short_taps)
    msgs, qs = sent[:GROUP], sent[GROUP:]
    early = swap(out_weight[:cut], BITS_FAR)
    msgs = [msgs[0]] + [swap(msgs[m], SLOT_BITS[m]) for m in (1, 2, 3)]
    spec, lspec, qre, qim, par, taps = call(
        0.3,
        lambda *refs: filters_kernel(rows, modes, *refs),
        [(s, F32) for s in ((size_m, quarter), (2 * rows, quarter), (modes, rows, quarter), (modes, rows, quarter),
                            (4, modes, quarter), (3, 7, quarter))],
        (scal, mix_taps, pole_rate, pole_angle, residue, skip[None], short_taps, consts),
    )
    spec, qs = lax.optimization_barrier((spec, qs))
    qs = [qs[0]] + [swap(qs[m], SLOT_BITS[m]) for m in (1, 2, 3)]
    med, st, out, rim, gate, ends = call(
        0.6,
        lambda *refs: medium_kernel(rows, modes, *refs),
        [((GROUP, rows, quarter), F32), ((GROUP, 2, modes, quarter), F32), ((2 * modes + 8, quarter), F32),
         ((160, quarter), BF16), ((rows, quarter), BF16), ((32, quarter), F32)],
        (scal, taps, spec, qre, qim, par, consts, *msgs),
        [((total + 128, quarter), BF16), ((GROUP, rows, quarter), F32), ((GROUP, modes, quarter), F32), ((GROUP, modes, quarter), F32),
         ((GROUP, 32, quarter), F32)],
    )
    out, rim, early = lax.optimization_barrier((out, rim, early))
    state_in, rim_in = swap(out, BIT_PART), swap(rim, BIT_PART)
    later, query = call(
        3.1,
        lambda *refs: intra_kernel(rows, *refs),
        [((GROUP - 1, rows, quarter), F32), ((total, quarter), F32)],
        (scal, taps, med, lspec, consts, *qs),
        [((quarter // 128, total + 8, 128), F32)],
    )
    late, later = lax.optimization_barrier((out_weight[cut:], later))
    out_late = far_swap(late, True)
    (hidden,) = call(
        5.2,
        lambda *refs: hidden_kernel(rows, modes, *refs),
        [((total, quarter), BF16)],
        (scal, taps, state_in, rim_in, gate, ends, spec, lspec, st, par, qre, qim, later, query, consts),
        [((GROUP, modes, 2, 8, quarter), F32), ((rows + 128, quarter), BF16), ((1, rows, quarter), F32),
         ((1, modes, quarter), F32), ((1, modes, quarter), F32), ((1, rows, quarter), F32)],
    )
    hidden, late = lax.optimization_barrier((hidden, out_weight[cut:]))
    in_late = far_swap(late, False)
    hid = [hidden] + [swap(hidden, SLOT_BITS[m]) for m in (1, 2)]
    hid[1], hid[2], out_late = lax.optimization_barrier((hid[1], hid[2], out_late))
    hid += [swap(hid[2][:total // 2], SLOT_BITS[1]), swap(hid[1][total // 2:], SLOT_BITS[2])]
    half = out_weight.shape[1] // 2
    blocks = {}
    for c in (1, 0):
        keep, send = call(
            1.2,
            lambda *refs: project_kernel(c, *refs),
            [((total, half), F32), ((total, half), BF16)],
            (scal, *hid, out_weight, early, out_late, in_late),
            [((width, 2 * half), BF16)],
        )
        send, hid = lax.optimization_barrier((send, hid))
        parts = call(
            0.4,
            lambda *refs: sort_kernel(rows, *refs),
            [((rows, half), BF16)] * GROUP,
            (scal, keep, swap(send, BIT_CORE)),
        )
        for n, part in enumerate(parts):
            blocks[n, c] = lax.ppermute(part, AXES, homeward(n >> 1, n & 1, c))
    blocks = [blocks[n, c] for n in range(GROUP) for c in (0, 1)]
    (mixed,) = call(1.3, gather_kernel, [((rows, 4 * half), BF16)], (scal, *blocks))
    return mixed


def from_behind(block, axis, distance):
    devices = range(lax.axis_size(axis))
    route = [(i - distance, i) for i in devices if i - distance in devices]
    return lax.ppermute(block, axis, route)


def depthwise(ext, taps):
    width = taps.shape[1]
    kernel = taps[::-1][:, None, :]
    out = lax.conv_general_dilated(
        ext[None],
        kernel,
        (1,),
        "VALID",
        dimension_numbers=("NWC", "WIO", "NWC"),
        feature_group_count=width,
        precision=lax.Precision.HIGHEST,
    )
    return out[0]


def general_body(streams, short_taps, mix_taps, pole_rate, pole_angle, residue, skip, out_weight):
    rows, three, width = streams.shape
    modes = pole_rate.shape[0]
    short = short_taps.reshape(7, three * width)
    rim = from_behind(streams[rows - 6 :], "ctx", 1)
    ext = jnp.concatenate([rim, streams], 0).astype(jnp.float32).reshape(rows + 6, three * width)
    conv = depthwise(ext, short).reshape(rows, three, width)
    gate = (conv[:, 1] * conv[:, 2]).astype(jnp.bfloat16)
    gate_rim = from_behind(gate[rows - 127 :], "ctx", 1)
    gate_ext = jnp.concatenate([gate_rim, gate], 0)
    query = conv[:, 0]
    medium = depthwise(gate_ext.astype(jnp.float32), mix_taps)
    amp = jnp.sqrt(1.0 - jnp.exp(-2.0 * pole_rate))
    res_re = residue[0] * amp
    res_im = residue[1] * amp
    steps = jnp.arange(rows).astype(jnp.float32)[:, None]
    flipped = medium[::-1]

    def first_pass(mode, carry):
        filt, end_re, end_im = carry
        rate = pole_rate[mode][None]
        angle = pole_angle[mode][None]
        mag = jnp.exp(-rate * steps)
        cosk = mag * jnp.cos(angle * steps)
        sink = mag * jnp.sin(angle * steps)
        filt = filt + res_re[mode][None] * cosk - res_im[mode][None] * sink
        end_re = end_re.at[mode].set(jnp.sum(flipped * cosk, 0))
        end_im = end_im.at[mode].set(jnp.sum(flipped * sink, 0))
        return (filt, end_re, end_im)

    zero_state = jnp.zeros((modes, width), jnp.float32)
    filt, end_re, end_im = lax.fori_loop(
        0, modes, first_pass, (jnp.zeros((rows, width), jnp.float32), zero_state, zero_state)
    )
    dec_mag = jnp.exp(-pole_rate * rows)
    dec_re = dec_mag * jnp.cos(pole_angle * rows)
    dec_im = dec_mag * jnp.sin(pole_angle * rows)

    def relay_step(turn, received):
        in_re, in_im = received
        out_re = dec_re * in_re - dec_im * in_im + end_re
        out_im = dec_re * in_im + dec_im * in_re + end_im
        return from_behind((out_re, out_im), "ctx", 1)

    st_re, st_im = lax.fori_loop(0, lax.axis_size("ctx") - 1, relay_step, (zero_state, zero_state))
    later = steps + 1.0

    def second_pass(mode, inflow):
        rate = pole_rate[mode][None]
        angle = pole_angle[mode][None]
        mag = jnp.exp(-rate * later)
        cos1 = mag * jnp.cos(angle * later)
        sin1 = mag * jnp.sin(angle * later)
        are = res_re[mode] * st_re[mode] - res_im[mode] * st_im[mode]
        aim = res_re[mode] * st_im[mode] + res_im[mode] * st_re[mode]
        return inflow + are[None] * cos1 - aim[None] * sin1

    inflow = lax.fori_loop(0, modes, second_pass, jnp.zeros((rows, width), jnp.float32))
    padded = jnp.concatenate([jnp.zeros((rows - 1, width), jnp.float32), medium], 0)
    intra = depthwise(padded, filt)
    longf = intra + inflow + skip[None] * medium
    hidden = (query * longf).astype(jnp.bfloat16)
    partial_out = jnp.dot(
        hidden,
        lax.all_gather(out_weight, "ctx", axis=1, tiled=True),
        preferred_element_type=jnp.float32,
    )
    return lax.psum_scatter(partial_out, "tp", scatter_dimension=1, tiled=True).astype(jnp.bfloat16)


def solution(mesh):
    fast = dict(mesh.shape) == {"ctx": 8, "tp": 4}
    return jax.shard_map(
        fast_body if fast else general_body,
        mesh=mesh,
        in_specs=(
            P("ctx", None, "tp"),
            P(None, None, "tp"),
            P(None, "tp"),
            P(None, "tp"),
            P(None, "tp"),
            P(None, None, "tp"),
            P("tp"),
            P("tp", "ctx"),
        ),
        out_specs=P("ctx", "tp"),
        check_vma=False,
    )
```

```python
import jax
import jax.numpy as jnp
import ml_dtypes
import numpy as np
from jax import lax
from jax.experimental import pallas as pl
from jax.experimental.pallas import tpu as pltpu
from jax.sharding import PartitionSpec as P

F32 = jnp.float32
BF16 = jnp.bfloat16
AXES = ("ctx", "tp")
GROUP = 4
BIT_CORE, BIT_PART, BITS_FAR = 1, 16, 24
EARLY = 9
SLOT_BITS = (0, 4, 8, 12)
VMEM = pl.BlockSpec(memory_space=pltpu.VMEM)
SMEM = pl.BlockSpec(memory_space=pltpu.SMEM)


def swap(block, bits):
    return lax.ppermute(block, AXES, [(i, i ^ bits) for i in range(32)])


def homeward(a, b, c):
    route = []
    for i in range(32):
        high, low, y, core = i >> 3 & 1, i >> 2 & 1, i >> 1 & 1, i & 1
        part, row = i >> 4, y ^ c
        route.append((i, part * 16 + (core ^ a) * 8 + (low ^ b) * 4 + row * 2 + (high ^ part ^ row)))
    return route


def outer(i):
    return (i >> 4) == (i >> 3 & 1)


def far_swap(block, ends):
    return lax.ppermute(block, AXES, [(i, i ^ BITS_FAR) for i in range(32) if outer(i) == ends])


def split_const(mat):
    hi = mat.astype(ml_dtypes.bfloat16)
    lo = (mat - hi.astype(np.float64)).astype(ml_dtypes.bfloat16)
    return hi, lo


def odd_dft(size, rows_in):
    freq = 2 * np.pi * (np.arange(size // 2) + 0.5) / size
    ang = freq[:, None] * np.arange(rows_in)
    return np.concatenate([np.cos(ang), -np.sin(ang)], 0)


def odd_idft(size, rows_out):
    freq = 2 * np.pi * (np.arange(size // 2) + 0.5) / size
    ang = np.asarray(rows_out)[:, None] * freq
    return np.concatenate([np.cos(ang), -np.sin(ang)], 1) * (2.0 / size)


def mm(a, b):
    return jnp.dot(a, b, preferred_element_type=F32)


def split(x):
    hi = x.astype(BF16)
    return hi, (x - hi.astype(F32)).astype(BF16)


def mm3(hi, lo, x):
    xh, xl = split(x)
    return mm(hi, xh) + mm(lo, xh) + mm(hi, xl)


def cmul(spec, filt):
    half = spec.shape[0] // 2
    a, b, c, d = spec[:half], spec[half:], filt[:half], filt[half:]
    return jnp.concatenate([a * c - b * d, a * d + b * c], 0)


class View:
    def __init__(self, ref, top, high, wide):
        self.ref, self.top, self.high, self.wide = ref, top, high, wide

    def __getitem__(self, key):
        wide = self.wide if key is Ellipsis else key[1].stop
        return self.ref[self.top:self.top + self.high, :wide]


def views(consts, rows, size):
    out, top = [], 0
    for high, wide in ((size, size), (2 * rows, size), (2 * rows, rows), (rows, 2 * rows)):
        for _ in range(2):
            out.append(View(consts, top, high, wide))
            top += high
    return out


def params(**kw):
    return pltpu.CompilerParams(vmem_limit_bytes=16 * 1024 * 1024, **kw)


def filters_kernel(rows, modes, g_ref, taps_ref, rate_all, angle_all, res_all, skip_all, short_all, consts,
                   spec_ref, lspec_ref, qre_ref, qim_ref, par_ref, short_ref):
    width = spec_ref.shape[1]
    ntap = taps_ref.shape[0]
    cmh, cml, _, _, clh, cll, _, _ = views(consts, rows, spec_ref.shape[0])
    at = pl.ds(pl.multiple_of(g_ref[0] * width, width), width)
    spec_ref[...] = mm3(cmh[:, :ntap], cml[:, :ntap], taps_ref[:, at])
    short_ref[...] = short_all[:, :, at]
    rate_ref, angle_ref, res_ref, skip_ref = rate_all[:, at], angle_all[:, at], res_all[:, :, at], skip_all[:, at]
    rate, angle = rate_ref[...], angle_ref[...]
    amp = jnp.sqrt(1.0 - jnp.exp(-2.0 * rate))
    rre, rim = res_ref[0] * amp, res_ref[1] * amp

    def power(n):
        mag = jnp.exp(-rate * n)
        return mag * jnp.cos(angle * n), mag * jnp.sin(angle * n)

    p1, p8, pend = power(1.0), power(8.0), power(float(rows))
    par_ref[0], par_ref[1] = rre * p1[0] - rim * p1[1], rre * p1[1] + rim * p1[0]
    par_ref[2], par_ref[3] = pend
    steps = lax.broadcasted_iota(jnp.int32, (8, width), 0).astype(F32)
    filt = [jnp.zeros((8, width), F32) for _ in range(rows // 8)]
    for m in range(modes):
        ang = angle[m:m + 1] * steps
        mag = jnp.exp(-rate[m:m + 1] * steps)
        cre, cim = mag * jnp.cos(ang), mag * jnp.sin(ang)
        sre, sim = p8[0][m:m + 1], p8[1][m:m + 1]
        wre, wim = rre[m:m + 1], rim[m:m + 1]
        for j in range(rows // 8):
            qre_ref[m, j * 8:j * 8 + 8] = cre
            qim_ref[m, j * 8:j * 8 + 8] = cim
            filt[j] = filt[j] + wre * cre - wim * cim
            cre, cim = cre * sre - cim * sim, cre * sim + cim * sre
    first = lax.broadcasted_iota(jnp.int32, (8, width), 0) == 0
    filt[0] = filt[0] + jnp.where(first, skip_ref[...], 0.0)
    lspec_ref[...] = mm3(clh[...], cll[...], jnp.concatenate(filt, 0))


def prepare_kernel(rows, g_ref, x_hbm, t_hbm, o0, o1, o2, o3, p0, p1, p2, p3, x_ref, t_ref, kx, vx, gate, sems):
    outs, queries = (o0, o1, o2, o3), (p0, p1, p2, p3)
    g = g_ref[0]
    quarter = o0.shape[1]
    tiles = x_ref.shape[2] // 128
    short = pltpu.make_async_copy(t_hbm, t_ref, sems.at[tiles])
    short.start()
    loads = []
    for lt in range(tiles):
        ls = slice(lt * 128, lt * 128 + 128)
        loads.append(pltpu.make_async_copy(x_hbm.at[:, :, ls], x_ref.at[:, :, ls], sems.at[lt]))
        loads[-1].start()
    short.wait()
    for lt in range(tiles):
        ls = slice(lt * 128, lt * 128 + 128)
        loads[lt].wait()
        for src, ext in ((1, kx), (2, vx)):
            ext[lt, :8] = jnp.zeros((8, 128), F32)
            ext[lt, 8:] = x_ref[src, :, ls].astype(F32)
        tk = [jnp.broadcast_to(t_ref[1, j:j + 1, ls], (8, 128)) for j in range(7)]
        tv = [jnp.broadcast_to(t_ref[2, j:j + 1, ls], (8, 128)) for j in range(7)]
        for r in range(0, rows, 16):
            both = []
            for h in (0, 8):
                sk, sv = tk[0] * kx[lt, 8 + r + h:16 + r + h], tv[0] * vx[lt, 8 + r + h:16 + r + h]
                for j in range(1, 7):
                    o = 8 + r + h - j
                    sk, sv = sk + tk[j] * kx[lt, o:o + 8], sv + tv[j] * vx[lt, o:o + 8]
                both.append(sk * sv)
            gate[r:r + 16, ls] = jnp.concatenate(both, 0).astype(BF16)
    for m, (out, query) in enumerate(zip(outs, queries)):
        at = pl.ds(pl.multiple_of((g ^ m) * quarter, quarter), quarter)
        out[:rows] = gate[:, at]
        for i in (1, 2):
            ends = [x_ref[i, :16, at].astype(F32)[:8], x_ref[i, rows - 16:, at].astype(F32)[8:]]
            row = rows + 16 * (i - 1)
            out[row:row + 16] = jnp.concatenate(ends, 0).astype(BF16)
        out[rows + 32:rows + 48] = x_ref[0, rows - 16:, at]
        query[...] = x_ref[0, :, at]


def first_gates(before, ends, taps):
    out = []
    for i in (0, 1):
        ext = jnp.concatenate([before[16 * i + 8:16 * i + 16], ends[16 * i:16 * i + 8]], 0)
        t = taps[1 + i]
        acc = t[0:1] * ext[8:16]
        for j in range(1, 7):
            acc = acc + t[j:j + 1] * ext[8 - j:16 - j]
        out.append(acc)
    return out[0] * out[1]


def tail_part(tail, taps):
    ext = jnp.concatenate([tail, jnp.zeros_like(tail)], 0)
    out = taps[1:2] * ext[7:15]
    for lag in range(2, 7):
        out = out + taps[lag:lag + 1] * ext[8 - lag:16 - lag]
    return out


def end_states(rows, modes, per, flip, blocks, qre_ref, qim_ref, er, ei, width):
    for lt in range(width // 128):
        ls = slice(lt * 128, lt * 128 + 128)
        for m0 in range(0, modes, per):
            def step(j, acc):
                at = pl.ds(pl.multiple_of(j * 8, 8), 8)
                x = [flip[b, at, ls] for b in blocks]
                out = []
                for i in range(per):
                    qr, qi = qre_ref[m0 + i, at, ls], qim_ref[m0 + i, at, ls]
                    for b in range(len(blocks)):
                        k = (i * len(blocks) + b) * 2
                        out += [acc[k] + x[b] * qr, acc[k + 1] + x[b] * qi]
                return tuple(out)
            acc = lax.fori_loop(0, rows // 8, step, (jnp.zeros((8, 128), F32),) * (2 * len(blocks) * per), unroll=10 if len(blocks) > 1 else 20)
            for i in range(per):
                for b in range(len(blocks)):
                    k = (i * len(blocks) + b) * 2
                    er[b, m0 + i:m0 + i + 1, ls] = jnp.sum(acc[k], 0, keepdims=True)
                    ei[b, m0 + i:m0 + i + 1, ls] = jnp.sum(acc[k + 1], 0, keepdims=True)


def medium_of(gates, spec, cmh, cml, imh, iml):
    return mm3(imh[...], iml[...], cmul(mm(cmh[...], gates) + mm(cml[...], gates), spec))


def medium_kernel(rows, modes, g_ref, t_ref, spec_ref, qre_ref, qim_ref, par_ref,
                  consts, q0, q1, q2, q3,
                  med_ref, st_ref, out_ref, rim_ref, gate_ref, ends_ref, gx, flip, er, ei, ends):
    g = g_ref[0]
    cmh, cml, imh, iml = views(consts, rows, spec_ref.shape[0])[:4]
    width = gate_ref.shape[1]
    gx[:128] = jnp.zeros_like(gx[:128])
    for m, msg in enumerate((q0, q1, q2, q3)):
        gx[pl.ds(pl.multiple_of(128 + (g ^ m) * rows, 16), rows), :] = msg[:rows]
        ends[g ^ m] = msg[rows:rows + 32].astype(F32)
    gate_ref[...] = gx[128:128 + rows]
    ends_ref[...] = ends[0]
    rim_ref[:128] = gx[GROUP * rows:]
    rim_ref[128:160] = ends[GROUP - 1].astype(BF16)
    for b in range(1, GROUP):
        top = 128 + b * rows
        head = first_gates(ends[b - 1], ends[b], t_ref)
        gx[top:top + 16] = jnp.concatenate([head, gx[top:top + 16].astype(F32)[8:]], 0).astype(BF16)
    ext = jnp.concatenate([gx[b * rows:b * rows + rows + 128] for b in range(GROUP)], 1)
    both = medium_of(ext, jnp.concatenate([spec_ref[...]] * GROUP, 1), cmh, cml, imh, iml)
    for b in range(GROUP):
        med_ref[b] = both[:rows, b * width:(b + 1) * width]
        flip[b] = both[rows:, b * width:(b + 1) * width]
    end_states(rows, modes, 4, flip, range(GROUP), qre_ref, qim_ref, er, ei, width)
    dre, dim = par_ref[2], par_ref[3]
    sre = jnp.zeros((modes, width), F32)
    sim = sre
    for b in range(GROUP):
        st_ref[b, 0], st_ref[b, 1] = er[b], ei[b]
        sre, sim = dre * sre - dim * sim + er[b], dre * sim + dim * sre + ei[b]
    out_ref[:modes] = sre
    out_ref[modes:2 * modes] = sim
    for m, q in enumerate((q0, q1, q2, q3)):
        @pl.when((g ^ m) == GROUP - 1)
        def _():
            out_ref[2 * modes:] = q[rows + 32:].astype(F32)[8:]


def intra_kernel(rows, g_ref, t_ref, med_ref, lspec_ref, consts, q0, q1, q2, q3, intra_ref, query_ref, qx):
    g = g_ref[0]
    _, _, _, _, clh, cll, ilh, ill = views(consts, rows, med_ref.shape[1] + 128)
    for b in range(1, GROUP):
        intra_ref[b - 1] = mm3(ilh[...], ill[...], cmul(mm3(clh[...], cll[...], med_ref[b]), lspec_ref[...]))
    total = GROUP * rows
    for lt in range(query_ref.shape[1] // 128):
        ls = slice(lt * 128, lt * 128 + 128)
        qx[lt, :8] = jnp.zeros((8, 128), F32)
        for m, q in enumerate((q0, q1, q2, q3)):
            qx[lt, pl.ds(pl.multiple_of((g ^ m) * rows + 8, 8), rows), :] = q[:, ls].astype(F32)
        t = [jnp.broadcast_to(t_ref[0, j:j + 1, ls], (8, 128)) for j in range(7)]
        for r in range(0, total, 8):
            acc = t[0] * qx[lt, 8 + r:16 + r]
            for j in range(1, 7):
                acc = acc + t[j] * qx[lt, 8 + r - j:16 + r - j]
            query_ref[r:r + 8, ls] = acc


def hidden_kernel(rows, modes, g_ref, t_ref, in_ref, rim_ref, gate_ref, ends_ref, spec_ref, lspec_ref, st_ref, par_ref,
                  qre_ref, qim_ref, later_ref, query_ref, consts,
                  hid_ref, amp, gx, flip, er, ei, intra):
    part = g_ref[1]
    live = (part > 0).astype(F32)
    width = query_ref.shape[1]
    cmh, cml, imh, iml, clh, cll, ilh, ill = views(consts, rows, gx.shape[0])
    gx[:128] = (rim_ref[:128].astype(F32) * live).astype(BF16)
    head = first_gates(rim_ref[128:160].astype(F32) * live, ends_ref[...], t_ref)
    gx[128:] = gate_ref[...]
    gx[128:144] = jnp.concatenate([head, gate_ref[:16].astype(F32)[8:]], 0).astype(BF16)
    both = medium_of(gx[...], spec_ref[...], cmh, cml, imh, iml)
    flip[0] = both[rows:]
    intra[0] = mm3(ilh[...], ill[...], cmul(mm3(clh[...], cll[...], both[:rows]), lspec_ref[...]))
    end_states(rows, modes, 8, flip, range(1), qre_ref, qim_ref, er, ei, width)
    sre, sim = in_ref[:modes] * live, in_ref[modes:2 * modes] * live
    rre, rim, dre, dim = par_ref[0], par_ref[1], par_ref[2], par_ref[3]
    for b in range(GROUP):
        are, aim = rre * sre - rim * sim, rre * sim + rim * sre
        for m in range(modes):
            amp[b, m, 0] = jnp.broadcast_to(are[m:m + 1], (8, width))
            amp[b, m, 1] = jnp.broadcast_to(aim[m:m + 1], (8, width))
        ere, eim = (er[0], ei[0]) if b == 0 else (st_ref[b, 0], st_ref[b, 1])
        sre, sim = dre * sre - dim * sim + ere, dre * sim + dim * sre + eim
    query_ref[:8] = query_ref[:8] + tail_part(in_ref[2 * modes:] * live, t_ref[0])
    for lt in range(width // 128):
        ls = slice(lt * 128, lt * 128 + 128)

        def step(j, carry):
            at = [pl.ds(pl.multiple_of(j * 16 + 8 * i, 8), 8) for i in range(2)]
            acc = [[intra[0, at[i], ls] for i in range(2)]]
            acc += [[later_ref[b, at[i], ls] for i in range(2)] for b in range(GROUP - 1)]
            for m in range(modes):
                qr = [qre_ref[m, at[i], ls] for i in range(2)]
                qi = [qim_ref[m, at[i], ls] for i in range(2)]
                for b in range(GROUP):
                    ar, ai = amp[b, m, 0, :, ls], amp[b, m, 1, :, ls]
                    for i in range(2):
                        acc[b][i] = acc[b][i] + ar * qr[i] - ai * qi[i]
            for b in range(GROUP):
                row = pl.multiple_of(b * rows + j * 16, 16)
                long = jnp.concatenate(acc[b], 0)
                hid_ref[pl.ds(row, 16), ls] = (query_ref[pl.ds(row, 16), ls] * long).astype(BF16)
            return carry

        lax.fori_loop(0, rows // 16, step, 0)


def halves(core, wide):
    half = wide // 2
    return [pl.ds(pl.multiple_of(k * half, half), half) for k in (core, 1 - core)]


def project_kernel(g_ref, h0, h1, h2, wa_ref, early, out_late, in_late, acc_ref, wb_ref):
    g, same, core, at_end, cut = g_ref[0], g_ref[2], g_ref[3], g_ref[6], early.shape[0]
    quarter = h0.shape[1]
    wb_ref[:cut] = early[...]

    @pl.when(at_end > 0)
    def _():
        wb_ref[cut:] = out_late[...]

    @pl.when(at_end == 0)
    def _():
        wb_ref[cut:] = in_late[...]

    at = [pl.ds(pl.multiple_of((g ^ m) * quarter, quarter), quarter) for m in range(GROUP - 1)]
    x = jnp.concatenate([h0[...], h1[...], h2[...]], 1)
    for weight, c in ((wa_ref, 1 - same), (wb_ref, same)):
        for k, cols in enumerate(halves(core, wa_ref.shape[1])):
            acc_ref[c, k] = mm(x, jnp.concatenate([weight[a, cols] for a in at], 0))


def finish_kernel(c, g_ref, acc_ref, top, low, wa_ref, wb_ref, keep_ref, send_ref):
    own, quarter = g_ref[2] != c, top.shape[1]
    at = pl.ds(pl.multiple_of((g_ref[0] ^ (GROUP - 1)) * quarter, quarter), quarter)
    x = jnp.concatenate([top[...], low[...]], 0)
    mine, other = [mm(x, jnp.where(own, wa_ref[at, cols], wb_ref[at, cols])) for cols in halves(g_ref[3], wa_ref.shape[1])]
    send_ref[...] = (acc_ref[c, 1] + other).astype(BF16)
    keep_ref[...] = acc_ref[c, 0] + mine


def sort_kernel(rows, g_ref, keep_ref, got_ref, *outs):
    low, core = g_ref[4], g_ref[3]
    for n, out in enumerate(outs):
        block = 2 * (core ^ (n >> 1)) + (low ^ (n & 1))
        at = pl.ds(pl.multiple_of(block * rows, rows), rows)
        out[...] = (keep_ref[at, :] + got_ref[at, :].astype(F32)).astype(BF16)


def gather_kernel(g_ref, *refs):
    out_ref = refs[-1]
    low, high = g_ref[4], g_ref[5]
    width = refs[0].shape[1]
    for n in range(4):
        a, b = n >> 1, n & 1
        at = pl.ds(pl.multiple_of((2 * (low ^ b) + (high ^ a)) * width, width), width)
        out_ref[:, at] = (refs[2 * n][...].astype(F32) + refs[2 * n + 1][...].astype(F32)).astype(BF16)


def call(us, kernel, outs, args, scratch=()):
    return pl.pallas_call(
        kernel,
        out_shape=tuple(jax.ShapeDtypeStruct(s, d) for s, d in outs),
        in_specs=[SMEM] + [VMEM] * (len(args) - 1),
        out_specs=(VMEM,) * len(outs),
        scratch_shapes=[pltpu.VMEM(s, d) for s, d in scratch],
        compiler_params=params(),
        cost_estimate=pl.CostEstimate(flops=int(us * 1.15e9), bytes_accessed=int(us * 3.69e6), transcendentals=0),
    )(*args)


def fast_body(streams, short_taps, mix_taps, pole_rate, pole_angle, residue, skip, out_weight):
    rows, _, width = streams.shape
    modes = pole_rate.shape[0]
    ntap = mix_taps.shape[0]
    quarter = width // GROUP
    total = GROUP * rows
    ctx, tp = lax.axis_index("ctx"), lax.axis_index("tp")
    g, part = ctx % GROUP, ctx // GROUP
    core, y = tp % 2, tp // 2
    scal = jnp.stack([g, part, (y == part).astype(jnp.int32), core, g % 2, g // 2, (part == g // 2).astype(jnp.int32)]).astype(jnp.int32)

    cut = width * EARLY // 16
    size_m = rows + ntap
    back = np.concatenate([np.arange(ntap, size_m), np.arange(ntap, size_m)[::-1]])
    mats = [odd_dft(size_m, size_m), odd_idft(size_m, back), odd_dft(2 * rows, rows), odd_idft(2 * rows, np.arange(rows))]
    consts = np.concatenate([
        np.pad(half, ((0, 0), (0, 2 * rows - half.shape[1]))) for mat in mats for half in split_const(mat)], 0)

    short_taps = short_taps.transpose(1, 0, 2)
    anywhere = pl.BlockSpec(memory_space=pltpu.HBM)
    sent = pl.pallas_call(
        lambda *refs: prepare_kernel(rows, *refs),
        out_shape=tuple(jax.ShapeDtypeStruct((r, quarter), BF16) for r in (rows + 48,) * GROUP + (rows,) * GROUP),
        in_specs=[SMEM, anywhere, anywhere],
        out_specs=(VMEM,) * (2 * GROUP),
        scratch_shapes=[pltpu.VMEM((3, rows, width), BF16), pltpu.VMEM((3, 7, width), F32)]
        + [pltpu.VMEM((width // 128, rows + 8, 128), F32)] * 2
        + [pltpu.VMEM((rows, width), BF16), pltpu.SemaphoreType.DMA((width // 128 + 1,))],
        compiler_params=params(),
        cost_estimate=pl.CostEstimate(flops=int(2e9), bytes_accessed=int(6e6), transcendentals=0),
    )(scal, streams.transpose(1, 0, 2), short_taps)
    msgs, qs = sent[:GROUP], sent[GROUP:]
    early = swap(out_weight[:cut], BITS_FAR)
    msgs = [msgs[0]] + [swap(msgs[m], SLOT_BITS[m]) for m in (1, 2, 3)]
    spec, lspec, qre, qim, par, taps = call(
        0.3,
        lambda *refs: filters_kernel(rows, modes, *refs),
        [(s, F32) for s in ((size_m, quarter), (2 * rows, quarter), (modes, rows, quarter), (modes, rows, quarter),
                            (4, modes, quarter), (3, 7, quarter))],
        (scal, mix_taps, pole_rate, pole_angle, residue, skip[None], short_taps, consts),
    )
    spec, qs = lax.optimization_barrier((spec, qs))
    qs = [qs[0]] + [swap(qs[m], SLOT_BITS[m]) for m in (1, 2, 3)]
    med, st, out, rim, gate, ends = call(
        0.6,
        lambda *refs: medium_kernel(rows, modes, *refs),
        [((GROUP, rows, quarter), F32), ((GROUP, 2, modes, quarter), F32), ((2 * modes + 8, quarter), F32),
         ((160, quarter), BF16), ((rows, quarter), BF16), ((32, quarter), F32)],
        (scal, taps, spec, qre, qim, par, consts, *msgs),
        [((total + 128, quarter), BF16), ((GROUP, rows, quarter), F32), ((GROUP, modes, quarter), F32), ((GROUP, modes, quarter), F32),
         ((GROUP, 32, quarter), F32)],
    )
    out, rim, early = lax.optimization_barrier((out, rim, early))
    state_in, rim_in = swap(out, BIT_PART), swap(rim, BIT_PART)
    later, query = call(
        3.1,
        lambda *refs: intra_kernel(rows, *refs),
        [((GROUP - 1, rows, quarter), F32), ((total, quarter), F32)],
        (scal, taps, med, lspec, consts, *qs),
        [((quarter // 128, total + 8, 128), F32)],
    )
    late, later = lax.optimization_barrier((out_weight[cut:], later))
    out_late = far_swap(late, True)
    (hidden,) = call(
        5.2,
        lambda *refs: hidden_kernel(rows, modes, *refs),
        [((total, quarter), BF16)],
        (scal, taps, state_in, rim_in, gate, ends, spec, lspec, st, par, qre, qim, later, query, consts),
        [((GROUP, modes, 2, 8, quarter), F32), ((rows + 128, quarter), BF16), ((1, rows, quarter), F32),
         ((1, modes, quarter), F32), ((1, modes, quarter), F32), ((1, rows, quarter), F32)],
    )
    hidden, late = lax.optimization_barrier((hidden, out_weight[cut:]))
    in_late = far_swap(late, False)
    hid = [hidden] + [swap(hidden, SLOT_BITS[m]) for m in (1, 2)]
    hid[1], out_late = lax.optimization_barrier((hid[1], out_late))
    passed = swap(hid[1][rows:], SLOT_BITS[2])
    hid += [swap(hid[2][:rows], SLOT_BITS[1]), passed]
    half = out_weight.shape[1] // 2
    acc, far = call(
        2.0,
        project_kernel,
        [((2, 2, total, half), F32), ((width, 2 * half), BF16)],
        (scal, *hid[:3], out_weight, early, out_late, in_late),
    )
    blocks, last = {}, hid[3:]
    for c in (1, 0):
        keep, send = call(
            0.8,
            lambda *refs: finish_kernel(c, *refs),
            [((total, half), F32), ((total, half), BF16)],
            (scal, acc, *last, out_weight, far),
        )
        send, last = lax.optimization_barrier((send, last))
        parts = call(
            0.4,
            lambda *refs: sort_kernel(rows, *refs),
            [((rows, half), BF16)] * GROUP,
            (scal, keep, swap(send, BIT_CORE)),
        )
        for n, part in enumerate(parts):
            blocks[n, c] = lax.ppermute(part, AXES, homeward(n >> 1, n & 1, c))
    blocks = [blocks[n, c] for n in range(GROUP) for c in (0, 1)]
    (mixed,) = call(1.3, gather_kernel, [((rows, 4 * half), BF16)], (scal, *blocks))
    return mixed


def from_behind(block, axis, distance):
    devices = range(lax.axis_size(axis))
    route = [(i - distance, i) for i in devices if i - distance in devices]
    return lax.ppermute(block, axis, route)


def depthwise(ext, taps):
    width = taps.shape[1]
    kernel = taps[::-1][:, None, :]
    out = lax.conv_general_dilated(
        ext[None],
        kernel,
        (1,),
        "VALID",
        dimension_numbers=("NWC", "WIO", "NWC"),
        feature_group_count=width,
        precision=lax.Precision.HIGHEST,
    )
    return out[0]


def general_body(streams, short_taps, mix_taps, pole_rate, pole_angle, residue, skip, out_weight):
    rows, three, width = streams.shape
    modes = pole_rate.shape[0]
    short = short_taps.reshape(7, three * width)
    rim = from_behind(streams[rows - 6 :], "ctx", 1)
    ext = jnp.concatenate([rim, streams], 0).astype(jnp.float32).reshape(rows + 6, three * width)
    conv = depthwise(ext, short).reshape(rows, three, width)
    gate = (conv[:, 1] * conv[:, 2]).astype(jnp.bfloat16)
    gate_rim = from_behind(gate[rows - 127 :], "ctx", 1)
    gate_ext = jnp.concatenate([gate_rim, gate], 0)
    query = conv[:, 0]
    medium = depthwise(gate_ext.astype(jnp.float32), mix_taps)
    amp = jnp.sqrt(1.0 - jnp.exp(-2.0 * pole_rate))
    res_re = residue[0] * amp
    res_im = residue[1] * amp
    steps = jnp.arange(rows).astype(jnp.float32)[:, None]
    flipped = medium[::-1]

    def first_pass(mode, carry):
        filt, end_re, end_im = carry
        rate = pole_rate[mode][None]
        angle = pole_angle[mode][None]
        mag = jnp.exp(-rate * steps)
        cosk = mag * jnp.cos(angle * steps)
        sink = mag * jnp.sin(angle * steps)
        filt = filt + res_re[mode][None] * cosk - res_im[mode][None] * sink
        end_re = end_re.at[mode].set(jnp.sum(flipped * cosk, 0))
        end_im = end_im.at[mode].set(jnp.sum(flipped * sink, 0))
        return (filt, end_re, end_im)

    zero_state = jnp.zeros((modes, width), jnp.float32)
    filt, end_re, end_im = lax.fori_loop(
        0, modes, first_pass, (jnp.zeros((rows, width), jnp.float32), zero_state, zero_state)
    )
    dec_mag = jnp.exp(-pole_rate * rows)
    dec_re = dec_mag * jnp.cos(pole_angle * rows)
    dec_im = dec_mag * jnp.sin(pole_angle * rows)

    def relay_step(turn, received):
        in_re, in_im = received
        out_re = dec_re * in_re - dec_im * in_im + end_re
        out_im = dec_re * in_im + dec_im * in_re + end_im
        return from_behind((out_re, out_im), "ctx", 1)

    st_re, st_im = lax.fori_loop(0, lax.axis_size("ctx") - 1, relay_step, (zero_state, zero_state))
    later = steps + 1.0

    def second_pass(mode, inflow):
        rate = pole_rate[mode][None]
        angle = pole_angle[mode][None]
        mag = jnp.exp(-rate * later)
        cos1 = mag * jnp.cos(angle * later)
        sin1 = mag * jnp.sin(angle * later)
        are = res_re[mode] * st_re[mode] - res_im[mode] * st_im[mode]
        aim = res_re[mode] * st_im[mode] + res_im[mode] * st_re[mode]
        return inflow + are[None] * cos1 - aim[None] * sin1

    inflow = lax.fori_loop(0, modes, second_pass, jnp.zeros((rows, width), jnp.float32))
    padded = jnp.concatenate([jnp.zeros((rows - 1, width), jnp.float32), medium], 0)
    intra = depthwise(padded, filt)
    longf = intra + inflow + skip[None] * medium
    hidden = (query * longf).astype(jnp.bfloat16)
    partial_out = jnp.dot(
        hidden,
        lax.all_gather(out_weight, "ctx", axis=1, tiled=True),
        preferred_element_type=jnp.float32,
    )
    return lax.psum_scatter(partial_out, "tp", scatter_dimension=1, tiled=True).astype(jnp.bfloat16)


def solution(mesh):
    fast = dict(mesh.shape) == {"ctx": 8, "tp": 4}
    return jax.shard_map(
        fast_body if fast else general_body,
        mesh=mesh,
        in_specs=(
            P("ctx", None, "tp"),
            P(None, None, "tp"),
            P(None, "tp"),
            P(None, "tp"),
            P(None, "tp"),
            P(None, None, "tp"),
            P("tp"),
            P("tp", "ctx"),
        ),
        out_specs=P("ctx", "tp"),
        check_vma=False,
    )
```

```python
import jax
import jax.numpy as jnp
import ml_dtypes
import numpy as np
from jax import lax
from jax.experimental import pallas as pl
from jax.experimental.pallas import tpu as pltpu
from jax.sharding import PartitionSpec as P

F32 = jnp.float32
BF16 = jnp.bfloat16
AXES = ("ctx", "tp")
GROUP = 4
BIT_CORE, BIT_PART, BITS_FAR = 1, 16, 24
EARLY = 9
SLOT_BITS = (0, 4, 8, 12)
VMEM = pl.BlockSpec(memory_space=pltpu.VMEM)
SMEM = pl.BlockSpec(memory_space=pltpu.SMEM)


def swap(block, bits):
    return lax.ppermute(block, AXES, [(i, i ^ bits) for i in range(32)])


def homeward(a, b, c):
    route = []
    for i in range(32):
        high, low, y, core = i >> 3 & 1, i >> 2 & 1, i >> 1 & 1, i & 1
        part, row = i >> 4, y ^ c
        route.append((i, part * 16 + (core ^ a) * 8 + (low ^ b) * 4 + row * 2 + (high ^ part ^ row)))
    return route


def outer(i):
    return (i >> 4) == (i >> 3 & 1)


def far_swap(block, ends):
    return lax.ppermute(block, AXES, [(i, i ^ BITS_FAR) for i in range(32) if outer(i) == ends])


def split_const(mat):
    hi = mat.astype(ml_dtypes.bfloat16)
    lo = (mat - hi.astype(np.float64)).astype(ml_dtypes.bfloat16)
    return hi, lo


def odd_dft(size, rows_in):
    freq = 2 * np.pi * (np.arange(size // 2) + 0.5) / size
    ang = freq[:, None] * np.arange(rows_in)
    return np.concatenate([np.cos(ang), -np.sin(ang)], 0)


def odd_idft(size, rows_out):
    freq = 2 * np.pi * (np.arange(size // 2) + 0.5) / size
    ang = np.asarray(rows_out)[:, None] * freq
    return np.concatenate([np.cos(ang), -np.sin(ang)], 1) * (2.0 / size)


def mm(a, b):
    return jnp.dot(a, b, preferred_element_type=F32)


def split(x):
    hi = x.astype(BF16)
    return hi, (x - hi.astype(F32)).astype(BF16)


def mm3(hi, lo, x):
    xh, xl = split(x)
    return mm(hi, xh) + mm(lo, xh) + mm(hi, xl)


def cmul(spec, filt):
    half = spec.shape[0] // 2
    a, b, c, d = spec[:half], spec[half:], filt[:half], filt[half:]
    return jnp.concatenate([a * c - b * d, a * d + b * c], 0)


class View:
    def __init__(self, ref, top, high, wide):
        self.ref, self.top, self.high, self.wide = ref, top, high, wide

    def __getitem__(self, key):
        wide = self.wide if key is Ellipsis else key[1].stop
        return self.ref[self.top:self.top + self.high, :wide]


def views(consts, rows, size):
    out, top = [], 0
    for high, wide in ((size, size), (2 * rows, size), (2 * rows, rows), (rows, 2 * rows)):
        for _ in range(2):
            out.append(View(consts, top, high, wide))
            top += high
    return out


def params(**kw):
    return pltpu.CompilerParams(vmem_limit_bytes=16 * 1024 * 1024, **kw)


def filters_kernel(rows, modes, g_ref, taps_ref, rate_all, angle_all, res_all, skip_all, short_all, consts,
                   spec_ref, lspec_ref, qre_ref, qim_ref, par_ref, short_ref):
    width = spec_ref.shape[1]
    ntap = taps_ref.shape[0]
    cmh, cml, _, _, clh, cll, _, _ = views(consts, rows, spec_ref.shape[0])
    at = pl.ds(pl.multiple_of(g_ref[0] * width, width), width)
    spec_ref[...] = mm3(cmh[:, :ntap], cml[:, :ntap], taps_ref[:, at])
    short_ref[...] = short_all[:, :, at]
    rate_ref, angle_ref, res_ref, skip_ref = rate_all[:, at], angle_all[:, at], res_all[:, :, at], skip_all[:, at]
    rate, angle = rate_ref[...], angle_ref[...]
    amp = jnp.sqrt(1.0 - jnp.exp(-2.0 * rate))
    rre, rim = res_ref[0] * amp, res_ref[1] * amp

    def power(n):
        mag = jnp.exp(-rate * n)
        return mag * jnp.cos(angle * n), mag * jnp.sin(angle * n)

    p1, p8, pend = power(1.0), power(8.0), power(float(rows))
    par_ref[0], par_ref[1] = rre * p1[0] - rim * p1[1], rre * p1[1] + rim * p1[0]
    par_ref[2], par_ref[3] = pend
    steps = lax.broadcasted_iota(jnp.int32, (8, width), 0).astype(F32)
    filt = [jnp.zeros((8, width), F32) for _ in range(rows // 8)]
    for m in range(modes):
        ang = angle[m:m + 1] * steps
        mag = jnp.exp(-rate[m:m + 1] * steps)
        cre, cim = mag * jnp.cos(ang), mag * jnp.sin(ang)
        sre, sim = p8[0][m:m + 1], p8[1][m:m + 1]
        wre, wim = rre[m:m + 1], rim[m:m + 1]
        for j in range(rows // 8):
            qre_ref[m, j * 8:j * 8 + 8] = cre
            qim_ref[m, j * 8:j * 8 + 8] = cim
            filt[j] = filt[j] + wre * cre - wim * cim
            cre, cim = cre * sre - cim * sim, cre * sim + cim * sre
    first = lax.broadcasted_iota(jnp.int32, (8, width), 0) == 0
    filt[0] = filt[0] + jnp.where(first, skip_ref[...], 0.0)
    lspec_ref[...] = mm3(clh[...], cll[...], jnp.concatenate(filt, 0))


def prepare_kernel(rows, g_ref, x_hbm, t_hbm, o0, o1, o2, o3, p0, p1, p2, p3, x_ref, t_ref, kx, vx, gate, sems):
    outs, queries = (o0, o1, o2, o3), (p0, p1, p2, p3)
    g = g_ref[0]
    quarter = o0.shape[1]
    tiles = x_ref.shape[2] // 128
    short = pltpu.make_async_copy(t_hbm, t_ref, sems.at[tiles])
    short.start()
    loads = []
    for lt in range(tiles):
        ls = slice(lt * 128, lt * 128 + 128)
        loads.append(pltpu.make_async_copy(x_hbm.at[:, :, ls], x_ref.at[:, :, ls], sems.at[lt]))
        loads[-1].start()
    short.wait()
    for lt in range(tiles):
        ls = slice(lt * 128, lt * 128 + 128)
        loads[lt].wait()
        for src, ext in ((1, kx), (2, vx)):
            ext[lt, :8] = jnp.zeros((8, 128), F32)
            ext[lt, 8:] = x_ref[src, :, ls].astype(F32)
        tk = [jnp.broadcast_to(t_ref[1, j:j + 1, ls], (8, 128)) for j in range(7)]
        tv = [jnp.broadcast_to(t_ref[2, j:j + 1, ls], (8, 128)) for j in range(7)]
        for r in range(0, rows, 16):
            both = []
            for h in (0, 8):
                sk, sv = tk[0] * kx[lt, 8 + r + h:16 + r + h], tv[0] * vx[lt, 8 + r + h:16 + r + h]
                for j in range(1, 7):
                    o = 8 + r + h - j
                    sk, sv = sk + tk[j] * kx[lt, o:o + 8], sv + tv[j] * vx[lt, o:o + 8]
                both.append(sk * sv)
            gate[r:r + 16, ls] = jnp.concatenate(both, 0).astype(BF16)
    for m, (out, query) in enumerate(zip(outs, queries)):
        at = pl.ds(pl.multiple_of((g ^ m) * quarter, quarter), quarter)
        out[:rows] = gate[:, at]
        for i in (1, 2):
            ends = [x_ref[i, :16, at].astype(F32)[:8], x_ref[i, rows - 16:, at].astype(F32)[8:]]
            row = rows + 16 * (i - 1)
            out[row:row + 16] = jnp.concatenate(ends, 0).astype(BF16)
        out[rows + 32:rows + 48] = x_ref[0, rows - 16:, at]
        query[...] = x_ref[0, :, at]


def first_gates(before, ends, taps):
    out = []
    for i in (0, 1):
        ext = jnp.concatenate([before[16 * i + 8:16 * i + 16], ends[16 * i:16 * i + 8]], 0)
        t = taps[1 + i]
        acc = t[0:1] * ext[8:16]
        for j in range(1, 7):
            acc = acc + t[j:j + 1] * ext[8 - j:16 - j]
        out.append(acc)
    return out[0] * out[1]


def tail_part(tail, taps):
    ext = jnp.concatenate([tail, jnp.zeros_like(tail)], 0)
    out = taps[1:2] * ext[7:15]
    for lag in range(2, 7):
        out = out + taps[lag:lag + 1] * ext[8 - lag:16 - lag]
    return out


def end_states(rows, modes, per, flip, blocks, qre_ref, qim_ref, er, ei, width):
    for lt in range(width // 128):
        ls = slice(lt * 128, lt * 128 + 128)
        for m0 in range(0, modes, per):
            def step(j, acc):
                at = pl.ds(pl.multiple_of(j * 8, 8), 8)
                x = [flip[b, at, ls] for b in blocks]
                out = []
                for i in range(per):
                    qr, qi = qre_ref[m0 + i, at, ls], qim_ref[m0 + i, at, ls]
                    for b in range(len(blocks)):
                        k = (i * len(blocks) + b) * 2
                        out += [acc[k] + x[b] * qr, acc[k + 1] + x[b] * qi]
                return tuple(out)
            acc = lax.fori_loop(0, rows // 8, step, (jnp.zeros((8, 128), F32),) * (2 * len(blocks) * per), unroll=10 if len(blocks) > 1 else 20)
            for i in range(per):
                for b in range(len(blocks)):
                    k = (i * len(blocks) + b) * 2
                    er[b, m0 + i:m0 + i + 1, ls] = jnp.sum(acc[k], 0, keepdims=True)
                    ei[b, m0 + i:m0 + i + 1, ls] = jnp.sum(acc[k + 1], 0, keepdims=True)


def medium_of(gates, spec, cmh, cml, imh, iml):
    return mm3(imh[...], iml[...], cmul(mm(cmh[...], gates) + mm(cml[...], gates), spec))


def medium_kernel(rows, modes, g_ref, t_ref, spec_ref, qre_ref, qim_ref, par_ref,
                  consts, q0, q1, q2, q3,
                  med_ref, st_ref, out_ref, rim_ref, gate_ref, ends_ref, gx, flip, er, ei, ends):
    g = g_ref[0]
    cmh, cml, imh, iml = views(consts, rows, spec_ref.shape[0])[:4]
    width = gate_ref.shape[1]
    gx[:128] = jnp.zeros_like(gx[:128])
    for m, msg in enumerate((q0, q1, q2, q3)):
        gx[pl.ds(pl.multiple_of(128 + (g ^ m) * rows, 16), rows), :] = msg[:rows]
        ends[g ^ m] = msg[rows:rows + 32].astype(F32)
    gate_ref[...] = gx[128:128 + rows]
    ends_ref[...] = ends[0]
    rim_ref[:128] = gx[GROUP * rows:]
    rim_ref[128:160] = ends[GROUP - 1].astype(BF16)
    for b in range(1, GROUP):
        top = 128 + b * rows
        head = first_gates(ends[b - 1], ends[b], t_ref)
        gx[top:top + 16] = jnp.concatenate([head, gx[top:top + 16].astype(F32)[8:]], 0).astype(BF16)
    ext = jnp.concatenate([gx[b * rows:b * rows + rows + 128] for b in range(GROUP)], 1)
    both = medium_of(ext, jnp.concatenate([spec_ref[...]] * GROUP, 1), cmh, cml, imh, iml)
    for b in range(GROUP):
        med_ref[b] = both[:rows, b * width:(b + 1) * width]
        flip[b] = both[rows:, b * width:(b + 1) * width]
    end_states(rows, modes, 4, flip, range(GROUP), qre_ref, qim_ref, er, ei, width)
    dre, dim = par_ref[2], par_ref[3]
    sre = jnp.zeros((modes, width), F32)
    sim = sre
    for b in range(GROUP):
        st_ref[b, 0], st_ref[b, 1] = er[b], ei[b]
        sre, sim = dre * sre - dim * sim + er[b], dre * sim + dim * sre + ei[b]
    out_ref[:modes] = sre
    out_ref[modes:2 * modes] = sim
    for m, q in enumerate((q0, q1, q2, q3)):
        @pl.when((g ^ m) == GROUP - 1)
        def _():
            out_ref[2 * modes:] = q[rows + 32:].astype(F32)[8:]


def intra_kernel(rows, g_ref, t_ref, med_ref, lspec_ref, consts, q0, q1, q2, q3, intra_ref, query_ref, qx):
    g = g_ref[0]
    _, _, _, _, clh, cll, ilh, ill = views(consts, rows, med_ref.shape[1] + 128)
    for b in range(1, GROUP):
        intra_ref[b - 1] = mm3(ilh[...], ill[...], cmul(mm3(clh[...], cll[...], med_ref[b]), lspec_ref[...]))
    total = GROUP * rows
    for lt in range(query_ref.shape[1] // 128):
        ls = slice(lt * 128, lt * 128 + 128)
        qx[lt, :8] = jnp.zeros((8, 128), F32)
        for m, q in enumerate((q0, q1, q2, q3)):
            qx[lt, pl.ds(pl.multiple_of((g ^ m) * rows + 8, 8), rows), :] = q[:, ls].astype(F32)
        t = [jnp.broadcast_to(t_ref[0, j:j + 1, ls], (8, 128)) for j in range(7)]
        for r in range(0, total, 8):
            acc = t[0] * qx[lt, 8 + r:16 + r]
            for j in range(1, 7):
                acc = acc + t[j] * qx[lt, 8 + r - j:16 + r - j]
            query_ref[r:r + 8, ls] = acc


def hidden_kernel(rows, modes, g_ref, t_ref, in_ref, rim_ref, gate_ref, ends_ref, spec_ref, lspec_ref, st_ref, par_ref,
                  qre_ref, qim_ref, later_ref, query_ref, consts,
                  hid_ref, amp, gx, flip, er, ei, intra):
    part = g_ref[1]
    live = (part > 0).astype(F32)
    width = query_ref.shape[1]
    cmh, cml, imh, iml, clh, cll, ilh, ill = views(consts, rows, gx.shape[0])
    gx[:128] = (rim_ref[:128].astype(F32) * live).astype(BF16)
    head = first_gates(rim_ref[128:160].astype(F32) * live, ends_ref[...], t_ref)
    gx[128:] = gate_ref[...]
    gx[128:144] = jnp.concatenate([head, gate_ref[:16].astype(F32)[8:]], 0).astype(BF16)
    both = medium_of(gx[...], spec_ref[...], cmh, cml, imh, iml)
    flip[0] = both[rows:]
    intra[0] = mm3(ilh[...], ill[...], cmul(mm3(clh[...], cll[...], both[:rows]), lspec_ref[...]))
    end_states(rows, modes, 8, flip, range(1), qre_ref, qim_ref, er, ei, width)
    sre, sim = in_ref[:modes] * live, in_ref[modes:2 * modes] * live
    rre, rim, dre, dim = par_ref[0], par_ref[1], par_ref[2], par_ref[3]
    for b in range(GROUP):
        are, aim = rre * sre - rim * sim, rre * sim + rim * sre
        for m in range(modes):
            amp[b, m, 0] = jnp.broadcast_to(are[m:m + 1], (8, width))
            amp[b, m, 1] = jnp.broadcast_to(aim[m:m + 1], (8, width))
        ere, eim = (er[0], ei[0]) if b == 0 else (st_ref[b, 0], st_ref[b, 1])
        sre, sim = dre * sre - dim * sim + ere, dre * sim + dim * sre + eim
    query_ref[:8] = query_ref[:8] + tail_part(in_ref[2 * modes:] * live, t_ref[0])
    for lt in range(width // 128):
        ls = slice(lt * 128, lt * 128 + 128)

        def step(j, carry):
            at = [pl.ds(pl.multiple_of(j * 16 + 8 * i, 8), 8) for i in range(2)]
            acc = [[intra[0, at[i], ls] for i in range(2)]]
            acc += [[later_ref[b, at[i], ls] for i in range(2)] for b in range(GROUP - 1)]
            for m in range(modes):
                qr = [qre_ref[m, at[i], ls] for i in range(2)]
                qi = [qim_ref[m, at[i], ls] for i in range(2)]
                for b in range(GROUP):
                    ar, ai = amp[b, m, 0, :, ls], amp[b, m, 1, :, ls]
                    for i in range(2):
                        acc[b][i] = acc[b][i] + ar * qr[i] - ai * qi[i]
            for b in range(GROUP):
                row = pl.multiple_of(b * rows + j * 16, 16)
                long = jnp.concatenate(acc[b], 0)
                hid_ref[pl.ds(row, 16), ls] = (query_ref[pl.ds(row, 16), ls] * long).astype(BF16)
            return carry

        lax.fori_loop(0, rows // 16, step, 0)


def halves(core, wide):
    half = wide // 2
    return [pl.ds(pl.multiple_of(k * half, half), half) for k in (core, 1 - core)]


def project_kernel(g_ref, h0, h1, h2, wa_ref, early, out_late, in_late, acc_ref, wb_ref):
    g, same, core, at_end, cut = g_ref[0], g_ref[2], g_ref[3], g_ref[6], early.shape[0]
    quarter = h0.shape[1]
    wb_ref[:cut] = early[...]

    @pl.when(at_end > 0)
    def _():
        wb_ref[cut:] = out_late[...]

    @pl.when(at_end == 0)
    def _():
        wb_ref[cut:] = in_late[...]

    at = [pl.ds(pl.multiple_of((g ^ m) * quarter, quarter), quarter) for m in range(GROUP - 1)]
    x = jnp.concatenate([h0[...], h1[...], h2[...]], 1)
    for weight, c in ((wa_ref, 1 - same), (wb_ref, same)):
        for k, cols in enumerate(halves(core, wa_ref.shape[1])):
            acc_ref[c, k] = mm(x, jnp.concatenate([weight[a, cols] for a in at], 0))


def finish_kernel(c, g_ref, acc_ref, top, low, wa_ref, wb_ref, keep_ref, send_ref):
    own, quarter = g_ref[2] != c, top.shape[1]
    at = pl.ds(pl.multiple_of((g_ref[0] ^ (GROUP - 1)) * quarter, quarter), quarter)
    x = jnp.concatenate([top[...], low[...]], 0)
    mine, other = [mm(x, jnp.where(own, wa_ref[at, cols], wb_ref[at, cols])) for cols in halves(g_ref[3], wa_ref.shape[1])]
    send_ref[...] = (acc_ref[c, 1] + other).astype(BF16)
    keep_ref[...] = acc_ref[c, 0] + mine


def sort_kernel(rows, g_ref, keep_ref, got_ref, *outs):
    low, core = g_ref[4], g_ref[3]
    for n, out in enumerate(outs):
        block = 2 * (core ^ (n >> 1)) + (low ^ (n & 1))
        at = pl.ds(pl.multiple_of(block * rows, rows), rows)
        out[...] = (keep_ref[at, :] + got_ref[at, :].astype(F32)).astype(BF16)


def gather_kernel(g_ref, *refs):
    out_ref = refs[-1]
    low, high = g_ref[4], g_ref[5]
    width = refs[0].shape[1]
    for n in range(4):
        a, b = n >> 1, n & 1
        at = pl.ds(pl.multiple_of((2 * (low ^ b) + (high ^ a)) * width, width), width)
        out_ref[:, at] = (refs[2 * n][...].astype(F32) + refs[2 * n + 1][...].astype(F32)).astype(BF16)


def call(us, kernel, outs, args, scratch=()):
    return pl.pallas_call(
        kernel,
        out_shape=tuple(jax.ShapeDtypeStruct(s, d) for s, d in outs),
        in_specs=[SMEM] + [VMEM] * (len(args) - 1),
        out_specs=(VMEM,) * len(outs),
        scratch_shapes=[pltpu.VMEM(s, d) for s, d in scratch],
        compiler_params=params(),
        cost_estimate=pl.CostEstimate(flops=int(us * 1.15e9), bytes_accessed=int(us * 3.69e6), transcendentals=0),
    )(*args)


def fast_body(streams, short_taps, mix_taps, pole_rate, pole_angle, residue, skip, out_weight):
    rows, _, width = streams.shape
    modes = pole_rate.shape[0]
    ntap = mix_taps.shape[0]
    quarter = width // GROUP
    total = GROUP * rows
    ctx, tp = lax.axis_index("ctx"), lax.axis_index("tp")
    g, part = ctx % GROUP, ctx // GROUP
    core, y = tp % 2, tp // 2
    scal = jnp.stack([g, part, (y == part).astype(jnp.int32), core, g % 2, g // 2, (part == g // 2).astype(jnp.int32)]).astype(jnp.int32)

    cut = width * EARLY // 16
    size_m = rows + ntap
    back = np.concatenate([np.arange(ntap, size_m), np.arange(ntap, size_m)[::-1]])
    mats = [odd_dft(size_m, size_m), odd_idft(size_m, back), odd_dft(2 * rows, rows), odd_idft(2 * rows, np.arange(rows))]
    consts = np.concatenate([
        np.pad(half, ((0, 0), (0, 2 * rows - half.shape[1]))) for mat in mats for half in split_const(mat)], 0)

    short_taps = short_taps.transpose(1, 0, 2)
    anywhere = pl.BlockSpec(memory_space=pltpu.HBM)
    sent = pl.pallas_call(
        lambda *refs: prepare_kernel(rows, *refs),
        out_shape=tuple(jax.ShapeDtypeStruct((r, quarter), BF16) for r in (rows + 48,) * GROUP + (rows,) * GROUP),
        in_specs=[SMEM, anywhere, anywhere],
        out_specs=(VMEM,) * (2 * GROUP),
        scratch_shapes=[pltpu.VMEM((3, rows, width), BF16), pltpu.VMEM((3, 7, width), F32)]
        + [pltpu.VMEM((width // 128, rows + 8, 128), F32)] * 2
        + [pltpu.VMEM((rows, width), BF16), pltpu.SemaphoreType.DMA((width // 128 + 1,))],
        compiler_params=params(),
        cost_estimate=pl.CostEstimate(flops=int(2e9), bytes_accessed=int(6e6), transcendentals=0),
    )(scal, streams.transpose(1, 0, 2), short_taps)
    msgs, qs = sent[:GROUP], sent[GROUP:]
    early = swap(out_weight[:cut], BITS_FAR)
    msgs = [msgs[0]] + [swap(msgs[m], SLOT_BITS[m]) for m in (1, 2, 3)]
    spec, lspec, qre, qim, par, taps = call(
        0.3,
        lambda *refs: filters_kernel(rows, modes, *refs),
        [(s, F32) for s in ((size_m, quarter), (2 * rows, quarter), (modes, rows, quarter), (modes, rows, quarter),
                            (4, modes, quarter), (3, 7, quarter))],
        (scal, mix_taps, pole_rate, pole_angle, residue, skip[None], short_taps, consts),
    )
    spec, qs = lax.optimization_barrier((spec, qs))
    qs = [qs[0]] + [swap(qs[m], SLOT_BITS[m]) for m in (1, 2, 3)]
    med, st, out, rim, gate, ends = call(
        0.6,
        lambda *refs: medium_kernel(rows, modes, *refs),
        [((GROUP, rows, quarter), F32), ((GROUP, 2, modes, quarter), F32), ((2 * modes + 8, quarter), F32),
         ((160, quarter), BF16), ((rows, quarter), BF16), ((32, quarter), F32)],
        (scal, taps, spec, qre, qim, par, consts, *msgs),
        [((total + 128, quarter), BF16), ((GROUP, rows, quarter), F32), ((GROUP, modes, quarter), F32), ((GROUP, modes, quarter), F32),
         ((GROUP, 32, quarter), F32)],
    )
    out, rim, early = lax.optimization_barrier((out, rim, early))
    state_in, rim_in = swap(out, BIT_PART), swap(rim, BIT_PART)
    later, query = call(
        3.1,
        lambda *refs: intra_kernel(rows, *refs),
        [((GROUP - 1, rows, quarter), F32), ((total, quarter), F32)],
        (scal, taps, med, lspec, consts, *qs),
        [((quarter // 128, total + 8, 128), F32)],
    )
    late, later = lax.optimization_barrier((out_weight[cut:], later))
    out_late = far_swap(late, True)
    late, later = lax.optimization_barrier((out_weight[cut:], later))
    in_late = far_swap(late, False)
    (hidden,) = call(
        5.2,
        lambda *refs: hidden_kernel(rows, modes, *refs),
        [((total, quarter), BF16)],
        (scal, taps, state_in, rim_in, gate, ends, spec, lspec, st, par, qre, qim, later, query, consts),
        [((GROUP, modes, 2, 8, quarter), F32), ((rows + 128, quarter), BF16), ((1, rows, quarter), F32),
         ((1, modes, quarter), F32), ((1, modes, quarter), F32), ((1, rows, quarter), F32)],
    )
    hid = [hidden] + [swap(hidden, SLOT_BITS[m]) for m in (1, 2)]
    hid[1], out_late = lax.optimization_barrier((hid[1], out_late))
    passed = swap(hid[1][rows:], SLOT_BITS[2])
    hid += [swap(hid[2][:rows], SLOT_BITS[1]), passed]
    half = out_weight.shape[1] // 2
    acc, far = call(
        2.0,
        project_kernel,
        [((2, 2, total, half), F32), ((width, 2 * half), BF16)],
        (scal, *hid[:3], out_weight, early, out_late, in_late),
    )
    blocks, last = {}, hid[3:]
    for c in (1, 0):
        keep, send = call(
            0.8,
            lambda *refs: finish_kernel(c, *refs),
            [((total, half), F32), ((total, half), BF16)],
            (scal, acc, *last, out_weight, far),
        )
        send, last = lax.optimization_barrier((send, last))
        parts = call(
            0.4,
            lambda *refs: sort_kernel(rows, *refs),
            [((rows, half), BF16)] * GROUP,
            (scal, keep, swap(send, BIT_CORE)),
        )
        for n, part in enumerate(parts):
            blocks[n, c] = lax.ppermute(part, AXES, homeward(n >> 1, n & 1, c))
    blocks = [blocks[n, c] for n in range(GROUP) for c in (0, 1)]
    (mixed,) = call(1.3, gather_kernel, [((rows, 4 * half), BF16)], (scal, *blocks))
    return mixed


def from_behind(block, axis, distance):
    devices = range(lax.axis_size(axis))
    route = [(i - distance, i) for i in devices if i - distance in devices]
    return lax.ppermute(block, axis, route)


def depthwise(ext, taps):
    width = taps.shape[1]
    kernel = taps[::-1][:, None, :]
    out = lax.conv_general_dilated(
        ext[None],
        kernel,
        (1,),
        "VALID",
        dimension_numbers=("NWC", "WIO", "NWC"),
        feature_group_count=width,
        precision=lax.Precision.HIGHEST,
    )
    return out[0]


def general_body(streams, short_taps, mix_taps, pole_rate, pole_angle, residue, skip, out_weight):
    rows, three, width = streams.shape
    modes = pole_rate.shape[0]
    short = short_taps.reshape(7, three * width)
    rim = from_behind(streams[rows - 6 :], "ctx", 1)
    ext = jnp.concatenate([rim, streams], 0).astype(jnp.float32).reshape(rows + 6, three * width)
    conv = depthwise(ext, short).reshape(rows, three, width)
    gate = (conv[:, 1] * conv[:, 2]).astype(jnp.bfloat16)
    gate_rim = from_behind(gate[rows - 127 :], "ctx", 1)
    gate_ext = jnp.concatenate([gate_rim, gate], 0)
    query = conv[:, 0]
    medium = depthwise(gate_ext.astype(jnp.float32), mix_taps)
    amp = jnp.sqrt(1.0 - jnp.exp(-2.0 * pole_rate))
    res_re = residue[0] * amp
    res_im = residue[1] * amp
    steps = jnp.arange(rows).astype(jnp.float32)[:, None]
    flipped = medium[::-1]

    def first_pass(mode, carry):
        filt, end_re, end_im = carry
        rate = pole_rate[mode][None]
        angle = pole_angle[mode][None]
        mag = jnp.exp(-rate * steps)
        cosk = mag * jnp.cos(angle * steps)
        sink = mag * jnp.sin(angle * steps)
        filt = filt + res_re[mode][None] * cosk - res_im[mode][None] * sink
        end_re = end_re.at[mode].set(jnp.sum(flipped * cosk, 0))
        end_im = end_im.at[mode].set(jnp.sum(flipped * sink, 0))
        return (filt, end_re, end_im)

    zero_state = jnp.zeros((modes, width), jnp.float32)
    filt, end_re, end_im = lax.fori_loop(
        0, modes, first_pass, (jnp.zeros((rows, width), jnp.float32), zero_state, zero_state)
    )
    dec_mag = jnp.exp(-pole_rate * rows)
    dec_re = dec_mag * jnp.cos(pole_angle * rows)
    dec_im = dec_mag * jnp.sin(pole_angle * rows)

    def relay_step(turn, received):
        in_re, in_im = received
        out_re = dec_re * in_re - dec_im * in_im + end_re
        out_im = dec_re * in_im + dec_im * in_re + end_im
        return from_behind((out_re, out_im), "ctx", 1)

    st_re, st_im = lax.fori_loop(0, lax.axis_size("ctx") - 1, relay_step, (zero_state, zero_state))
    later = steps + 1.0

    def second_pass(mode, inflow):
        rate = pole_rate[mode][None]
        angle = pole_angle[mode][None]
        mag = jnp.exp(-rate * later)
        cos1 = mag * jnp.cos(angle * later)
        sin1 = mag * jnp.sin(angle * later)
        are = res_re[mode] * st_re[mode] - res_im[mode] * st_im[mode]
        aim = res_re[mode] * st_im[mode] + res_im[mode] * st_re[mode]
        return inflow + are[None] * cos1 - aim[None] * sin1

    inflow = lax.fori_loop(0, modes, second_pass, jnp.zeros((rows, width), jnp.float32))
    padded = jnp.concatenate([jnp.zeros((rows - 1, width), jnp.float32), medium], 0)
    intra = depthwise(padded, filt)
    longf = intra + inflow + skip[None] * medium
    hidden = (query * longf).astype(jnp.bfloat16)
    partial_out = jnp.dot(
        hidden,
        lax.all_gather(out_weight, "ctx", axis=1, tiled=True),
        preferred_element_type=jnp.float32,
    )
    return lax.psum_scatter(partial_out, "tp", scatter_dimension=1, tiled=True).astype(jnp.bfloat16)


def solution(mesh):
    fast = dict(mesh.shape) == {"ctx": 8, "tp": 4}
    return jax.shard_map(
        fast_body if fast else general_body,
        mesh=mesh,
        in_specs=(
            P("ctx", None, "tp"),
            P(None, None, "tp"),
            P(None, "tp"),
            P(None, "tp"),
            P(None, "tp"),
            P(None, None, "tp"),
            P("tp"),
            P("tp", "ctx"),
        ),
        out_specs=P("ctx", "tp"),
        check_vma=False,
    )
```

```python
import jax
import jax.numpy as jnp
import ml_dtypes
import numpy as np
from jax import lax
from jax.experimental import pallas as pl
from jax.experimental.pallas import tpu as pltpu
from jax.sharding import PartitionSpec as P

F32 = jnp.float32
BF16 = jnp.bfloat16
AXES = ("ctx", "tp")
GROUP = 4
BIT_CORE, BIT_PART, BITS_FAR = 1, 16, 24
EARLY = 9
SLOT_BITS = (0, 4, 8, 12)
VMEM = pl.BlockSpec(memory_space=pltpu.VMEM)
SMEM = pl.BlockSpec(memory_space=pltpu.SMEM)


def swap(block, bits):
    return lax.ppermute(block, AXES, [(i, i ^ bits) for i in range(32)])


def homeward(a, b, c):
    route = []
    for i in range(32):
        high, low, y, core = i >> 3 & 1, i >> 2 & 1, i >> 1 & 1, i & 1
        part, row = i >> 4, y ^ c
        route.append((i, part * 16 + (core ^ a) * 8 + (low ^ b) * 4 + row * 2 + (high ^ part ^ row)))
    return route


def outer(i):
    return (i >> 4) == (i >> 3 & 1)


def far_swap(block, ends):
    return lax.ppermute(block, AXES, [(i, i ^ BITS_FAR) for i in range(32) if outer(i) == ends])


def split_const(mat):
    hi = mat.astype(ml_dtypes.bfloat16)
    lo = (mat - hi.astype(np.float64)).astype(ml_dtypes.bfloat16)
    return hi, lo


def odd_dft(size, rows_in):
    freq = 2 * np.pi * (np.arange(size // 2) + 0.5) / size
    ang = freq[:, None] * np.arange(rows_in)
    return np.concatenate([np.cos(ang), -np.sin(ang)], 0)


def odd_idft(size, rows_out):
    freq = 2 * np.pi * (np.arange(size // 2) + 0.5) / size
    ang = np.asarray(rows_out)[:, None] * freq
    return np.concatenate([np.cos(ang), -np.sin(ang)], 1) * (2.0 / size)


def mm(a, b):
    return jnp.dot(a, b, preferred_element_type=F32)


def split(x):
    hi = x.astype(BF16)
    return hi, (x - hi.astype(F32)).astype(BF16)


def mm3(hi, lo, x):
    xh, xl = split(x)
    return mm(hi, xh) + mm(lo, xh) + mm(hi, xl)


def cmul(spec, filt):
    half = spec.shape[0] // 2
    a, b, c, d = spec[:half], spec[half:], filt[:half], filt[half:]
    return jnp.concatenate([a * c - b * d, a * d + b * c], 0)


class View:
    def __init__(self, ref, top, high, wide):
        self.ref, self.top, self.high, self.wide = ref, top, high, wide

    def __getitem__(self, key):
        wide = self.wide if key is Ellipsis else key[1].stop
        return self.ref[self.top:self.top + self.high, :wide]


def views(consts, rows, size):
    out, top = [], 0
    for high, wide in ((size, size), (2 * rows, size), (2 * rows, rows), (rows, 2 * rows)):
        for _ in range(2):
            out.append(View(consts, top, high, wide))
            top += high
    return out


def params(**kw):
    return pltpu.CompilerParams(vmem_limit_bytes=16 * 1024 * 1024, **kw)


def filters_kernel(rows, modes, g_ref, taps_ref, rate_all, angle_all, res_all, skip_all, short_all, consts,
                   spec_ref, lspec_ref, qre_ref, qim_ref, par_ref, short_ref):
    width = spec_ref.shape[1]
    ntap = taps_ref.shape[0]
    cmh, cml, _, _, clh, cll, _, _ = views(consts, rows, spec_ref.shape[0])
    at = pl.ds(pl.multiple_of(g_ref[0] * width, width), width)
    spec_ref[...] = mm3(cmh[:, :ntap], cml[:, :ntap], taps_ref[:, at])
    short_ref[...] = short_all[:, :, at]
    rate_ref, angle_ref, res_ref, skip_ref = rate_all[:, at], angle_all[:, at], res_all[:, :, at], skip_all[:, at]
    rate, angle = rate_ref[...], angle_ref[...]
    amp = jnp.sqrt(1.0 - jnp.exp(-2.0 * rate))
    rre, rim = res_ref[0] * amp, res_ref[1] * amp

    def power(n):
        mag = jnp.exp(-rate * n)
        return mag * jnp.cos(angle * n), mag * jnp.sin(angle * n)

    p1, p8, pend = power(1.0), power(8.0), power(float(rows))
    par_ref[0], par_ref[1] = rre * p1[0] - rim * p1[1], rre * p1[1] + rim * p1[0]
    par_ref[2], par_ref[3] = pend
    steps = lax.broadcasted_iota(jnp.int32, (8, width), 0).astype(F32)
    filt = [jnp.zeros((8, width), F32) for _ in range(rows // 8)]
    for m in range(modes):
        ang = angle[m:m + 1] * steps
        mag = jnp.exp(-rate[m:m + 1] * steps)
        cre, cim = mag * jnp.cos(ang), mag * jnp.sin(ang)
        sre, sim = p8[0][m:m + 1], p8[1][m:m + 1]
        wre, wim = rre[m:m + 1], rim[m:m + 1]
        for j in range(rows // 8):
            qre_ref[m, j * 8:j * 8 + 8] = cre
            qim_ref[m, j * 8:j * 8 + 8] = cim
            filt[j] = filt[j] + wre * cre - wim * cim
            cre, cim = cre * sre - cim * sim, cre * sim + cim * sre
    first = lax.broadcasted_iota(jnp.int32, (8, width), 0) == 0
    filt[0] = filt[0] + jnp.where(first, skip_ref[...], 0.0)
    lspec_ref[...] = mm3(clh[...], cll[...], jnp.concatenate(filt, 0))


def prepare_kernel(rows, g_ref, x_hbm, t_hbm, o0, o1, o2, o3, p0, p1, p2, p3, x_ref, t_ref, kx, vx, gate, sems):
    outs, queries = (o0, o1, o2, o3), (p0, p1, p2, p3)
    g = g_ref[0]
    quarter = o0.shape[1]
    tiles = x_ref.shape[2] // 128
    short = pltpu.make_async_copy(t_hbm, t_ref, sems.at[tiles])
    short.start()
    loads = []
    for lt in range(tiles):
        ls = slice(lt * 128, lt * 128 + 128)
        loads.append(pltpu.make_async_copy(x_hbm.at[:, :, ls], x_ref.at[:, :, ls], sems.at[lt]))
        loads[-1].start()
    short.wait()
    for lt in range(tiles):
        ls = slice(lt * 128, lt * 128 + 128)
        loads[lt].wait()
        for src, ext in ((1, kx), (2, vx)):
            ext[lt, :8] = jnp.zeros((8, 128), F32)
            ext[lt, 8:] = x_ref[src, :, ls].astype(F32)
        tk = [jnp.broadcast_to(t_ref[1, j:j + 1, ls], (8, 128)) for j in range(7)]
        tv = [jnp.broadcast_to(t_ref[2, j:j + 1, ls], (8, 128)) for j in range(7)]
        for r in range(0, rows, 16):
            both = []
            for h in (0, 8):
                sk, sv = tk[0] * kx[lt, 8 + r + h:16 + r + h], tv[0] * vx[lt, 8 + r + h:16 + r + h]
                for j in range(1, 7):
                    o = 8 + r + h - j
                    sk, sv = sk + tk[j] * kx[lt, o:o + 8], sv + tv[j] * vx[lt, o:o + 8]
                both.append(sk * sv)
            gate[r:r + 16, ls] = jnp.concatenate(both, 0).astype(BF16)
    for m, (out, query) in enumerate(zip(outs, queries)):
        at = pl.ds(pl.multiple_of((g ^ m) * quarter, quarter), quarter)
        out[:rows] = gate[:, at]
        for i in (1, 2):
            ends = [x_ref[i, :16, at].astype(F32)[:8], x_ref[i, rows - 16:, at].astype(F32)[8:]]
            row = rows + 16 * (i - 1)
            out[row:row + 16] = jnp.concatenate(ends, 0).astype(BF16)
        out[rows + 32:rows + 48] = x_ref[0, rows - 16:, at]
        query[...] = x_ref[0, :, at]


def first_gates(before, ends, taps):
    out = []
    for i in (0, 1):
        ext = jnp.concatenate([before[16 * i + 8:16 * i + 16], ends[16 * i:16 * i + 8]], 0)
        t = taps[1 + i]
        acc = t[0:1] * ext[8:16]
        for j in range(1, 7):
            acc = acc + t[j:j + 1] * ext[8 - j:16 - j]
        out.append(acc)
    return out[0] * out[1]


def tail_part(tail, taps):
    ext = jnp.concatenate([tail, jnp.zeros_like(tail)], 0)
    out = taps[1:2] * ext[7:15]
    for lag in range(2, 7):
        out = out + taps[lag:lag + 1] * ext[8 - lag:16 - lag]
    return out


def end_states(rows, modes, per, flip, blocks, qre_ref, qim_ref, er, ei, width):
    for lt in range(width // 128):
        ls = slice(lt * 128, lt * 128 + 128)
        for m0 in range(0, modes, per):
            def step(j, acc):
                at = pl.ds(pl.multiple_of(j * 8, 8), 8)
                x = [flip[b, at, ls] for b in blocks]
                out = []
                for i in range(per):
                    qr, qi = qre_ref[m0 + i, at, ls], qim_ref[m0 + i, at, ls]
                    for b in range(len(blocks)):
                        k = (i * len(blocks) + b) * 2
                        out += [acc[k] + x[b] * qr, acc[k + 1] + x[b] * qi]
                return tuple(out)
            acc = lax.fori_loop(0, rows // 8, step, (jnp.zeros((8, 128), F32),) * (2 * len(blocks) * per), unroll=10 if len(blocks) > 1 else 20)
            for i in range(per):
                for b in range(len(blocks)):
                    k = (i * len(blocks) + b) * 2
                    er[b, m0 + i:m0 + i + 1, ls] = jnp.sum(acc[k], 0, keepdims=True)
                    ei[b, m0 + i:m0 + i + 1, ls] = jnp.sum(acc[k + 1], 0, keepdims=True)


def medium_of(gates, spec, cmh, cml, imh, iml):
    return mm3(imh[...], iml[...], cmul(mm(cmh[...], gates) + mm(cml[...], gates), spec))


def medium_kernel(rows, modes, g_ref, t_ref, spec_ref, qre_ref, qim_ref, par_ref,
                  consts, q0, q1, q2, q3,
                  med_ref, st_ref, out_ref, rim_ref, gate_ref, ends_ref, gx, flip, er, ei, ends):
    g = g_ref[0]
    cmh, cml, imh, iml = views(consts, rows, spec_ref.shape[0])[:4]
    width = gate_ref.shape[1]
    gx[:128] = jnp.zeros_like(gx[:128])
    for m, msg in enumerate((q0, q1, q2, q3)):
        gx[pl.ds(pl.multiple_of(128 + (g ^ m) * rows, 16), rows), :] = msg[:rows]
        ends[g ^ m] = msg[rows:rows + 32].astype(F32)
    gate_ref[...] = gx[128:128 + rows]
    ends_ref[...] = ends[0]
    rim_ref[:128] = gx[GROUP * rows:]
    rim_ref[128:160] = ends[GROUP - 1].astype(BF16)
    for b in range(1, GROUP):
        top = 128 + b * rows
        head = first_gates(ends[b - 1], ends[b], t_ref)
        gx[top:top + 16] = jnp.concatenate([head, gx[top:top + 16].astype(F32)[8:]], 0).astype(BF16)
    ext = jnp.concatenate([gx[b * rows:b * rows + rows + 128] for b in range(GROUP)], 1)
    both = medium_of(ext, jnp.concatenate([spec_ref[...]] * GROUP, 1), cmh, cml, imh, iml)
    for b in range(GROUP):
        med_ref[b] = both[:rows, b * width:(b + 1) * width]
        flip[b] = both[rows:, b * width:(b + 1) * width]
    end_states(rows, modes, 4, flip, range(GROUP), qre_ref, qim_ref, er, ei, width)
    dre, dim = par_ref[2], par_ref[3]
    sre = jnp.zeros((modes, width), F32)
    sim = sre
    for b in range(GROUP):
        st_ref[b, 0], st_ref[b, 1] = er[b], ei[b]
        sre, sim = dre * sre - dim * sim + er[b], dre * sim + dim * sre + ei[b]
    out_ref[:modes] = sre
    out_ref[modes:2 * modes] = sim
    for m, q in enumerate((q0, q1, q2, q3)):
        @pl.when((g ^ m) == GROUP - 1)
        def _():
            out_ref[2 * modes:] = q[rows + 32:].astype(F32)[8:]


def intra_kernel(rows, g_ref, t_ref, med_ref, lspec_ref, consts, q0, q1, q2, q3, intra_ref, query_ref, qx):
    g = g_ref[0]
    _, _, _, _, clh, cll, ilh, ill = views(consts, rows, med_ref.shape[1] + 128)
    for b in range(1, GROUP):
        intra_ref[b - 1] = mm3(ilh[...], ill[...], cmul(mm3(clh[...], cll[...], med_ref[b]), lspec_ref[...]))
    total = GROUP * rows
    for lt in range(query_ref.shape[1] // 128):
        ls = slice(lt * 128, lt * 128 + 128)
        qx[lt, :8] = jnp.zeros((8, 128), F32)
        for m, q in enumerate((q0, q1, q2, q3)):
            qx[lt, pl.ds(pl.multiple_of((g ^ m) * rows + 8, 8), rows), :] = q[:, ls].astype(F32)
        t = [jnp.broadcast_to(t_ref[0, j:j + 1, ls], (8, 128)) for j in range(7)]
        for r in range(0, total, 8):
            acc = t[0] * qx[lt, 8 + r:16 + r]
            for j in range(1, 7):
                acc = acc + t[j] * qx[lt, 8 + r - j:16 + r - j]
            query_ref[r:r + 8, ls] = acc


def hidden_kernel(rows, modes, g_ref, t_ref, in_ref, rim_ref, gate_ref, ends_ref, spec_ref, lspec_ref, st_ref, par_ref,
                  qre_ref, qim_ref, later_ref, query_ref, consts,
                  hid_ref, amp, gx, flip, er, ei, intra):
    part = g_ref[1]
    live = (part > 0).astype(F32)
    width = query_ref.shape[1]
    cmh, cml, imh, iml, clh, cll, ilh, ill = views(consts, rows, gx.shape[0])
    gx[:128] = (rim_ref[:128].astype(F32) * live).astype(BF16)
    head = first_gates(rim_ref[128:160].astype(F32) * live, ends_ref[...], t_ref)
    gx[128:] = gate_ref[...]
    gx[128:144] = jnp.concatenate([head, gate_ref[:16].astype(F32)[8:]], 0).astype(BF16)
    both = medium_of(gx[...], spec_ref[...], cmh, cml, imh, iml)
    flip[0] = both[rows:]
    intra[0] = mm3(ilh[...], ill[...], cmul(mm3(clh[...], cll[...], both[:rows]), lspec_ref[...]))
    end_states(rows, modes, 8, flip, range(1), qre_ref, qim_ref, er, ei, width)
    sre, sim = in_ref[:modes] * live, in_ref[modes:2 * modes] * live
    rre, rim, dre, dim = par_ref[0], par_ref[1], par_ref[2], par_ref[3]
    for b in range(GROUP):
        are, aim = rre * sre - rim * sim, rre * sim + rim * sre
        for m in range(modes):
            amp[b, m, 0] = jnp.broadcast_to(are[m:m + 1], (8, width))
            amp[b, m, 1] = jnp.broadcast_to(aim[m:m + 1], (8, width))
        ere, eim = (er[0], ei[0]) if b == 0 else (st_ref[b, 0], st_ref[b, 1])
        sre, sim = dre * sre - dim * sim + ere, dre * sim + dim * sre + eim
    query_ref[:8] = query_ref[:8] + tail_part(in_ref[2 * modes:] * live, t_ref[0])
    for lt in range(width // 128):
        ls = slice(lt * 128, lt * 128 + 128)

        def step(j, carry):
            at = [pl.ds(pl.multiple_of(j * 16 + 8 * i, 8), 8) for i in range(2)]
            acc = [[intra[0, at[i], ls] for i in range(2)]]
            acc += [[later_ref[b, at[i], ls] for i in range(2)] for b in range(GROUP - 1)]
            for m in range(modes):
                qr = [qre_ref[m, at[i], ls] for i in range(2)]
                qi = [qim_ref[m, at[i], ls] for i in range(2)]
                for b in range(GROUP):
                    ar, ai = amp[b, m, 0, :, ls], amp[b, m, 1, :, ls]
                    for i in range(2):
                        acc[b][i] = acc[b][i] + ar * qr[i] - ai * qi[i]
            for b in range(GROUP):
                row = pl.multiple_of(b * rows + j * 16, 16)
                long = jnp.concatenate(acc[b], 0)
                hid_ref[pl.ds(row, 16), ls] = (query_ref[pl.ds(row, 16), ls] * long).astype(BF16)
            return carry

        lax.fori_loop(0, rows // 16, step, 0)


def halves(core, wide):
    half = wide // 2
    return [pl.ds(pl.multiple_of(k * half, half), half) for k in (core, 1 - core)]


def project_kernel(g_ref, h0, h1, h2, wa_ref, early, out_late, in_late, acc_ref, wb_ref):
    g, same, core, at_end, cut = g_ref[0], g_ref[2], g_ref[3], g_ref[6], early.shape[0]
    quarter = h0.shape[1]
    wb_ref[:cut] = early[...]

    @pl.when(at_end > 0)
    def _():
        wb_ref[cut:] = out_late[...]

    @pl.when(at_end == 0)
    def _():
        wb_ref[cut:] = in_late[...]

    at = [pl.ds(pl.multiple_of((g ^ m) * quarter, quarter), quarter) for m in range(GROUP - 1)]
    x = jnp.concatenate([h0[...], h1[...], h2[...]], 1)
    for weight, c in ((wa_ref, 1 - same), (wb_ref, same)):
        for k, cols in enumerate(halves(core, wa_ref.shape[1])):
            acc_ref[c, k] = mm(x, jnp.concatenate([weight[a, cols] for a in at], 0))


def finish_kernel(c, g_ref, acc_ref, top, low, wa_ref, wb_ref, keep_ref, send_ref):
    own, quarter = g_ref[2] != c, top.shape[1]
    at = pl.ds(pl.multiple_of((g_ref[0] ^ (GROUP - 1)) * quarter, quarter), quarter)
    x = jnp.concatenate([top[...], low[...]], 0)
    mine, other = [mm(x, jnp.where(own, wa_ref[at, cols], wb_ref[at, cols])) for cols in halves(g_ref[3], wa_ref.shape[1])]
    send_ref[...] = (acc_ref[c, 1] + other).astype(BF16)
    keep_ref[...] = acc_ref[c, 0] + mine


def sort_kernel(rows, g_ref, keep_ref, got_ref, *outs):
    low, core = g_ref[4], g_ref[3]
    for n, out in enumerate(outs):
        block = 2 * (core ^ (n >> 1)) + (low ^ (n & 1))
        at = pl.ds(pl.multiple_of(block * rows, rows), rows)
        out[...] = (keep_ref[at, :] + got_ref[at, :].astype(F32)).astype(BF16)


def gather_kernel(g_ref, *refs):
    out_ref = refs[-1]
    low, high = g_ref[4], g_ref[5]
    width = refs[0].shape[1]
    for n in range(4):
        a, b = n >> 1, n & 1
        at = pl.ds(pl.multiple_of((2 * (low ^ b) + (high ^ a)) * width, width), width)
        out_ref[:, at] = (refs[2 * n][...].astype(F32) + refs[2 * n + 1][...].astype(F32)).astype(BF16)


def call(us, kernel, outs, args, scratch=()):
    return pl.pallas_call(
        kernel,
        out_shape=tuple(jax.ShapeDtypeStruct(s, d) for s, d in outs),
        in_specs=[SMEM] + [VMEM] * (len(args) - 1),
        out_specs=(VMEM,) * len(outs),
        scratch_shapes=[pltpu.VMEM(s, d) for s, d in scratch],
        compiler_params=params(),
        cost_estimate=pl.CostEstimate(flops=int(us * 1.15e9), bytes_accessed=int(us * 3.69e6), transcendentals=0),
    )(*args)


def fast_body(streams, short_taps, mix_taps, pole_rate, pole_angle, residue, skip, out_weight):
    rows, _, width = streams.shape
    modes = pole_rate.shape[0]
    ntap = mix_taps.shape[0]
    quarter = width // GROUP
    total = GROUP * rows
    ctx, tp = lax.axis_index("ctx"), lax.axis_index("tp")
    g, part = ctx % GROUP, ctx // GROUP
    core, y = tp % 2, tp // 2
    scal = jnp.stack([g, part, (y == part).astype(jnp.int32), core, g % 2, g // 2, (part == g // 2).astype(jnp.int32)]).astype(jnp.int32)

    cut = width * EARLY // 16
    size_m = rows + ntap
    back = np.concatenate([np.arange(ntap, size_m), np.arange(ntap, size_m)[::-1]])
    mats = [odd_dft(size_m, size_m), odd_idft(size_m, back), odd_dft(2 * rows, rows), odd_idft(2 * rows, np.arange(rows))]
    consts = np.concatenate([
        np.pad(half, ((0, 0), (0, 2 * rows - half.shape[1]))) for mat in mats for half in split_const(mat)], 0)

    short_taps = short_taps.transpose(1, 0, 2)
    anywhere = pl.BlockSpec(memory_space=pltpu.HBM)
    sent = pl.pallas_call(
        lambda *refs: prepare_kernel(rows, *refs),
        out_shape=tuple(jax.ShapeDtypeStruct((r, quarter), BF16) for r in (rows + 48,) * GROUP + (rows,) * GROUP),
        in_specs=[SMEM, anywhere, anywhere],
        out_specs=(VMEM,) * (2 * GROUP),
        scratch_shapes=[pltpu.VMEM((3, rows, width), BF16), pltpu.VMEM((3, 7, width), F32)]
        + [pltpu.VMEM((width // 128, rows + 8, 128), F32)] * 2
        + [pltpu.VMEM((rows, width), BF16), pltpu.SemaphoreType.DMA((width // 128 + 1,))],
        compiler_params=params(),
        cost_estimate=pl.CostEstimate(flops=int(2e9), bytes_accessed=int(6e6), transcendentals=0),
    )(scal, streams.transpose(1, 0, 2), short_taps)
    msgs, qs = sent[:GROUP], sent[GROUP:]
    early = swap(out_weight[:cut], BITS_FAR)
    msgs = [msgs[0]] + [swap(msgs[m], SLOT_BITS[m]) for m in (1, 2, 3)]
    spec, lspec, qre, qim, par, taps = call(
        0.3,
        lambda *refs: filters_kernel(rows, modes, *refs),
        [(s, F32) for s in ((size_m, quarter), (2 * rows, quarter), (modes, rows, quarter), (modes, rows, quarter),
                            (4, modes, quarter), (3, 7, quarter))],
        (scal, mix_taps, pole_rate, pole_angle, residue, skip[None], short_taps, consts),
    )
    spec, qs = lax.optimization_barrier((spec, qs))
    qs = [qs[0]] + [swap(qs[m], SLOT_BITS[m]) for m in (1, 2, 3)]
    med, st, out, rim, gate, ends = call(
        0.6,
        lambda *refs: medium_kernel(rows, modes, *refs),
        [((GROUP, rows, quarter), F32), ((GROUP, 2, modes, quarter), F32), ((2 * modes + 8, quarter), F32),
         ((160, quarter), BF16), ((rows, quarter), BF16), ((32, quarter), F32)],
        (scal, taps, spec, qre, qim, par, consts, *msgs),
        [((total + 128, quarter), BF16), ((GROUP, rows, quarter), F32), ((GROUP, modes, quarter), F32), ((GROUP, modes, quarter), F32),
         ((GROUP, 32, quarter), F32)],
    )
    out, rim, early = lax.optimization_barrier((out, rim, early))
    state_in, rim_in = swap(out, BIT_PART), swap(rim, BIT_PART)
    later, query = call(
        3.1,
        lambda *refs: intra_kernel(rows, *refs),
        [((GROUP - 1, rows, quarter), F32), ((total, quarter), F32)],
        (scal, taps, med, lspec, consts, *qs),
        [((quarter // 128, total + 8, 128), F32)],
    )
    late, later = lax.optimization_barrier((out_weight[cut:], later))
    out_late = far_swap(late, True)
    late, later = lax.optimization_barrier((out_weight[cut:], later))
    in_late = far_swap(late, False)
    (hidden,) = call(
        5.2,
        lambda *refs: hidden_kernel(rows, modes, *refs),
        [((total, quarter), BF16)],
        (scal, taps, state_in, rim_in, gate, ends, spec, lspec, st, par, qre, qim, later, query, consts),
        [((GROUP, modes, 2, 8, quarter), F32), ((rows + 128, quarter), BF16), ((1, rows, quarter), F32),
         ((1, modes, quarter), F32), ((1, modes, quarter), F32), ((1, rows, quarter), F32)],
    )
    hid = [hidden] + [swap(hidden, SLOT_BITS[m]) for m in (1, 2)]
    hid[1], out_late = lax.optimization_barrier((hid[1], out_late))
    passed = swap(hid[1][96:], SLOT_BITS[2])
    hid += [swap(hid[2][:96], SLOT_BITS[1]), passed]
    half = out_weight.shape[1] // 2
    acc, far = call(
        2.0,
        project_kernel,
        [((2, 2, total, half), F32), ((width, 2 * half), BF16)],
        (scal, *hid[:3], out_weight, early, out_late, in_late),
    )
    blocks, last = {}, hid[3:]
    for c in (1, 0):
        keep, send = call(
            0.8,
            lambda *refs: finish_kernel(c, *refs),
            [((total, half), F32), ((total, half), BF16)],
            (scal, acc, *last, out_weight, far),
        )
        send, last = lax.optimization_barrier((send, last))
        parts = call(
            0.4,
            lambda *refs: sort_kernel(rows, *refs),
            [((rows, half), BF16)] * GROUP,
            (scal, keep, swap(send, BIT_CORE)),
        )
        for n, part in enumerate(parts):
            blocks[n, c] = lax.ppermute(part, AXES, homeward(n >> 1, n & 1, c))
    blocks = [blocks[n, c] for n in range(GROUP) for c in (0, 1)]
    (mixed,) = call(1.3, gather_kernel, [((rows, 4 * half), BF16)], (scal, *blocks))
    return mixed


def from_behind(block, axis, distance):
    devices = range(lax.axis_size(axis))
    route = [(i - distance, i) for i in devices if i - distance in devices]
    return lax.ppermute(block, axis, route)


def depthwise(ext, taps):
    width = taps.shape[1]
    kernel = taps[::-1][:, None, :]
    out = lax.conv_general_dilated(
        ext[None],
        kernel,
        (1,),
        "VALID",
        dimension_numbers=("NWC", "WIO", "NWC"),
        feature_group_count=width,
        precision=lax.Precision.HIGHEST,
    )
    return out[0]


def general_body(streams, short_taps, mix_taps, pole_rate, pole_angle, residue, skip, out_weight):
    rows, three, width = streams.shape
    modes = pole_rate.shape[0]
    short = short_taps.reshape(7, three * width)
    rim = from_behind(streams[rows - 6 :], "ctx", 1)
    ext = jnp.concatenate([rim, streams], 0).astype(jnp.float32).reshape(rows + 6, three * width)
    conv = depthwise(ext, short).reshape(rows, three, width)
    gate = (conv[:, 1] * conv[:, 2]).astype(jnp.bfloat16)
    gate_rim = from_behind(gate[rows - 127 :], "ctx", 1)
    gate_ext = jnp.concatenate([gate_rim, gate], 0)
    query = conv[:, 0]
    medium = depthwise(gate_ext.astype(jnp.float32), mix_taps)
    amp = jnp.sqrt(1.0 - jnp.exp(-2.0 * pole_rate))
    res_re = residue[0] * amp
    res_im = residue[1] * amp
    steps = jnp.arange(rows).astype(jnp.float32)[:, None]
    flipped = medium[::-1]

    def first_pass(mode, carry):
        filt, end_re, end_im = carry
        rate = pole_rate[mode][None]
        angle = pole_angle[mode][None]
        mag = jnp.exp(-rate * steps)
        cosk = mag * jnp.cos(angle * steps)
        sink = mag * jnp.sin(angle * steps)
        filt = filt + res_re[mode][None] * cosk - res_im[mode][None] * sink
        end_re = end_re.at[mode].set(jnp.sum(flipped * cosk, 0))
        end_im = end_im.at[mode].set(jnp.sum(flipped * sink, 0))
        return (filt, end_re, end_im)

    zero_state = jnp.zeros((modes, width), jnp.float32)
    filt, end_re, end_im = lax.fori_loop(
        0, modes, first_pass, (jnp.zeros((rows, width), jnp.float32), zero_state, zero_state)
    )
    dec_mag = jnp.exp(-pole_rate * rows)
    dec_re = dec_mag * jnp.cos(pole_angle * rows)
    dec_im = dec_mag * jnp.sin(pole_angle * rows)

    def relay_step(turn, received):
        in_re, in_im = received
        out_re = dec_re * in_re - dec_im * in_im + end_re
        out_im = dec_re * in_im + dec_im * in_re + end_im
        return from_behind((out_re, out_im), "ctx", 1)

    st_re, st_im = lax.fori_loop(0, lax.axis_size("ctx") - 1, relay_step, (zero_state, zero_state))
    later = steps + 1.0

    def second_pass(mode, inflow):
        rate = pole_rate[mode][None]
        angle = pole_angle[mode][None]
        mag = jnp.exp(-rate * later)
        cos1 = mag * jnp.cos(angle * later)
        sin1 = mag * jnp.sin(angle * later)
        are = res_re[mode] * st_re[mode] - res_im[mode] * st_im[mode]
        aim = res_re[mode] * st_im[mode] + res_im[mode] * st_re[mode]
        return inflow + are[None] * cos1 - aim[None] * sin1

    inflow = lax.fori_loop(0, modes, second_pass, jnp.zeros((rows, width), jnp.float32))
    padded = jnp.concatenate([jnp.zeros((rows - 1, width), jnp.float32), medium], 0)
    intra = depthwise(padded, filt)
    longf = intra + inflow + skip[None] * medium
    hidden = (query * longf).astype(jnp.bfloat16)
    partial_out = jnp.dot(
        hidden,
        lax.all_gather(out_weight, "ctx", axis=1, tiled=True),
        preferred_element_type=jnp.float32,
    )
    return lax.psum_scatter(partial_out, "tp", scatter_dimension=1, tiled=True).astype(jnp.bfloat16)


def solution(mesh):
    fast = dict(mesh.shape) == {"ctx": 8, "tp": 4}
    return jax.shard_map(
        fast_body if fast else general_body,
        mesh=mesh,
        in_specs=(
            P("ctx", None, "tp"),
            P(None, None, "tp"),
            P(None, "tp"),
            P(None, "tp"),
            P(None, "tp"),
            P(None, None, "tp"),
            P("tp"),
            P("tp", "ctx"),
        ),
        out_specs=P("ctx", "tp"),
        check_vma=False,
    )
```
